32 devices in a mesh: groups: 1, cells: 32 (over z, y, x, core).
Axes of the slice: x: 2, y: 2, z: 4, core: 2. Of those that a mesh axis runs over, the one named last changes fastest.
Arguments:
- rna_counts: bfloat16 [2048, 4096], P(('groups', 'cells')), may hold values from 1 to 30, as said below
- atac_counts: bfloat16 [2048, 16384], P(('groups', 'cells')), may hold values from 1 to 30, as said below
- cell_factor: float32 [64, 2048], P(None, ('groups', 'cells')), may hold values from 0.1 to 3, as said below
- gene_factor: float32 [64, 4096], P(None, ('groups', 'cells')), may hold values from 0.1 to 3, as said below
- peak_factor: float32 [64, 16384], P(None, ('groups', 'cells')), may hold values from 0.1 to 3, as said below
- link_gene: int32 [256], P(('groups', 'cells')), may hold values from 0 to 31
- link_peak: int32 [256], P(('groups', 'cells')), may hold values from 0 to 127
- link_weight: int32 [256], P(('groups', 'cells')), may hold values from 1 to 4
- link_count: int32 [32], P(('groups', 'cells')), may hold values from 1 to 8, as said below
Outputs:
- cell_out: float32 [64, 2048], P(None, ('groups', 'cells'))
- gene_out: float32 [64, 4096], P(None, ('groups', 'cells'))
- peak_out: float32 [64, 16384], P(None, ('groups', 'cells'))
The draws below stay inside these ranges and needn't reach their ends.
Inputs may be any that keep to these rules, and one draw needn't show every extreme that they name: `rna_counts`: nonnegative counts. `atac_counts`: nonnegative counts. `cell_factor`: positive loadings. `gene_factor`: positive loadings. `peak_factor`: positive loadings. `link_count`: at least one live slot on every index, and some index has all 8 slots live.
All inputs are finite; a program needn't handle non-finite values.
Results may differ from the reference program's by a relative error of at most 0.00068.
Values may be sent and summed in bfloat16 or wider, within the bound.
No kernel may reach another device: no remote copies, remote signals or barrier semaphores. Data moves between devices by JAX's collectives and lax.ppermute only.
A program may use at most 64 MiB of HBM per device.

```python
import jax
import jax.numpy as jnp
from jax import lax

K = 64
G = 4096
P_SIZE = 16384
BLOCK = 128
LINK_MAX = 8
ROUNDS = 2
CELLS = 2048
LINKS = 256
N_CELLS = 32


def draw_loadings(key, columns):
    base = jnp.exp(jax.random.uniform(key, (K, columns), jnp.float32, jnp.log(0.1), 0.0))
    rising = 1.0 + jnp.arange(columns, dtype=jnp.float32) / columns
    return base * rising[None, :]


def draw_counts(key, columns, salt):
    cell_key = jax.random.fold_in(key, 31)
    feature_key = jax.random.fold_in(key, salt)
    noise_key = jax.random.fold_in(key, salt + 1)
    cell_part = jnp.exp(1.5 * jax.random.normal(cell_key, (CELLS, K), jnp.float32))
    feature_part = jnp.exp(2.0 * jax.random.normal(feature_key, (K, columns), jnp.float32))
    noise = jnp.exp(0.4 * jax.random.normal(noise_key, (CELLS, columns), jnp.float32))
    planted = jnp.dot(cell_part, feature_part) / (3.0 * K)
    return jnp.clip(planted * noise, 1.0, 30.0).astype(jnp.bfloat16)


def draw_rna_counts(key, part):
    return draw_counts(key, G, 41)


def draw_atac_counts(key, part):
    return draw_counts(key, P_SIZE, 51)


def draw_cell_factor(key, part):
    return draw_loadings(jax.random.fold_in(key, 11), CELLS)


def draw_gene_factor(key, part):
    return draw_loadings(jax.random.fold_in(key, 12), G)


def draw_peak_factor(key, part):
    return draw_loadings(jax.random.fold_in(key, 13), P_SIZE)


def draw_link_count(key, part):
    counts = jax.random.randint(jax.random.fold_in(key, 21), (N_CELLS,), 1, LINK_MAX + 1)
    fullest = jax.random.randint(jax.random.fold_in(key, 22), (), 0, N_CELLS)
    return jnp.where(jnp.arange(N_CELLS, dtype=jnp.int32) == fullest, LINK_MAX, counts).astype(jnp.int32)


def plant(drawn, rng, low, top_value):
    index_at = [jax.random.randint(jax.random.fold_in(rng, axis), (), 0, length) for axis, length in enumerate(drawn.shape)]
    main_axis = drawn.shape.index(max(drawn.shape))
    beside = index_at[:main_axis] + [(index_at[main_axis] + 1) % drawn.shape[main_axis]] + index_at[main_axis + 1:]
    return drawn.at[tuple(index_at)].set(low).at[tuple(beside)].set(top_value)


def setup_inputs(seed: int = 0, part: int = 0) -> dict:
    arg_keys = jax.random.split(jax.random.key(seed), 10)
    part_keys = jax.random.split(jax.random.fold_in(arg_keys[9], part), 10)
    return {
        "rna_counts": draw_rna_counts(jax.random.fold_in(jax.random.fold_in(arg_keys[9], part), 71), part),
        "atac_counts": draw_atac_counts(jax.random.fold_in(jax.random.fold_in(arg_keys[9], part), 71), part),
        "cell_factor": draw_cell_factor(jax.random.fold_in(jax.random.fold_in(arg_keys[9], part), 71), part),
        "gene_factor": draw_gene_factor(jax.random.fold_in(jax.random.fold_in(arg_keys[9], part), 71), part),
        "peak_factor": draw_peak_factor(jax.random.fold_in(jax.random.fold_in(arg_keys[9], part), 71), part),
        "link_gene": plant(jax.random.randint(part_keys[5], (LINKS,), 0, G // BLOCK), jax.random.fold_in(part_keys[5], 1), 0, (G // BLOCK) - 1).astype(jnp.int32),
        "link_peak": plant(jax.random.randint(part_keys[6], (LINKS,), 0, P_SIZE // BLOCK), jax.random.fold_in(part_keys[6], 1), 0, (P_SIZE // BLOCK) - 1).astype(jnp.int32),
        "link_weight": plant(jax.random.randint(part_keys[7], (LINKS,), 1, 5), jax.random.fold_in(part_keys[7], 1), 1, 4).astype(jnp.int32),
        "link_count": draw_link_count(jax.random.fold_in(jax.random.fold_in(arg_keys[9], part), 71), part),
    }


EPSILON = 1e-6


def block_table(link_gene, link_peak, link_weight, link_count):
    live_slots = jnp.arange(LINK_MAX, dtype=jnp.int32)[None, :] < link_count[:, None]
    live_weight = jnp.where(live_slots.reshape(LINKS), link_weight, 0).astype(jnp.float32)
    gene_hot = (link_gene[:, None] == jnp.arange(G // BLOCK, dtype=jnp.int32)[None, :]).astype(jnp.float32)
    peak_hot = (link_peak[:, None] == jnp.arange(P_SIZE // BLOCK, dtype=jnp.int32)[None, :]).astype(jnp.float32)
    return jnp.dot((gene_hot * live_weight[:, None]).T, peak_hot, precision=lax.Precision.HIGHEST)


def couple(link_table, source):
    blocked = source.astype(jnp.float32).reshape(K, link_table.shape[1], BLOCK)
    result = jnp.einsum("kpc,gp->kgc", blocked, link_table, precision=lax.Precision.HIGHEST)
    return result.reshape(K, link_table.shape[0] * BLOCK)


def reference(rna_counts, atac_counts, cell_factor, gene_factor, peak_factor, link_gene, link_peak, link_weight, link_count):
    link_table = block_table(link_gene, link_peak, link_weight, link_count)
    link_scale = CELLS / 4.0
    for sweep_index in range(ROUNDS):
        cell_low = cell_factor.astype(jnp.bfloat16)
        gram_cells = jnp.dot(cell_factor, cell_factor.T, precision=lax.Precision.HIGHEST)
        gene_low = gene_factor.astype(jnp.bfloat16)
        peak_low = peak_factor.astype(jnp.bfloat16)
        gene_num = jnp.dot(cell_low, rna_counts, preferred_element_type=jnp.float32) + link_scale * couple(link_table, peak_low)
        peak_num = jnp.dot(cell_low, atac_counts, preferred_element_type=jnp.float32) + link_scale * couple(link_table.T, gene_low)
        gene_factor = gene_factor * gene_num / (jnp.dot(gram_cells, gene_factor, precision=lax.Precision.HIGHEST) + EPSILON)
        peak_factor = peak_factor * peak_num / (jnp.dot(gram_cells, peak_factor, precision=lax.Precision.HIGHEST) + EPSILON)
        gene_new = gene_factor.astype(jnp.bfloat16)
        peak_new = peak_factor.astype(jnp.bfloat16)
        gram_features = jnp.dot(gene_new, gene_new.T, preferred_element_type=jnp.float32) + jnp.dot(peak_new, peak_new.T, preferred_element_type=jnp.float32)
        cell_num = jnp.dot(gene_new, rna_counts.T, preferred_element_type=jnp.float32) + jnp.dot(peak_new, atac_counts.T, preferred_element_type=jnp.float32)
        cell_factor = cell_factor * cell_num / (jnp.dot(gram_features, cell_factor, precision=lax.Precision.HIGHEST) + EPSILON)
    return cell_factor, gene_factor, peak_factor
```

```python
import jax
import jax.numpy as jnp
from jax import lax
from jax.sharding import PartitionSpec as P

BLOCK = 128
ROUNDS = 2
EPSILON = 1e-06
AXIS = "cells"


def flip(value, bit):
    count = lax.axis_size(AXIS)
    return lax.ppermute(value, AXIS, [(i, i ^ bit) for i in range(count)])


def in_order(bit, mine, other):
    mine_first = (lax.axis_index(AXIS) & bit) == 0
    return jnp.where(mine_first, mine, other), jnp.where(mine_first, other, mine)


def bits_below(size):
    return [1 << b for b in range(size.bit_length() - 1)]


def own_table(link_gene, link_peak, link_weight, link_count, gene_blocks, peak_blocks):
    slot_ids = jnp.arange(link_gene.shape[0], dtype=jnp.int32)
    live_weight = jnp.where(slot_ids < link_count[0], link_weight, 0).astype(jnp.float32)
    gene_hot = (link_gene[:, None] == jnp.arange(gene_blocks, dtype=jnp.int32)[None, :]).astype(
        jnp.float32
    )
    peak_hot = (link_peak[:, None] == jnp.arange(peak_blocks, dtype=jnp.int32)[None, :]).astype(
        jnp.float32
    )
    return jnp.dot((gene_hot * live_weight[:, None]).T, peak_hot, precision=lax.Precision.HIGHEST)


def split_low(value):
    high = lax.reduce_precision(value, exponent_bits=8, mantissa_bits=7)
    return high.astype(jnp.bfloat16), (value - high).astype(jnp.bfloat16)


def gather_half(value, half):
    for bit in bits_below(half):
        value = jnp.concatenate(in_order(bit, value, flip(value, bit)), axis=1)
    return value


def scatter_half(value, half):
    for bit in reversed(bits_below(half)):
        low, high = jnp.split(value, 2, axis=1)
        clear = (lax.axis_index(AXIS) & bit) == 0
        value = jnp.where(clear, low, high) + flip(jnp.where(clear, high, low), bit)
    return value


def weigh(weights, source):
    rank = source.shape[0]
    blocks = source.astype(jnp.float32).reshape(rank, weights.shape[1], BLOCK)
    result = jnp.einsum("ksc,ts->ktc", blocks, weights, precision=lax.Precision.HIGHEST)
    return result.reshape(rank, weights.shape[0] * BLOCK)


def coupling(link_table, factors, widths):
    gene_width, peak_width = widths
    half = lax.axis_size(AXIS) // 2
    me = lax.axis_index(AXIS)
    side, place = me // half, me % half
    low = factors.astype(jnp.bfloat16)
    genes, peaks = low[:, : 2 * gene_width], low[:, 2 * gene_width :]
    own_gene = jnp.where(side == 0, genes[:, :gene_width], genes[:, gene_width:])
    side_blocks = half * gene_width // BLOCK
    peak_blocks = peak_width // BLOCK
    side_rows = lax.dynamic_slice_in_dim(link_table, side * side_blocks, side_blocks, 0)
    weights = jnp.concatenate(
        [
            lax.dynamic_slice_in_dim(side_rows, (place + s * half) * peak_blocks, peak_blocks, 1)
            for s in range(2)
        ],
        axis=1,
    )
    to_gene = scatter_half(weigh(weights, peaks), half)
    to_peak = weigh(weights.T, gather_half(own_gene, half))
    nothing = jnp.zeros_like(to_gene)
    return jnp.concatenate([*(jnp.where(side == s, to_gene, nothing) for s in range(2)), to_peak], axis=1)


def shards(
    rna_counts,
    atac_counts,
    cell_factor,
    gene_factor,
    peak_factor,
    link_gene,
    link_peak,
    link_weight,
    link_count,
):
    count = lax.axis_size(AXIS)
    half = count // 2
    me = lax.axis_index(AXIS)
    side = me // half
    rank, cells = cell_factor.shape
    gene_width, peak_width = gene_factor.shape[1], peak_factor.shape[1]
    features = 2 * (gene_width + peak_width)
    link_scale = cells * count / 4.0

    link_table = own_table(
        link_gene,
        link_peak,
        link_weight,
        link_count,
        rna_counts.shape[1] // BLOCK,
        atac_counts.shape[1] // BLOCK,
    )
    for bit in bits_below(count):
        link_table = link_table + flip(link_table, bit)

    def by_place(counts, width):
        return counts.reshape(cells, 2, half, width).transpose(2, 0, 1, 3).reshape(half, cells, 2 * width)

    cell_pair = jnp.concatenate([part.T for part in split_low(cell_factor)], axis=1)
    parcels = jnp.concatenate(
        [
            by_place(rna_counts, gene_width),
            by_place(atac_counts, peak_width),
            jnp.broadcast_to(cell_pair[None], (half, cells, 2 * rank)),
        ],
        axis=2,
    )
    halves = [list(range(half)), list(range(half, count))]
    received = lax.all_to_all(parcels, AXIS, 0, 0, axis_index_groups=halves, tiled=True)
    received = received.reshape(half * cells, features + 2 * rank)
    counts, cell_pair = received[:, :features], received[:, features:]

    gene_pair = in_order(half, gene_factor, flip(gene_factor, half))
    peak_pair = in_order(half, peak_factor, flip(peak_factor, half))
    factors = jnp.concatenate([*gene_pair, *peak_pair], axis=1)
    cell_low, cell_rest = cell_pair[:, :rank].T, cell_pair[:, rank:].T
    cell_state = cell_factor

    for sweep_index in range(ROUNDS):
        links = link_scale * coupling(link_table, factors, (gene_width, peak_width))
        pair = jnp.concatenate([cell_low, cell_rest], axis=0)
        squares = lax.dot_general(
            pair, pair, (((1,), (1,)), ((), ())), preferred_element_type=jnp.float32
        )
        gram_cells = (
            squares[:rank, :rank] + squares[:rank, rank:] + squares[rank:, :rank] + squares[rank:, rank:]
        )
        sums = jnp.dot(cell_low, counts, preferred_element_type=jnp.float32) + links
        groups = sums.reshape(rank, features // gene_width, gene_width)
        largest = jnp.max(groups, axis=2)
        scaled = (groups / largest[:, :, None]).astype(jnp.float16).reshape(rank, features)
        beside_other = flip(jnp.concatenate([gram_cells, largest], axis=1), half)
        groups_other = flip(scaled, half).astype(jnp.float32).reshape(groups.shape)
        gram_cells = gram_cells + beside_other[:, :rank]
        sums = sums + (groups_other * beside_other[:, rank:, None]).reshape(rank, features)
        factors = (
            factors
            * sums
            / (jnp.dot(gram_cells, factors, precision=lax.Precision.HIGHEST) + EPSILON)
        )
        low = factors.astype(jnp.bfloat16)
        gram_features = lax.dot_general(
            low, low, (((1,), (1,)), ((), ())), preferred_element_type=jnp.float32
        )
        cell_sums = lax.dot_general(
            low, counts, (((1,), (1,)), ((), ())), preferred_element_type=jnp.float32
        )
        last = sweep_index == ROUNDS - 1
        if last:
            for bit in reversed(bits_below(half)):
                left, right = jnp.split(cell_sums, 2, axis=1)
                clear = (me & bit) == 0
                sent = jnp.concatenate([jnp.where(clear, right, left), gram_features], axis=1)
                got = flip(sent, bit)
                kept = cell_sums.shape[1] // 2
                cell_sums = jnp.where(clear, left, right) + got[:, :kept]
                gram_features = gram_features + got[:, kept:]
        else:
            left, right = jnp.split(cell_sums, 2, axis=1)
            clear = (me & 1) == 0
            sent = jnp.concatenate([jnp.where(clear, right, left), gram_features], axis=1)
            kept = jnp.concatenate([jnp.where(clear, left, right), gram_features], axis=1)
            for bit in bits_below(half):
                kept = kept + flip(sent, bit)
                sent = kept
            width = cell_sums.shape[1] // 2
            cell_sums, gram_features = kept[:, :width], kept[:, width:]
            low_rest = [jnp.where(clear, *jnp.split(part, 2, axis=1)) for part in (cell_low, cell_rest)]
            cell_state = low_rest[0].astype(jnp.float32) + low_rest[1].astype(jnp.float32)
        cell_state = (
            cell_state
            * cell_sums
            / (jnp.dot(gram_features, cell_state, precision=lax.Precision.HIGHEST) + EPSILON)
        )
        if not last:
            pair = jnp.concatenate(split_low(cell_state), axis=0)
            pair = jnp.concatenate(in_order(1, pair, flip(pair, 1)), axis=1)
            cell_low, cell_rest = pair[:rank], pair[rank:]
            mine = lax.dynamic_slice_in_dim(pair, (me % half) * cells, cells, 1).astype(jnp.float32)
            cell_state = mine[:rank] + mine[rank:]

    def own(first, width):
        return jnp.where(side == 0, factors[:, first : first + width], factors[:, first + width : first + 2 * width])

    return cell_state, own(0, gene_width), own(2 * gene_width, peak_width)


def solution(mesh):
    columns = P(None, ("groups", "cells"))
    slots = P(("groups", "cells"))
    in_specs = (P(("groups", "cells"), None),) * 2 + (columns,) * 3 + (slots,) * 4
    return jax.shard_map(
        shards, mesh=mesh, in_specs=in_specs, out_specs=(columns,) * 3, check_vma=False
    )
```

```python
import functools

import jax
import jax.numpy as jnp
from jax import lax
from jax.experimental import pallas as pl
from jax.experimental.pallas import tpu as pltpu
from jax.sharding import PartitionSpec as P

BLOCK = 128
ROUNDS = 2
EPSILON = 1e-06
TINY = 1e-30
AXIS = "cells"
PARAMS = pltpu.CompilerParams(vmem_limit_bytes=32 * 1024 * 1024)
SMEM = pl.BlockSpec(memory_space=pltpu.SMEM)
VMEM = pl.BlockSpec(memory_space=pltpu.VMEM)


def flip(value, bit):
    count = lax.axis_size(AXIS)
    return lax.ppermute(value, AXIS, [(i, i ^ bit) for i in range(count)])


def in_order(bit, mine, other):
    mine_first = (lax.axis_index(AXIS) & bit) == 0
    return jnp.where(mine_first, mine, other), jnp.where(mine_first, other, mine)


def bits_below(size):
    return [1 << b for b in range(size.bit_length() - 1)]


def own_table(link_gene, link_peak, link_weight, link_count, gene_blocks, peak_blocks):
    slot_ids = jnp.arange(link_gene.shape[0], dtype=jnp.int32)
    live_weight = jnp.where(slot_ids < link_count[0], link_weight, 0).astype(jnp.float32)
    gene_hot = (link_gene[:, None] == jnp.arange(gene_blocks, dtype=jnp.int32)[None, :]).astype(
        jnp.float32
    )
    peak_hot = (link_peak[:, None] == jnp.arange(peak_blocks, dtype=jnp.int32)[None, :]).astype(
        jnp.float32
    )
    return jnp.dot((gene_hot * live_weight[:, None]).T, peak_hot, precision=lax.Precision.HIGHEST)


def split_low(value):
    high = lax.reduce_precision(value, exponent_bits=8, mantissa_bits=7)
    return high.astype(jnp.bfloat16), (value - high).astype(jnp.bfloat16)


def gather_half(value, half):
    for bit in bits_below(half):
        value = jnp.concatenate(in_order(bit, value, flip(value, bit)), axis=1)
    return value


def scatter_half(value, half):
    for bit in reversed(bits_below(half)):
        low, high = jnp.split(value, 2, axis=1)
        clear = (lax.axis_index(AXIS) & bit) == 0
        value = jnp.where(clear, low, high) + flip(jnp.where(clear, high, low), bit)
    return value


def weigh(weights, source):
    rank = source.shape[0]
    blocks = source.astype(jnp.float32).reshape(rank, weights.shape[1], BLOCK)
    result = jnp.einsum("ksc,ts->ktc", blocks, weights, precision=lax.Precision.HIGHEST)
    return result.reshape(rank, weights.shape[0] * BLOCK)


def coupling(link_table, factors, widths):
    gene_width, peak_width = widths
    half = lax.axis_size(AXIS) // 2
    me = lax.axis_index(AXIS)
    side, place = me // half, me % half
    low = factors.astype(jnp.bfloat16)
    genes, peaks = low[:, : 2 * gene_width], low[:, 2 * gene_width :]
    own_gene = jnp.where(side == 0, genes[:, :gene_width], genes[:, gene_width:])
    side_blocks = half * gene_width // BLOCK
    peak_blocks = peak_width // BLOCK
    side_rows = lax.dynamic_slice_in_dim(link_table, side * side_blocks, side_blocks, 0)
    weights = jnp.concatenate(
        [
            lax.dynamic_slice_in_dim(side_rows, (place + s * half) * peak_blocks, peak_blocks, 1)
            for s in range(2)
        ],
        axis=1,
    )
    to_gene = scatter_half(weigh(weights, peaks), half)
    to_peak = weigh(weights.T, gather_half(own_gene, half))
    nothing = jnp.zeros_like(to_gene)
    return jnp.concatenate([*(jnp.where(side == s, to_gene, nothing) for s in range(2)), to_peak], axis=1)


def shards_any(
    rna_counts,
    atac_counts,
    cell_factor,
    gene_factor,
    peak_factor,
    link_gene,
    link_peak,
    link_weight,
    link_count,
):
    count = lax.axis_size(AXIS)
    half = count // 2
    me = lax.axis_index(AXIS)
    side = me // half
    rank, cells = cell_factor.shape
    gene_width, peak_width = gene_factor.shape[1], peak_factor.shape[1]
    features = 2 * (gene_width + peak_width)
    link_scale = cells * count / 4.0

    link_table = own_table(
        link_gene,
        link_peak,
        link_weight,
        link_count,
        rna_counts.shape[1] // BLOCK,
        atac_counts.shape[1] // BLOCK,
    )
    for bit in bits_below(count):
        link_table = link_table + flip(link_table, bit)

    def by_place(counts, width):
        return counts.reshape(cells, 2, half, width).transpose(2, 0, 1, 3).reshape(half, cells, 2 * width)

    cell_pair = jnp.concatenate([part.T for part in split_low(cell_factor)], axis=1)
    parcels = jnp.concatenate(
        [
            by_place(rna_counts, gene_width),
            by_place(atac_counts, peak_width),
            jnp.broadcast_to(cell_pair[None], (half, cells, 2 * rank)),
        ],
        axis=2,
    )
    halves = [list(range(half)), list(range(half, count))]
    received = lax.all_to_all(parcels, AXIS, 0, 0, axis_index_groups=halves, tiled=True)
    received = received.reshape(half * cells, features + 2 * rank)
    counts, cell_pair = received[:, :features], received[:, features:]

    gene_pair = in_order(half, gene_factor, flip(gene_factor, half))
    peak_pair = in_order(half, peak_factor, flip(peak_factor, half))
    factors = jnp.concatenate([*gene_pair, *peak_pair], axis=1)
    cell_low, cell_rest = cell_pair[:, :rank].T, cell_pair[:, rank:].T
    cell_state = cell_factor

    for sweep_index in range(ROUNDS):
        links = link_scale * coupling(link_table, factors, (gene_width, peak_width))
        pair = jnp.concatenate([cell_low, cell_rest], axis=0)
        squares = lax.dot_general(
            pair, pair, (((1,), (1,)), ((), ())), preferred_element_type=jnp.float32
        )
        gram_cells = (
            squares[:rank, :rank] + squares[:rank, rank:] + squares[rank:, :rank] + squares[rank:, rank:]
        )
        sums = jnp.dot(cell_low, counts, preferred_element_type=jnp.float32) + links
        groups = sums.reshape(rank, features // gene_width, gene_width)
        largest = jnp.max(groups, axis=2)
        scaled = (groups / largest[:, :, None]).astype(jnp.float16).reshape(rank, features)
        beside_other = flip(jnp.concatenate([gram_cells, largest], axis=1), half)
        groups_other = flip(scaled, half).astype(jnp.float32).reshape(groups.shape)
        gram_cells = gram_cells + beside_other[:, :rank]
        sums = sums + (groups_other * beside_other[:, rank:, None]).reshape(rank, features)
        factors = (
            factors
            * sums
            / (jnp.dot(gram_cells, factors, precision=lax.Precision.HIGHEST) + EPSILON)
        )
        low = factors.astype(jnp.bfloat16)
        gram_features = lax.dot_general(
            low, low, (((1,), (1,)), ((), ())), preferred_element_type=jnp.float32
        )
        cell_sums = lax.dot_general(
            low, counts, (((1,), (1,)), ((), ())), preferred_element_type=jnp.float32
        )
        last = sweep_index == ROUNDS - 1
        if last:
            for bit in reversed(bits_below(half)):
                left, right = jnp.split(cell_sums, 2, axis=1)
                clear = (me & bit) == 0
                sent = jnp.concatenate([jnp.where(clear, right, left), gram_features], axis=1)
                got = flip(sent, bit)
                kept = cell_sums.shape[1] // 2
                cell_sums = jnp.where(clear, left, right) + got[:, :kept]
                gram_features = gram_features + got[:, kept:]
        else:
            left, right = jnp.split(cell_sums, 2, axis=1)
            clear = (me & 1) == 0
            sent = jnp.concatenate([jnp.where(clear, right, left), gram_features], axis=1)
            kept = jnp.concatenate([jnp.where(clear, left, right), gram_features], axis=1)
            for bit in bits_below(half):
                kept = kept + flip(sent, bit)
                sent = kept
            width = cell_sums.shape[1] // 2
            cell_sums, gram_features = kept[:, :width], kept[:, width:]
            low_rest = [jnp.where(clear, *jnp.split(part, 2, axis=1)) for part in (cell_low, cell_rest)]
            cell_state = low_rest[0].astype(jnp.float32) + low_rest[1].astype(jnp.float32)
        cell_state = (
            cell_state
            * cell_sums
            / (jnp.dot(gram_features, cell_state, precision=lax.Precision.HIGHEST) + EPSILON)
        )
        if not last:
            pair = jnp.concatenate(split_low(cell_state), axis=0)
            pair = jnp.concatenate(in_order(1, pair, flip(pair, 1)), axis=1)
            cell_low, cell_rest = pair[:rank], pair[rank:]
            mine = lax.dynamic_slice_in_dim(pair, (me % half) * cells, cells, 1).astype(jnp.float32)
            cell_state = mine[:rank] + mine[rank:]

    def own(first, width):
        return jnp.where(side == 0, factors[:, first : first + width], factors[:, first + width : first + 2 * width])

    return cell_state, own(0, gene_width), own(2 * gene_width, peak_width)


def layout(bits):
    size = 1 << len(bits)
    return [
        sum(bit for i, bit in enumerate(bits) if position >> (len(bits) - 1 - i) & 1)
        for position in range(size)
    ]


def turned(bits, by):
    return bits[by:] + bits[:by]


def across(left, right):
    return lax.dot_general(left, right, (((1,), (1,)), ((), ())), preferred_element_type=jnp.float32)


def exact(left, right):
    return lax.dot_general(
        left,
        right,
        (((1,), (0,)), ((), ())),
        precision=lax.Precision.HIGHEST,
        preferred_element_type=jnp.float32,
    )


def halved(value):
    high = value.astype(jnp.bfloat16)
    return high, (value - high.astype(jnp.float32)).astype(jnp.bfloat16)


def struct(*shape, dtype=jnp.float32):
    return jax.ShapeDtypeStruct(shape, dtype)


def gram_of(high, rest):
    pair = jnp.concatenate([high, rest], axis=0)
    squares = across(pair, pair)
    rank = high.shape[0]
    return (squares[:rank, :rank] + squares[rank:, rank:]) + (squares[:rank, rank:] + squares[rank:, :rank])


def parcels_kernel(rna_0, rna_1, atac_0, atac_1, cell, gene, peak, slots, out):
    rank = cell.shape[0]
    cells = rna_0.shape[0]
    gene_width, peak_width = gene.shape[1], peak.shape[1]
    width = gene_width + peak_width
    cell_pair = jnp.concatenate(halved(cell[...]), axis=1)
    gene_low = gene[...].astype(jnp.bfloat16)
    peak_low = peak[...].astype(jnp.bfloat16)
    part = rank // 4
    for j in range(out.shape[0]):
        at = 0
        for source, size in ((rna_0, gene_width), (rna_1, gene_width), (atac_0, peak_width), (atac_1, peak_width)):
            out[j, 0:cells, at : at + size] = source[:, j * size : (j + 1) * size]
            at += size
        out[j, 0:cells, at:] = cell_pair
        for s in range(2):
            row = (2 * (j % 2) + s) * part
            out[j, cells:, s * width : s * width + gene_width] = gene_low[row : row + part]
            out[j, cells:, s * width + gene_width : (s + 1) * width] = peak_low[row : row + part]
        out[j, cells:, 2 * width :] = slots[...]


def parcels(rna_counts, atac_counts, cell_factor, gene_factor, peak_factor, slots, half):
    cells = rna_counts.shape[0]
    rank = cell_factor.shape[0]
    gene_width, peak_width = gene_factor.shape[1], peak_factor.shape[1]
    rows, lanes = cells + rank // 4, 2 * (gene_width + peak_width) + 2 * rank
    each = 4
    steps = half // each

    def columns(width, side):
        return pl.BlockSpec((cells, each * width), lambda i: (0, i + side * steps))

    def whole(array):
        return pl.BlockSpec(array.shape, lambda i: (0, 0))

    return pl.pallas_call(
        parcels_kernel,
        grid=(steps,),
        in_specs=[columns(gene_width, 0), columns(gene_width, 1), columns(peak_width, 0), columns(peak_width, 1)]
        + [whole(a) for a in (cell_factor, gene_factor, peak_factor, slots)],
        out_specs=pl.BlockSpec((each, rows, lanes), lambda i: (i, 0, 0)),
        out_shape=struct(half, rows, lanes, dtype=jnp.bfloat16),
        compiler_params=PARAMS,
    )(rna_counts, rna_counts, atac_counts, atac_counts, cell_factor, gene_factor, peak_factor, slots)


def first_sums_kernel(received, sums, gram):
    half, cells, features = received.shape[0], received.shape[1] - sums.shape[0] // 4, sums.shape[1]
    rank = sums.shape[0]
    high = jnp.concatenate([received[j, 0:cells, features : features + rank] for j in range(half)], axis=1)
    rest = jnp.concatenate([received[j, 0:cells, features + rank :] for j in range(half)], axis=1)
    counts = jnp.concatenate([received[j, 0:cells, 0:features] for j in range(half)], axis=0)
    sums[...] = jnp.dot(high, counts, preferred_element_type=jnp.float32)
    gram[...] = gram_of(high, rest)


def finish_sums(sums_value, gram_value, widths, sums, scaled, beside):
    rank, features = sums_value.shape
    largest = []
    for b in range(features // BLOCK):
        group = sums_value[:, b * BLOCK : (b + 1) * BLOCK]
        top = jnp.maximum(jnp.max(group, axis=1, keepdims=True), TINY)
        sums[:, b * BLOCK : (b + 1) * BLOCK] = group
        scaled[:, b * BLOCK : (b + 1) * BLOCK] = group / top
        largest.append(top)
    pad = jnp.zeros((rank, beside.shape[1] - rank - len(largest)), jnp.float32)
    beside[...] = jnp.concatenate([gram_value, *largest, pad], axis=1)


def first_links_kernel(
    link_scale, widths, spot, mine, other, sums_in, gram, sums, scaled, beside, table, table_sem, table_smem
):
    half = mine.shape[0]
    rank, features = sums_in.shape
    gene_width, peak_width = widths
    gene_blocks, peak_blocks = gene_width // BLOCK, peak_width // BLOCK
    width = gene_width + peak_width
    slots = mine[:, :, 2 * width :].reshape(half * mine.shape[1], 2 * rank).astype(jnp.float32)

    def hot(column, size, value):
        ids = lax.broadcasted_iota(jnp.int32, (slots.shape[0], size), 1).astype(jnp.float32)
        return jnp.where(slots[:, column : column + 1] == ids, value, 0.0).astype(jnp.bfloat16)

    table[...] = lax.dot_general(
        hot(0, table.shape[0], slots[:, 2:3]),
        hot(1, table.shape[1], 1.0),
        (((0,), (0,)), ((), ())),
        preferred_element_type=jnp.float32,
    )
    copy = pltpu.make_async_copy(table, table_smem, table_sem)
    copy.start()
    copy.wait()
    side, place, core = spot[0], spot[1], spot[2]
    total = [None] * (features // BLOCK)

    def add(target, weight, block):
        term = weight * block
        total[target] = term if total[target] is None else total[target] + term

    for j in range(half):
        blocks = []
        for b in range(width // BLOCK):
            pieces = [
                ref[j, :, s * width + b * BLOCK : s * width + (b + 1) * BLOCK] for ref in (mine, other) for s in range(2)
            ]
            blocks.append(jnp.concatenate(pieces, axis=0).astype(jnp.float32))
        for b in range(gene_blocks):
            row = (side * half + j) * gene_blocks + b
            for u in range(2 * peak_blocks):
                column = (place + u // peak_blocks * half) * peak_blocks + u % peak_blocks
                add(2 * gene_blocks + u, table_smem[row, column], blocks[b])
        for b in range(peak_blocks):
            column = (side * half + j) * peak_blocks + b
            for t in range(2 * gene_blocks):
                row = (place + t // gene_blocks * half) * gene_blocks + t % gene_blocks
                add(t, table_smem[row, column], blocks[gene_blocks + b])
    links = jnp.concatenate(total, axis=1)
    ahead, behind = links[: rank // 2], links[rank // 2 :]
    first = core == 0
    links = jnp.concatenate([jnp.where(first, ahead, behind), jnp.where(first, behind, ahead)], axis=0)
    finish_sums(sums_in[...] + link_scale * links, gram[...], widths, sums, scaled, beside)


def next_sums_kernel(
    link_scale, widths, orders, spot, table, mine, other, received, to_gene, genes, sums, scaled, beside
):
    half = received.shape[0]
    rank, features = sums.shape
    cells = mine.shape[1] * 2 // (2 * half)
    gene_width, peak_width = widths
    gene_blocks, peak_blocks = gene_width // BLOCK, peak_width // BLOCK
    side, place, core = spot[0], spot[1], spot[2]
    first = core == 0
    left, right = mine[...], other[...]
    even, odd = jnp.where(first, left, right), jnp.where(first, right, left)
    kept = half // 2 * cells
    high = jnp.concatenate([even[:, :kept], odd[:, :kept]], axis=1)
    rest = jnp.concatenate([even[:, kept:], odd[:, kept:]], axis=1)
    counts = jnp.concatenate([received[j, 0:cells, 0:features] for j in orders[0]], axis=0)
    products = jnp.dot(high, counts, preferred_element_type=jnp.float32)
    total = [None] * (2 * peak_blocks)
    for position, j in enumerate(orders[1]):
        for b in range(gene_blocks):
            at = (position * gene_blocks + b) * BLOCK
            block = genes[:, at : at + BLOCK].astype(jnp.float32)
            row = (side * half + j) * gene_blocks + b
            for u in range(2 * peak_blocks):
                column = (place + u // peak_blocks * half) * peak_blocks + u % peak_blocks
                term = table[row, column] * block
                total[u] = term if total[u] is None else total[u] + term
    gene_links = to_gene[...]
    nothing = jnp.zeros_like(gene_links)
    links = jnp.concatenate(
        [jnp.where(side == 0, gene_links, nothing), jnp.where(side == 0, nothing, gene_links), *total], axis=1
    )
    finish_sums(products + link_scale * links, gram_of(high, rest), widths, sums, scaled, beside)


def update_kernel(last, widths, orders, spot, table, sums, other, beside, beside_other, factors, received, *outs):
    half = received.shape[0]
    rank, features = sums.shape
    cells = received.shape[1] - rank // 4
    gene_width, peak_width = widths
    gene_blocks, peak_blocks = gene_width // BLOCK, peak_width // BLOCK
    side, place, core = spot[0], spot[1], spot[2]
    first = core == 0
    gram = beside[:, 0:rank] + beside_other[:, 0:rank]
    old = factors[...]
    below = exact(gram, old) + EPSILON
    whole = jnp.concatenate(
        [
            sums[:, b * BLOCK : (b + 1) * BLOCK]
            + other[:, b * BLOCK : (b + 1) * BLOCK] * beside_other[:, rank + b : rank + b + 1]
            for b in range(features // BLOCK)
        ],
        axis=1,
    )
    new = old * whole / below
    low = new.astype(jnp.bfloat16)
    cell_sums = jnp.concatenate([across(low, received[j, 0:cells, 0:features]) for j in orders[0]], axis=1)
    gram_features = across(low, low)
    kept, sent, *outs = outs
    split = half // 2 * cells
    left, right = cell_sums[:, :split], cell_sums[:, split:]
    for ref, value in ((kept, jnp.where(first, left, right)), (sent, jnp.where(first, right, left))):
        ref[:, :split] = value
        ref[:, split : split + rank] = gram_features
        ref[:, split + rank :] = jnp.zeros((rank, ref.shape[1] - split - rank), jnp.float32)

    def own(at, width):
        return jnp.where(side == 0, new[:, at : at + width], new[:, at + width : at + 2 * width])

    if last:
        gene_out, peak_out = outs
        gene_out[...] = own(0, gene_width)
        peak_out[...] = own(2 * gene_width, peak_width)
        return
    factors_out, links_kept, links_sent, gene_low = outs
    factors_out[...] = new
    gene_low[...] = own(0, gene_width).astype(jnp.bfloat16)
    peaks = low[:, 2 * gene_width :].astype(jnp.float32)
    peaks = [peaks[:, u * BLOCK : (u + 1) * BLOCK] for u in range(2 * peak_blocks)]
    for position in range(half // 2):
        pair = []
        for j in (orders[1][position], orders[1][position + half // 2]):
            parts = []
            for b in range(gene_blocks):
                row = (side * half + j) * gene_blocks + b
                part = None
                for u, block in enumerate(peaks):
                    column = (place + u // peak_blocks * half) * peak_blocks + u % peak_blocks
                    term = table[row, column] * block
                    part = term if part is None else part + term
                parts.append(part)
            pair.append(jnp.concatenate(parts, axis=1))
        at = position * gene_width
        links_kept[:, at : at + gene_width] = jnp.where(first, *pair)
        links_sent[:, at : at + gene_width] = jnp.where(first, pair[1], pair[0])


def cells_kernel(order, spot, totals, received_cells, pair, own):
    rank = totals.shape[0]
    cells = own.shape[1]
    kept = cells * len(order) // 2
    place, core = spot[1], spot[2]
    first = core == 0

    def state(j):
        terms = received_cells[j].astype(jnp.float32)
        return terms[:, :rank] + terms[:, rank:]

    old = jnp.concatenate(
        [
            jnp.where(first, state(order[s]), state(order[s + len(order) // 2]))
            for s in range(len(order) // 2)
        ],
        axis=1,
    )
    new = old * totals[:, :kept] / (exact(totals[:, kept : kept + rank], old) + EPSILON)
    pair[...] = jnp.concatenate(halved(new), axis=1)
    mine = new[:, :cells]
    for s in range(1, len(order) // 2):
        mine = jnp.where(place // 2 == order[s] // 2, new[:, s * cells : (s + 1) * cells], mine)
    own[...] = mine


def shards_blocks(
    rna_counts,
    atac_counts,
    cell_factor,
    gene_factor,
    peak_factor,
    link_gene,
    link_peak,
    link_weight,
    link_count,
):
    count = lax.axis_size(AXIS)
    half = count // 2
    me = lax.axis_index(AXIS)
    side, place, core = me // half, me % half, me % 2
    spot = jnp.stack([side, place, core]).astype(jnp.int32)
    rank, cells = cell_factor.shape
    gene_width, peak_width = gene_factor.shape[1], peak_factor.shape[1]
    widths = (gene_width, peak_width)
    width = gene_width + peak_width
    features = 2 * width
    link_scale = cells * count / 4.0
    table_shape = (rna_counts.shape[1] // BLOCK, atac_counts.shape[1] // BLOCK)
    chip_bits = bits_below(half)[1:]
    cell_bits, link_bits, gene_bits = (turned(chip_bits, i % len(chip_bits)) for i in range(3))
    cell_order = layout([1] + cell_bits)
    link_order = layout([1] + link_bits)
    gene_order = layout([1] + gene_bits[::-1])

    live = jnp.arange(link_gene.shape[0], dtype=jnp.int32) < link_count[0]
    slots = jnp.stack([link_gene, link_peak, jnp.where(live, link_weight, 0)], axis=1).astype(jnp.float32)
    slots = jnp.pad(slots, ((0, 0), (0, 2 * rank - slots.shape[1])))
    slots_other = flip(slots, half)
    state = jnp.concatenate([gene_factor, peak_factor], axis=1)
    state_other = flip(state, half)
    slots = jnp.concatenate([slots, slots_other], axis=0)
    slots = jnp.pad(slots, ((0, rank // 4 - slots.shape[0]), (0, 0))).astype(jnp.bfloat16)
    sent = parcels(rna_counts, atac_counts, cell_factor, gene_factor, peak_factor, slots, half)
    halves = [list(range(half)), list(range(half, count))]
    received = lax.all_to_all(sent, AXIS, 0, 0, axis_index_groups=halves, tiled=True)
    low, high = in_order(half, state, state_other)
    factors = jnp.concatenate(
        [low[:, :gene_width], high[:, :gene_width], low[:, gene_width:], high[:, gene_width:]], axis=1
    )

    sums_shapes = (struct(rank, features), struct(rank, features), struct(rank, 2 * rank))
    rows_other = flip(received[:, cells:, :features], 1)
    sums, gram = pl.pallas_call(
        first_sums_kernel,
        in_specs=[VMEM],
        out_specs=[VMEM] * 2,
        out_shape=(struct(rank, features), struct(rank, rank)),
        compiler_params=PARAMS,
    )(received)
    rows = rank // 4
    sums, scaled, beside, link_table = pl.pallas_call(
        functools.partial(first_links_kernel, link_scale, widths),
        grid=(1,),
        in_specs=[
            SMEM,
            pl.BlockSpec((half, rows, features + 2 * rank), lambda i: (0, cells // rows, 0)),
            VMEM,
            VMEM,
            VMEM,
        ],
        out_specs=[VMEM] * 4,
        out_shape=(*sums_shapes, struct(*table_shape)),
        scratch_shapes=[pltpu.SemaphoreType.DMA, pltpu.SMEM(table_shape, jnp.float32)],
        compiler_params=PARAMS,
    )(spot, received, rows_other, sums, gram)

    split = half // 2 * cells
    for sweep_index in range(ROUNDS):
        last = sweep_index == ROUNDS - 1
        beside_other = flip(beside, half)
        other = flip(scaled.astype(jnp.float16), half).astype(jnp.float32)
        lanes = -(-(split + rank) // BLOCK) * BLOCK
        outs = [struct(rank, lanes)] * 2
        if last:
            outs += [struct(rank, gene_width), struct(rank, peak_width)]
        else:
            outs += [struct(rank, features)] + [struct(rank, half // 2 * gene_width)] * 2
            outs += [struct(rank, gene_width, dtype=jnp.bfloat16)]
        kept, sent, *outs = pl.pallas_call(
            functools.partial(update_kernel, last, widths, (cell_order, link_order)),
            in_specs=[SMEM] * 2 + [VMEM] * 6,
            out_specs=[VMEM] * len(outs),
            out_shape=outs,
            compiler_params=PARAMS,
        )(spot, link_table, sums, other, beside, beside_other, factors, received)
        if last:
            gene_out, peak_out = outs
            totals = kept + flip(sent, 1)
            cell_sums, gram_features = totals[:, :split], totals[:, split : split + rank]
            for bit in cell_bits:
                left, right = jnp.split(cell_sums, 2, axis=1)
                clear = (me & bit) == 0
                got = flip(jnp.concatenate([jnp.where(clear, right, left), gram_features], axis=1), bit)
                cell_sums = jnp.where(clear, left, right) + got[:, : left.shape[1]]
                gram_features = gram_features + got[:, left.shape[1] :]
            cell_out = own_cells * cell_sums / (exact(gram_features, own_cells) + EPSILON)
            return cell_out, gene_out, peak_out
        factors, links_kept, links_sent, genes = outs
        totals = kept + flip(sent, 1)
        to_gene = links_kept + flip(links_sent, 1)
        for cell_bit, link_bit, gene_bit in zip(cell_bits, link_bits, gene_bits):
            totals_other = flip(totals, cell_bit)
            left, right = jnp.split(to_gene, 2, axis=1)
            clear = (me & link_bit) == 0
            to_gene_other = flip(jnp.where(clear, right, left), link_bit)
            genes_other = flip(genes, gene_bit)
            totals = totals + totals_other
            to_gene = jnp.where(clear, left, right) + to_gene_other
            genes = jnp.concatenate(in_order(gene_bit, genes, genes_other), axis=1)
        genes = jnp.concatenate(in_order(1, genes, flip(genes, 1)), axis=1)
        pair, own_cells = pl.pallas_call(
            functools.partial(cells_kernel, cell_order),
            grid=(1,),
            in_specs=[
                SMEM,
                VMEM,
                pl.BlockSpec((half, cells, 2 * rank), lambda i: (0, 0, features // (2 * rank))),
            ],
            out_specs=[VMEM] * 2,
            out_shape=(struct(rank, 2 * split, dtype=jnp.bfloat16), struct(rank, cells)),
            compiler_params=PARAMS,
        )(spot, totals, received)
        sums, scaled, beside = pl.pallas_call(
            functools.partial(next_sums_kernel, link_scale, widths, (cell_order, gene_order)),
            in_specs=[SMEM] * 2 + [VMEM] * 5,
            out_specs=[VMEM] * 3,
            out_shape=sums_shapes,
            compiler_params=PARAMS,
        )(spot, link_table, pair, flip(pair, 1), received, to_gene, genes)


def shards(rna_counts, atac_counts, cell_factor, gene_factor, peak_factor, link_gene, *links):
    half = lax.axis_size(AXIS) // 2
    rank, cells = cell_factor.shape
    gene_width, peak_width = gene_factor.shape[1], peak_factor.shape[1]
    features = 2 * (gene_width + peak_width)
    in_blocks = (
        half % 8 == 0
        and rank == cells
        and 2 * rank == BLOCK
        and gene_width % BLOCK == 0
        and peak_width % BLOCK == 0
        and features // BLOCK <= rank
        and 2 * link_gene.shape[0] <= rank // 4
        and max(rna_counts.shape[1], atac_counts.shape[1]) // BLOCK <= 256
    )
    run = shards_blocks if in_blocks else shards_any
    return run(rna_counts, atac_counts, cell_factor, gene_factor, peak_factor, link_gene, *links)


def solution(mesh):
    columns = P(None, ("groups", "cells"))
    slots = P(("groups", "cells"))
    in_specs = (P(("groups", "cells"), None),) * 2 + (columns,) * 3 + (slots,) * 4
    return jax.shard_map(
        shards, mesh=mesh, in_specs=in_specs, out_specs=(columns,) * 3, check_vma=False
    )
```

```python
import functools

import jax
import jax.numpy as jnp
from jax import lax
from jax.experimental import pallas as pl
from jax.experimental.pallas import tpu as pltpu
from jax.sharding import PartitionSpec as P

BLOCK = 128
ROUNDS = 2
EPSILON = 1e-06
CODES = 65535.0
AXIS = "cells"
PARAMS = pltpu.CompilerParams(vmem_limit_bytes=14 * 1024 * 1024)
SMEM = pl.BlockSpec(memory_space=pltpu.SMEM)
VMEM = pl.BlockSpec(memory_space=pltpu.VMEM)


def flip(value, bit):
    count = lax.axis_size(AXIS)
    return lax.ppermute(value, AXIS, [(i, i ^ bit) for i in range(count)])


def in_order(bit, mine, other):
    mine_first = (lax.axis_index(AXIS) & bit) == 0
    return jnp.where(mine_first, mine, other), jnp.where(mine_first, other, mine)


def bits_below(size):
    return [1 << b for b in range(size.bit_length() - 1)]


def own_table(link_gene, link_peak, link_weight, link_count, gene_blocks, peak_blocks):
    slot_ids = jnp.arange(link_gene.shape[0], dtype=jnp.int32)
    live_weight = jnp.where(slot_ids < link_count[0], link_weight, 0).astype(jnp.float32)
    gene_hot = (link_gene[:, None] == jnp.arange(gene_blocks, dtype=jnp.int32)[None, :]).astype(
        jnp.float32
    )
    peak_hot = (link_peak[:, None] == jnp.arange(peak_blocks, dtype=jnp.int32)[None, :]).astype(
        jnp.float32
    )
    return jnp.dot((gene_hot * live_weight[:, None]).T, peak_hot, precision=lax.Precision.HIGHEST)


def split_low(value):
    high = lax.reduce_precision(value, exponent_bits=8, mantissa_bits=7)
    return high.astype(jnp.bfloat16), (value - high).astype(jnp.bfloat16)


def gather_half(value, half):
    for bit in bits_below(half):
        value = jnp.concatenate(in_order(bit, value, flip(value, bit)), axis=1)
    return value


def scatter_half(value, half):
    for bit in reversed(bits_below(half)):
        low, high = jnp.split(value, 2, axis=1)
        clear = (lax.axis_index(AXIS) & bit) == 0
        value = jnp.where(clear, low, high) + flip(jnp.where(clear, high, low), bit)
    return value


def weigh(weights, source):
    rank = source.shape[0]
    blocks = source.astype(jnp.float32).reshape(rank, weights.shape[1], BLOCK)
    result = jnp.einsum("ksc,ts->ktc", blocks, weights, precision=lax.Precision.HIGHEST)
    return result.reshape(rank, weights.shape[0] * BLOCK)


def coupling(link_table, factors, widths):
    gene_width, peak_width = widths
    half = lax.axis_size(AXIS) // 2
    me = lax.axis_index(AXIS)
    side, place = me // half, me % half
    low = factors.astype(jnp.bfloat16)
    genes, peaks = low[:, : 2 * gene_width], low[:, 2 * gene_width :]
    own_gene = jnp.where(side == 0, genes[:, :gene_width], genes[:, gene_width:])
    side_blocks = half * gene_width // BLOCK
    peak_blocks = peak_width // BLOCK
    side_rows = lax.dynamic_slice_in_dim(link_table, side * side_blocks, side_blocks, 0)
    weights = jnp.concatenate(
        [
            lax.dynamic_slice_in_dim(side_rows, (place + s * half) * peak_blocks, peak_blocks, 1)
            for s in range(2)
        ],
        axis=1,
    )
    to_gene = scatter_half(weigh(weights, peaks), half)
    to_peak = weigh(weights.T, gather_half(own_gene, half))
    nothing = jnp.zeros_like(to_gene)
    return jnp.concatenate([*(jnp.where(side == s, to_gene, nothing) for s in range(2)), to_peak], axis=1)


def shards_any(
    rna_counts,
    atac_counts,
    cell_factor,
    gene_factor,
    peak_factor,
    link_gene,
    link_peak,
    link_weight,
    link_count,
):
    count = lax.axis_size(AXIS)
    half = count // 2
    me = lax.axis_index(AXIS)
    side = me // half
    rank, cells = cell_factor.shape
    gene_width, peak_width = gene_factor.shape[1], peak_factor.shape[1]
    features = 2 * (gene_width + peak_width)
    link_scale = cells * count / 4.0

    link_table = own_table(
        link_gene,
        link_peak,
        link_weight,
        link_count,
        rna_counts.shape[1] // BLOCK,
        atac_counts.shape[1] // BLOCK,
    )
    for bit in bits_below(count):
        link_table = link_table + flip(link_table, bit)

    def by_place(counts, width):
        return counts.reshape(cells, 2, half, width).transpose(2, 0, 1, 3).reshape(half, cells, 2 * width)

    cell_pair = jnp.concatenate([part.T for part in split_low(cell_factor)], axis=1)
    parcels = jnp.concatenate(
        [
            by_place(rna_counts, gene_width),
            by_place(atac_counts, peak_width),
            jnp.broadcast_to(cell_pair[None], (half, cells, 2 * rank)),
        ],
        axis=2,
    )
    halves = [list(range(half)), list(range(half, count))]
    received = lax.all_to_all(parcels, AXIS, 0, 0, axis_index_groups=halves, tiled=True)
    received = received.reshape(half * cells, features + 2 * rank)
    counts, cell_pair = received[:, :features], received[:, features:]

    gene_pair = in_order(half, gene_factor, flip(gene_factor, half))
    peak_pair = in_order(half, peak_factor, flip(peak_factor, half))
    factors = jnp.concatenate([*gene_pair, *peak_pair], axis=1)
    cell_low, cell_rest = cell_pair[:, :rank].T, cell_pair[:, rank:].T
    cell_state = cell_factor

    for sweep_index in range(ROUNDS):
        links = link_scale * coupling(link_table, factors, (gene_width, peak_width))
        pair = jnp.concatenate([cell_low, cell_rest], axis=0)
        squares = lax.dot_general(
            pair, pair, (((1,), (1,)), ((), ())), preferred_element_type=jnp.float32
        )
        gram_cells = (
            squares[:rank, :rank] + squares[:rank, rank:] + squares[rank:, :rank] + squares[rank:, rank:]
        )
        sums = jnp.dot(cell_low, counts, preferred_element_type=jnp.float32) + links
        gram_cells = gram_cells + flip(gram_cells, half)
        sums = sums + flip(sums, half)
        factors = (
            factors
            * sums
            / (jnp.dot(gram_cells, factors, precision=lax.Precision.HIGHEST) + EPSILON)
        )
        low = factors.astype(jnp.bfloat16)
        gram_features = lax.dot_general(
            low, low, (((1,), (1,)), ((), ())), preferred_element_type=jnp.float32
        )
        cell_sums = lax.dot_general(
            low, counts, (((1,), (1,)), ((), ())), preferred_element_type=jnp.float32
        )
        last = sweep_index == ROUNDS - 1
        if last:
            for bit in reversed(bits_below(half)):
                left, right = jnp.split(cell_sums, 2, axis=1)
                clear = (me & bit) == 0
                sent = jnp.concatenate([jnp.where(clear, right, left), gram_features], axis=1)
                got = flip(sent, bit)
                kept = cell_sums.shape[1] // 2
                cell_sums = jnp.where(clear, left, right) + got[:, :kept]
                gram_features = gram_features + got[:, kept:]
        else:
            left, right = jnp.split(cell_sums, 2, axis=1)
            clear = (me & 1) == 0
            sent = jnp.concatenate([jnp.where(clear, right, left), gram_features], axis=1)
            kept = jnp.concatenate([jnp.where(clear, left, right), gram_features], axis=1)
            for bit in bits_below(half):
                kept = kept + flip(sent, bit)
                sent = kept
            width = cell_sums.shape[1] // 2
            cell_sums, gram_features = kept[:, :width], kept[:, width:]
            low_rest = [jnp.where(clear, *jnp.split(part, 2, axis=1)) for part in (cell_low, cell_rest)]
            cell_state = low_rest[0].astype(jnp.float32) + low_rest[1].astype(jnp.float32)
        cell_state = (
            cell_state
            * cell_sums
            / (jnp.dot(gram_features, cell_state, precision=lax.Precision.HIGHEST) + EPSILON)
        )
        if not last:
            pair = jnp.concatenate(split_low(cell_state), axis=0)
            pair = jnp.concatenate(in_order(1, pair, flip(pair, 1)), axis=1)
            cell_low, cell_rest = pair[:rank], pair[rank:]
            mine = lax.dynamic_slice_in_dim(pair, (me % half) * cells, cells, 1).astype(jnp.float32)
            cell_state = mine[:rank] + mine[rank:]

    def own(first, width):
        return jnp.where(side == 0, factors[:, first : first + width], factors[:, first + width : first + 2 * width])

    return cell_state, own(0, gene_width), own(2 * gene_width, peak_width)


def layout(bits):
    size = 1 << len(bits)
    return [
        sum(bit for i, bit in enumerate(bits) if position >> (len(bits) - 1 - i) & 1)
        for position in range(size)
    ]


def turned(bits, by):
    return bits[by:] + bits[:by]


def across(left, right):
    return lax.dot_general(left, right, (((1,), (1,)), ((), ())), preferred_element_type=jnp.float32)


def exact(left, right):
    return lax.dot_general(
        left,
        right,
        (((1,), (0,)), ((), ())),
        precision=lax.Precision.HIGHEST,
        preferred_element_type=jnp.float32,
    )


def halved(value):
    high = value.astype(jnp.bfloat16)
    return high, (value - high.astype(jnp.float32)).astype(jnp.bfloat16)


def struct(*shape, dtype=jnp.float32):
    return jax.ShapeDtypeStruct(shape, dtype)


def gram_of(high, rest):
    pair = jnp.concatenate([high, rest], axis=0)
    squares = across(pair, pair)
    rank = high.shape[0]
    return (squares[:rank, :rank] + squares[rank:, rank:]) + (squares[:rank, rank:] + squares[rank:, :rank])


def parcels_kernel(rna_0, rna_1, atac_0, atac_1, cell, gene, peak, out):
    rank = cell.shape[0]
    cells = rna_0.shape[0]
    gene_width, peak_width = gene.shape[1], peak.shape[1]
    width = gene_width + peak_width
    cell_pair = jnp.concatenate(halved(cell[...]), axis=1)
    gene_low = gene[...].astype(jnp.bfloat16)
    peak_low = peak[...].astype(jnp.bfloat16)
    part = rank // 4
    for j in range(out.shape[0]):
        at = 0
        for source, size in ((rna_0, gene_width), (rna_1, gene_width), (atac_0, peak_width), (atac_1, peak_width)):
            out[j, 0:cells, at : at + size] = source[:, j * size : (j + 1) * size]
            at += size
        out[j, 0:cells, at:] = cell_pair
        for s in range(2):
            row = (2 * (j % 2) + s) * part
            out[j, cells:, s * width : s * width + gene_width] = gene_low[row : row + part]
            out[j, cells:, s * width + gene_width : (s + 1) * width] = peak_low[row : row + part]


def slots_kernel(spot, link_gene, link_peak, link_weight, link_count, out):
    slots = link_gene.shape[0]
    lane = lax.broadcasted_iota(jnp.int32, out.shape, 1) - spot[1] * slots
    row = lax.broadcasted_iota(jnp.int32, out.shape, 0)
    value = jnp.zeros(out.shape, jnp.float32)
    for s in range(slots):
        weight = jnp.where(s < link_count[0], link_weight[s], 0)
        for r, entry in enumerate((link_gene[s], link_peak[s], weight)):
            value = jnp.where((lane == s) & (row == r), entry.astype(jnp.float32), value)
    out[...] = value


def put_slots_kernel(mine, other, parcels_in, out, block, sems):
    block[...] = jnp.concatenate([mine[...], other[...]], axis=0).astype(jnp.bfloat16)
    half, rows, lanes = out.shape
    copies = [
        pltpu.make_async_copy(
            block, out.at[j, rows - block.shape[0] : rows, lanes - block.shape[1] : lanes], sems.at[j]
        )
        for j in range(half)
    ]
    for copy in copies:
        copy.start()
    for copy in copies:
        copy.wait()


def put_slots(mine, other, parcels_value):
    anywhere = pl.BlockSpec(memory_space=pl.ANY)
    return pl.pallas_call(
        put_slots_kernel,
        in_specs=[VMEM, VMEM, anywhere],
        out_specs=anywhere,
        out_shape=struct(*parcels_value.shape, dtype=parcels_value.dtype),
        scratch_shapes=[
            pltpu.VMEM((2 * mine.shape[0], mine.shape[1]), jnp.bfloat16),
            pltpu.SemaphoreType.DMA((parcels_value.shape[0],)),
        ],
        input_output_aliases={2: 0},
        compiler_params=PARAMS,
    )(mine, other, parcels_value)


def parcels(rna_counts, atac_counts, cell_factor, gene_factor, peak_factor, half):
    cells = rna_counts.shape[0]
    rank = cell_factor.shape[0]
    gene_width, peak_width = gene_factor.shape[1], peak_factor.shape[1]
    rows, lanes = cells + rank // 4, 2 * (gene_width + peak_width) + 2 * rank
    each = 4
    steps = half // each

    def columns(width, side):
        return pl.BlockSpec((cells, each * width), lambda i: (0, i + side * steps))

    def whole(array):
        return pl.BlockSpec(array.shape, lambda i: (0, 0))

    return pl.pallas_call(
        parcels_kernel,
        grid=(steps,),
        in_specs=[columns(gene_width, 0), columns(gene_width, 1), columns(peak_width, 0), columns(peak_width, 1)]
        + [whole(a) for a in (cell_factor, gene_factor, peak_factor)],
        out_specs=pl.BlockSpec((each, rows, lanes), lambda i: (i, 0, 0)),
        out_shape=struct(half, rows, lanes, dtype=jnp.bfloat16),
        compiler_params=PARAMS,
    )(rna_counts, rna_counts, atac_counts, atac_counts, cell_factor, gene_factor, peak_factor)


def first_sums_kernel(received, sums, gram):
    half, cells, features = received.shape[0], received.shape[1] - sums.shape[0] // 4, sums.shape[1]
    rank = sums.shape[0]
    high = jnp.concatenate([received[j, 0:cells, features : features + rank] for j in range(half)], axis=1)
    rest = jnp.concatenate([received[j, 0:cells, features + rank :] for j in range(half)], axis=1)
    counts = jnp.concatenate([received[j, 0:cells, 0:features] for j in range(half)], axis=0)
    sums[...] = jnp.dot(high, counts, preferred_element_type=jnp.float32)
    gram[...] = gram_of(high, rest)


def finish_sums(sums_value, gram_value, sums, coded, beside):
    rank, features = sums_value.shape
    least, step = [], []
    for b in range(features // BLOCK):
        group = sums_value[:, b * BLOCK : (b + 1) * BLOCK]
        sums[:, b * BLOCK : (b + 1) * BLOCK] = group
        low = jnp.min(group, axis=1, keepdims=True)
        spread = jnp.max(group, axis=1, keepdims=True) - low
        per = jnp.where(spread > 0.0, CODES / spread, 0.0)
        code = jnp.minimum(jnp.floor((group - low) * per + 0.5), CODES) - (CODES + 1) / 2
        coded[:, b * BLOCK : (b + 1) * BLOCK] = code.astype(jnp.int32).astype(jnp.int16)
        least.append(low)
        step.append(spread / CODES)
    pad = jnp.zeros((rank, beside.shape[1] - rank - 2 * len(least)), jnp.float32)
    beside[...] = jnp.concatenate([gram_value, *least, *step, pad], axis=1)


def first_links_kernel(
    link_scale, widths, spot, mine, other, sums_in, gram, sums, coded, beside, table, table_sem, table_smem
):
    half = mine.shape[0]
    rank, features = sums_in.shape
    gene_width, peak_width = widths
    gene_blocks, peak_blocks = gene_width // BLOCK, peak_width // BLOCK
    width = gene_width + peak_width
    slots = sum(mine[j, :, 2 * width :].astype(jnp.float32) for j in range(half))

    def hot(row, size, value):
        ids = lax.broadcasted_iota(jnp.int32, (size, slots.shape[1]), 0).astype(jnp.float32)
        return jnp.where(slots[row : row + 1] == ids, value, 0.0).astype(jnp.bfloat16)

    table[...] = sum(
        across(hot(row, table.shape[0], slots[row + 2 : row + 3]), hot(row + 1, table.shape[1], 1.0))
        for row in (0, slots.shape[0] // 2)
    )
    copy = pltpu.make_async_copy(table, table_smem, table_sem)
    copy.start()
    copy.wait()
    side, place, core = spot[0], spot[1], spot[2]
    total = [None] * (features // BLOCK)

    def add(target, weight, block):
        term = weight * block
        total[target] = term if total[target] is None else total[target] + term

    for j in range(half):
        blocks = []
        for b in range(width // BLOCK):
            pieces = [
                ref[j, :, s * width + b * BLOCK : s * width + (b + 1) * BLOCK] for ref in (mine, other) for s in range(2)
            ]
            blocks.append(jnp.concatenate(pieces, axis=0).astype(jnp.float32))
        for b in range(gene_blocks):
            row = (side * half + j) * gene_blocks + b
            for u in range(2 * peak_blocks):
                column = (place + u // peak_blocks * half) * peak_blocks + u % peak_blocks
                add(2 * gene_blocks + u, table_smem[row, column], blocks[b])
        for b in range(peak_blocks):
            column = (side * half + j) * peak_blocks + b
            for t in range(2 * gene_blocks):
                row = (place + t // gene_blocks * half) * gene_blocks + t % gene_blocks
                add(t, table_smem[row, column], blocks[gene_blocks + b])
    links = jnp.concatenate(total, axis=1)
    ahead, behind = links[: rank // 2], links[rank // 2 :]
    first = core == 0
    links = jnp.concatenate([jnp.where(first, ahead, behind), jnp.where(first, behind, ahead)], axis=0)
    finish_sums(sums_in[...] + link_scale * links, gram[...], sums, coded, beside)


def next_sums_kernel(
    link_scale, widths, orders, spot, table, mine, other, received, to_gene, genes, sums, coded, beside
):
    half = received.shape[0]
    rank, features = sums.shape
    cells = mine.shape[1] * 2 // (2 * half)
    gene_width, peak_width = widths
    gene_blocks, peak_blocks = gene_width // BLOCK, peak_width // BLOCK
    side, place, core = spot[0], spot[1], spot[2]
    first = core == 0
    left, right = mine[...], other[...]
    even, odd = jnp.where(first, left, right), jnp.where(first, right, left)
    kept = half // 2 * cells
    high = jnp.concatenate([even[:, :kept], odd[:, :kept]], axis=1)
    rest = jnp.concatenate([even[:, kept:], odd[:, kept:]], axis=1)
    counts = jnp.concatenate([received[j, 0:cells, 0:features] for j in orders[0]], axis=0)
    products = jnp.dot(high, counts, preferred_element_type=jnp.float32)
    total = [None] * (2 * peak_blocks)
    for position, j in enumerate(orders[1]):
        for b in range(gene_blocks):
            at = (position * gene_blocks + b) * BLOCK
            block = genes[:, at : at + BLOCK].astype(jnp.float32)
            row = (side * half + j) * gene_blocks + b
            for u in range(2 * peak_blocks):
                column = (place + u // peak_blocks * half) * peak_blocks + u % peak_blocks
                term = table[row, column] * block
                total[u] = term if total[u] is None else total[u] + term
    gene_links = to_gene[...]
    nothing = jnp.zeros_like(gene_links)
    links = jnp.concatenate(
        [jnp.where(side == 0, gene_links, nothing), jnp.where(side == 0, nothing, gene_links), *total], axis=1
    )
    finish_sums(products + link_scale * links, gram_of(high, rest), sums, coded, beside)


def update_kernel(last, widths, orders, spot, table, sums, other, beside, beside_other, factors, received, *outs):
    half = received.shape[0]
    rank, features = sums.shape
    cells = received.shape[1] - rank // 4
    gene_width, peak_width = widths
    gene_blocks, peak_blocks = gene_width // BLOCK, peak_width // BLOCK
    side, place, core = spot[0], spot[1], spot[2]
    first = core == 0
    gram = beside[:, 0:rank] + beside_other[:, 0:rank]
    old = factors[...]
    below = exact(gram, old) + EPSILON
    groups = features // BLOCK
    whole = []
    for b in range(groups):
        code = other[:, b * BLOCK : (b + 1) * BLOCK].astype(jnp.int32).astype(jnp.float32) + (CODES + 1) / 2
        least = beside_other[:, rank + b : rank + b + 1]
        step = beside_other[:, rank + groups + b : rank + groups + b + 1]
        whole.append(sums[:, b * BLOCK : (b + 1) * BLOCK] + (least + code * step))
    whole = jnp.concatenate(whole, axis=1)
    new = old * whole / below
    low = new.astype(jnp.bfloat16)
    cell_sums = jnp.concatenate([across(low, received[j, 0:cells, 0:features]) for j in orders[0]], axis=1)
    gram_features = across(low, low)
    kept, sent, *outs = outs
    split = half // 2 * cells
    left, right = cell_sums[:, :split], cell_sums[:, split:]
    for ref, value in ((kept, jnp.where(first, left, right)), (sent, jnp.where(first, right, left))):
        ref[:, :split] = value
        ref[:, split : split + rank] = gram_features
        ref[:, split + rank :] = jnp.zeros((rank, ref.shape[1] - split - rank), jnp.float32)

    def own(at, width):
        return jnp.where(side == 0, new[:, at : at + width], new[:, at + width : at + 2 * width])

    if last:
        gene_out, peak_out = outs
        gene_out[...] = own(0, gene_width)
        peak_out[...] = own(2 * gene_width, peak_width)
        return
    factors_out, links_kept, links_sent, gene_low = outs
    factors_out[...] = new
    gene_low[...] = own(0, gene_width).astype(jnp.bfloat16)
    peaks = low[:, 2 * gene_width :].astype(jnp.float32)
    peaks = [peaks[:, u * BLOCK : (u + 1) * BLOCK] for u in range(2 * peak_blocks)]
    for position in range(half // 2):
        pair = []
        for j in (orders[1][position], orders[1][position + half // 2]):
            parts = []
            for b in range(gene_blocks):
                row = (side * half + j) * gene_blocks + b
                part = None
                for u, block in enumerate(peaks):
                    column = (place + u // peak_blocks * half) * peak_blocks + u % peak_blocks
                    term = table[row, column] * block
                    part = term if part is None else part + term
                parts.append(part)
            pair.append(jnp.concatenate(parts, axis=1))
        at = position * gene_width
        links_kept[:, at : at + gene_width] = jnp.where(first, *pair)
        links_sent[:, at : at + gene_width] = jnp.where(first, pair[1], pair[0])


def cells_kernel(order, spot, totals, received_cells, pair, own):
    rank = totals.shape[0]
    cells = own.shape[1]
    kept = cells * len(order) // 2
    place, core = spot[1], spot[2]
    first = core == 0

    def state(j):
        terms = received_cells[j].astype(jnp.float32)
        return terms[:, :rank] + terms[:, rank:]

    old = jnp.concatenate(
        [
            jnp.where(first, state(order[s]), state(order[s + len(order) // 2]))
            for s in range(len(order) // 2)
        ],
        axis=1,
    )
    new = old * totals[:, :kept] / (exact(totals[:, kept : kept + rank], old) + EPSILON)
    pair[...] = jnp.concatenate(halved(new), axis=1)
    mine = new[:, :cells]
    for s in range(1, len(order) // 2):
        mine = jnp.where(place // 2 == order[s] // 2, new[:, s * cells : (s + 1) * cells], mine)
    own[...] = mine


def shards_blocks(
    rna_counts,
    atac_counts,
    cell_factor,
    gene_factor,
    peak_factor,
    link_gene,
    link_peak,
    link_weight,
    link_count,
):
    count = lax.axis_size(AXIS)
    half = count // 2
    me = lax.axis_index(AXIS)
    side, place, core = me // half, me % half, me % 2
    spot = jnp.stack([side, place, core]).astype(jnp.int32)
    rank, cells = cell_factor.shape
    gene_width, peak_width = gene_factor.shape[1], peak_factor.shape[1]
    widths = (gene_width, peak_width)
    width = gene_width + peak_width
    features = 2 * width
    link_scale = cells * count / 4.0
    table_shape = (rna_counts.shape[1] // BLOCK, atac_counts.shape[1] // BLOCK)
    chip_bits = bits_below(half)[1:]
    cell_bits, link_bits, gene_bits = (turned(chip_bits, i % len(chip_bits)) for i in range(3))
    cell_order = layout([1] + cell_bits)
    link_order = layout([1] + link_bits)
    gene_order = layout([1] + gene_bits[::-1])

    slots = pl.pallas_call(
        slots_kernel,
        in_specs=[SMEM] * 5,
        out_specs=VMEM,
        out_shape=struct(rank // 8, 2 * rank),
        compiler_params=PARAMS,
    )(spot, link_gene, link_peak, link_weight, link_count)
    slots_other = flip(slots, half)
    state = jnp.concatenate([gene_factor, peak_factor], axis=1)
    state_other = flip(state, half)
    sent = parcels(
        pltpu.with_memory_space_constraint(rna_counts, pltpu.HBM),
        pltpu.with_memory_space_constraint(atac_counts, pltpu.HBM),
        cell_factor,
        gene_factor,
        peak_factor,
        half,
    )
    sent = put_slots(slots, slots_other, sent)
    halves = [list(range(half)), list(range(half, count))]
    received = lax.all_to_all(sent, AXIS, 0, 0, axis_index_groups=halves, tiled=True)
    received, state_other = lax.optimization_barrier((received, state_other))
    low, high = in_order(half, state, state_other)
    factors = jnp.concatenate(
        [low[:, :gene_width], high[:, :gene_width], low[:, gene_width:], high[:, gene_width:]], axis=1
    )

    sums_shapes = (struct(rank, features), struct(rank, features, dtype=jnp.int16), struct(rank, 2 * rank))
    rows_other = flip(received[:, cells:, :features], 1)
    sums, gram = pl.pallas_call(
        first_sums_kernel,
        in_specs=[VMEM],
        out_specs=[VMEM] * 2,
        out_shape=(struct(rank, features), struct(rank, rank)),
        compiler_params=PARAMS,
    )(received)
    rows = rank // 4
    sums, coded, beside, link_table = pl.pallas_call(
        functools.partial(first_links_kernel, link_scale, widths),
        grid=(1,),
        in_specs=[
            SMEM,
            pl.BlockSpec((half, rows, features + 2 * rank), lambda i: (0, cells // rows, 0)),
            VMEM,
            VMEM,
            VMEM,
        ],
        out_specs=[VMEM] * 4,
        out_shape=(*sums_shapes, struct(*table_shape)),
        scratch_shapes=[pltpu.SemaphoreType.DMA, pltpu.SMEM(table_shape, jnp.float32)],
        compiler_params=PARAMS,
    )(spot, received, rows_other, sums, gram)

    split = half // 2 * cells
    for sweep_index in range(ROUNDS):
        last = sweep_index == ROUNDS - 1
        beside_other = flip(beside, half)
        other = flip(coded, half)
        lanes = -(-(split + rank) // BLOCK) * BLOCK
        outs = [struct(rank, lanes)] * 2
        if last:
            outs += [struct(rank, gene_width), struct(rank, peak_width)]
        else:
            outs += [struct(rank, features)] + [struct(rank, half // 2 * gene_width)] * 2
            outs += [struct(rank, gene_width, dtype=jnp.bfloat16)]
        kept, sent, *outs = pl.pallas_call(
            functools.partial(update_kernel, last, widths, (cell_order, link_order)),
            in_specs=[SMEM] * 2 + [VMEM] * 6,
            out_specs=[VMEM] * len(outs),
            out_shape=outs,
            compiler_params=PARAMS,
        )(spot, link_table, sums, other, beside, beside_other, factors, received)
        if last:
            gene_out, peak_out = outs
            totals = kept + flip(sent, 1)
            cell_sums, gram_features = totals[:, :split], totals[:, split : split + rank]
            for bit in cell_bits:
                left, right = jnp.split(cell_sums, 2, axis=1)
                clear = (me & bit) == 0
                got = flip(jnp.concatenate([jnp.where(clear, right, left), gram_features], axis=1), bit)
                cell_sums = jnp.where(clear, left, right) + got[:, : left.shape[1]]
                gram_features = gram_features + got[:, left.shape[1] :]
            cell_out = own_cells * cell_sums / (exact(gram_features, own_cells) + EPSILON)
            return cell_out, gene_out, peak_out
        factors, links_kept, links_sent, genes = outs
        totals = kept + flip(sent, 1)
        to_gene = links_kept + flip(links_sent, 1)
        for cell_bit, link_bit, gene_bit in zip(cell_bits, link_bits, gene_bits):
            left, right = jnp.split(to_gene, 2, axis=1)
            clear = (me & link_bit) == 0
            leaving, staying = jnp.where(clear, right, left), jnp.where(clear, left, right)
            totals, leaving, genes = lax.optimization_barrier((totals, leaving, genes))
            got = flip(totals, cell_bit), flip(leaving, link_bit), flip(genes, gene_bit)
            got = lax.optimization_barrier(got)
            totals = totals + got[0]
            to_gene = staying + got[1]
            genes = jnp.concatenate(in_order(gene_bit, genes, got[2]), axis=1)
        pair, own_cells = pl.pallas_call(
            functools.partial(cells_kernel, cell_order),
            grid=(1,),
            in_specs=[
                SMEM,
                VMEM,
                pl.BlockSpec((half, cells, 2 * rank), lambda i: (0, 0, features // (2 * rank))),
            ],
            out_specs=[VMEM] * 2,
            out_shape=(struct(rank, 2 * split, dtype=jnp.bfloat16), struct(rank, cells)),
            compiler_params=PARAMS,
        )(spot, totals, received)
        genes = jnp.concatenate(in_order(1, genes, flip(genes, 1)), axis=1)
        sums, coded, beside = pl.pallas_call(
            functools.partial(next_sums_kernel, link_scale, widths, (cell_order, gene_order)),
            in_specs=[SMEM] * 2 + [VMEM] * 5,
            out_specs=[VMEM] * 3,
            out_shape=sums_shapes,
            compiler_params=PARAMS,
        )(spot, link_table, pair, flip(pair, 1), received, to_gene, genes)


def shards(rna_counts, atac_counts, cell_factor, gene_factor, peak_factor, link_gene, *links):
    half = lax.axis_size(AXIS) // 2
    rank, cells = cell_factor.shape
    gene_width, peak_width = gene_factor.shape[1], peak_factor.shape[1]
    features = 2 * (gene_width + peak_width)
    in_blocks = (
        half % 8 == 0
        and rank == cells
        and 2 * rank == BLOCK
        and gene_width % BLOCK == 0
        and peak_width % BLOCK == 0
        and 2 * (features // BLOCK) <= rank
        and half * link_gene.shape[0] <= 2 * rank
        and rank % 64 == 0
        and max(rna_counts.shape[1], atac_counts.shape[1]) // BLOCK <= 256
    )
    run = shards_blocks if in_blocks else shards_any
    return run(rna_counts, atac_counts, cell_factor, gene_factor, peak_factor, link_gene, *links)


def solution(mesh):
    columns = P(None, ("groups", "cells"))
    slots = P(("groups", "cells"))
    in_specs = (P(("groups", "cells"), None),) * 2 + (columns,) * 3 + (slots,) * 4
    return jax.shard_map(
        shards, mesh=mesh, in_specs=in_specs, out_specs=(columns,) * 3, check_vma=False
    )
```

```python
import functools

import jax
import jax.numpy as jnp
from jax import lax
from jax.experimental import pallas as pl
from jax.experimental.pallas import tpu as pltpu
from jax.sharding import PartitionSpec as P

BLOCK = 128
ROUNDS = 2
EPSILON = 1e-06
CODES = 65535.0
AXIS = "cells"
PARAMS = pltpu.CompilerParams(vmem_limit_bytes=14 * 1024 * 1024)
SMEM = pl.BlockSpec(memory_space=pltpu.SMEM)
VMEM = pl.BlockSpec(memory_space=pltpu.VMEM)


def flip(value, bit):
    count = lax.axis_size(AXIS)
    return lax.ppermute(value, AXIS, [(i, i ^ bit) for i in range(count)])


def in_order(bit, mine, other):
    mine_first = (lax.axis_index(AXIS) & bit) == 0
    return jnp.where(mine_first, mine, other), jnp.where(mine_first, other, mine)


def bits_below(size):
    return [1 << b for b in range(size.bit_length() - 1)]


def own_table(link_gene, link_peak, link_weight, link_count, gene_blocks, peak_blocks):
    slot_ids = jnp.arange(link_gene.shape[0], dtype=jnp.int32)
    live_weight = jnp.where(slot_ids < link_count[0], link_weight, 0).astype(jnp.float32)
    gene_hot = (link_gene[:, None] == jnp.arange(gene_blocks, dtype=jnp.int32)[None, :]).astype(
        jnp.float32
    )
    peak_hot = (link_peak[:, None] == jnp.arange(peak_blocks, dtype=jnp.int32)[None, :]).astype(
        jnp.float32
    )
    return jnp.dot((gene_hot * live_weight[:, None]).T, peak_hot, precision=lax.Precision.HIGHEST)


def split_low(value):
    high = lax.reduce_precision(value, exponent_bits=8, mantissa_bits=7)
    return high.astype(jnp.bfloat16), (value - high).astype(jnp.bfloat16)


def gather_half(value, half):
    for bit in bits_below(half):
        value = jnp.concatenate(in_order(bit, value, flip(value, bit)), axis=1)
    return value


def scatter_half(value, half):
    for bit in reversed(bits_below(half)):
        low, high = jnp.split(value, 2, axis=1)
        clear = (lax.axis_index(AXIS) & bit) == 0
        value = jnp.where(clear, low, high) + flip(jnp.where(clear, high, low), bit)
    return value


def weigh(weights, source):
    rank = source.shape[0]
    blocks = source.astype(jnp.float32).reshape(rank, weights.shape[1], BLOCK)
    result = jnp.einsum("ksc,ts->ktc", blocks, weights, precision=lax.Precision.HIGHEST)
    return result.reshape(rank, weights.shape[0] * BLOCK)


def coupling(link_table, factors, widths):
    gene_width, peak_width = widths
    half = lax.axis_size(AXIS) // 2
    me = lax.axis_index(AXIS)
    side, place = me // half, me % half
    low = factors.astype(jnp.bfloat16)
    genes, peaks = low[:, : 2 * gene_width], low[:, 2 * gene_width :]
    own_gene = jnp.where(side == 0, genes[:, :gene_width], genes[:, gene_width:])
    side_blocks = half * gene_width // BLOCK
    peak_blocks = peak_width // BLOCK
    side_rows = lax.dynamic_slice_in_dim(link_table, side * side_blocks, side_blocks, 0)
    weights = jnp.concatenate(
        [
            lax.dynamic_slice_in_dim(side_rows, (place + s * half) * peak_blocks, peak_blocks, 1)
            for s in range(2)
        ],
        axis=1,
    )
    to_gene = scatter_half(weigh(weights, peaks), half)
    to_peak = weigh(weights.T, gather_half(own_gene, half))
    nothing = jnp.zeros_like(to_gene)
    return jnp.concatenate([*(jnp.where(side == s, to_gene, nothing) for s in range(2)), to_peak], axis=1)


def shards_any(
    rna_counts,
    atac_counts,
    cell_factor,
    gene_factor,
    peak_factor,
    link_gene,
    link_peak,
    link_weight,
    link_count,
):
    count = lax.axis_size(AXIS)
    half = count // 2
    me = lax.axis_index(AXIS)
    side = me // half
    rank, cells = cell_factor.shape
    gene_width, peak_width = gene_factor.shape[1], peak_factor.shape[1]
    features = 2 * (gene_width + peak_width)
    link_scale = cells * count / 4.0

    link_table = own_table(
        link_gene,
        link_peak,
        link_weight,
        link_count,
        rna_counts.shape[1] // BLOCK,
        atac_counts.shape[1] // BLOCK,
    )
    for bit in bits_below(count):
        link_table = link_table + flip(link_table, bit)

    def by_place(counts, width):
        return counts.reshape(cells, 2, half, width).transpose(2, 0, 1, 3).reshape(half, cells, 2 * width)

    cell_pair = jnp.concatenate([part.T for part in split_low(cell_factor)], axis=1)
    parcels = jnp.concatenate(
        [
            by_place(rna_counts, gene_width),
            by_place(atac_counts, peak_width),
            jnp.broadcast_to(cell_pair[None], (half, cells, 2 * rank)),
        ],
        axis=2,
    )
    halves = [list(range(half)), list(range(half, count))]
    received = lax.all_to_all(parcels, AXIS, 0, 0, axis_index_groups=halves, tiled=True)
    received = received.reshape(half * cells, features + 2 * rank)
    counts, cell_pair = received[:, :features], received[:, features:]

    gene_pair = in_order(half, gene_factor, flip(gene_factor, half))
    peak_pair = in_order(half, peak_factor, flip(peak_factor, half))
    factors = jnp.concatenate([*gene_pair, *peak_pair], axis=1)
    cell_low, cell_rest = cell_pair[:, :rank].T, cell_pair[:, rank:].T
    cell_state = cell_factor

    for sweep_index in range(ROUNDS):
        links = link_scale * coupling(link_table, factors, (gene_width, peak_width))
        pair = jnp.concatenate([cell_low, cell_rest], axis=0)
        squares = lax.dot_general(
            pair, pair, (((1,), (1,)), ((), ())), preferred_element_type=jnp.float32
        )
        gram_cells = (
            squares[:rank, :rank] + squares[:rank, rank:] + squares[rank:, :rank] + squares[rank:, rank:]
        )
        sums = jnp.dot(cell_low, counts, preferred_element_type=jnp.float32) + links
        gram_cells = gram_cells + flip(gram_cells, half)
        sums = sums + flip(sums, half)
        factors = (
            factors
            * sums
            / (jnp.dot(gram_cells, factors, precision=lax.Precision.HIGHEST) + EPSILON)
        )
        low = factors.astype(jnp.bfloat16)
        gram_features = lax.dot_general(
            low, low, (((1,), (1,)), ((), ())), preferred_element_type=jnp.float32
        )
        cell_sums = lax.dot_general(
            low, counts, (((1,), (1,)), ((), ())), preferred_element_type=jnp.float32
        )
        last = sweep_index == ROUNDS - 1
        if last:
            for bit in reversed(bits_below(half)):
                left, right = jnp.split(cell_sums, 2, axis=1)
                clear = (me & bit) == 0
                sent = jnp.concatenate([jnp.where(clear, right, left), gram_features], axis=1)
                got = flip(sent, bit)
                kept = cell_sums.shape[1] // 2
                cell_sums = jnp.where(clear, left, right) + got[:, :kept]
                gram_features = gram_features + got[:, kept:]
        else:
            left, right = jnp.split(cell_sums, 2, axis=1)
            clear = (me & 1) == 0
            sent = jnp.concatenate([jnp.where(clear, right, left), gram_features], axis=1)
            kept = jnp.concatenate([jnp.where(clear, left, right), gram_features], axis=1)
            for bit in bits_below(half):
                kept = kept + flip(sent, bit)
                sent = kept
            width = cell_sums.shape[1] // 2
            cell_sums, gram_features = kept[:, :width], kept[:, width:]
            low_rest = [jnp.where(clear, *jnp.split(part, 2, axis=1)) for part in (cell_low, cell_rest)]
            cell_state = low_rest[0].astype(jnp.float32) + low_rest[1].astype(jnp.float32)
        cell_state = (
            cell_state
            * cell_sums
            / (jnp.dot(gram_features, cell_state, precision=lax.Precision.HIGHEST) + EPSILON)
        )
        if not last:
            pair = jnp.concatenate(split_low(cell_state), axis=0)
            pair = jnp.concatenate(in_order(1, pair, flip(pair, 1)), axis=1)
            cell_low, cell_rest = pair[:rank], pair[rank:]
            mine = lax.dynamic_slice_in_dim(pair, (me % half) * cells, cells, 1).astype(jnp.float32)
            cell_state = mine[:rank] + mine[rank:]

    def own(first, width):
        return jnp.where(side == 0, factors[:, first : first + width], factors[:, first + width : first + 2 * width])

    return cell_state, own(0, gene_width), own(2 * gene_width, peak_width)


def layout(bits):
    size = 1 << len(bits)
    return [
        sum(bit for i, bit in enumerate(bits) if position >> (len(bits) - 1 - i) & 1)
        for position in range(size)
    ]


def turned(bits, by):
    return bits[by:] + bits[:by]


def across(left, right):
    return lax.dot_general(left, right, (((1,), (1,)), ((), ())), preferred_element_type=jnp.float32)


def exact(left, right):
    return lax.dot_general(
        left,
        right,
        (((1,), (0,)), ((), ())),
        precision=lax.Precision.HIGHEST,
        preferred_element_type=jnp.float32,
    )


def halved(value):
    high = value.astype(jnp.bfloat16)
    return high, (value - high.astype(jnp.float32)).astype(jnp.bfloat16)


def struct(*shape, dtype=jnp.float32):
    return jax.ShapeDtypeStruct(shape, dtype)


def gram_of(high, rest):
    pair = jnp.concatenate([high, rest], axis=0)
    squares = across(pair, pair)
    rank = high.shape[0]
    return (squares[:rank, :rank] + squares[rank:, rank:]) + (squares[:rank, rank:] + squares[rank:, :rank])


def parcels_kernel(rna_0, rna_1, atac_0, atac_1, cell, gene, peak, out):
    rank = cell.shape[0]
    cells = rna_0.shape[0]
    gene_width, peak_width = gene.shape[1], peak.shape[1]
    width = gene_width + peak_width
    cell_pair = jnp.concatenate(halved(cell[...]), axis=1)
    gene_low = gene[...].astype(jnp.bfloat16)
    peak_low = peak[...].astype(jnp.bfloat16)
    part = rank // 4
    for j in range(out.shape[0]):
        at = 0
        for source, size in ((rna_0, gene_width), (rna_1, gene_width), (atac_0, peak_width), (atac_1, peak_width)):
            out[j, 0:cells, at : at + size] = source[:, j * size : (j + 1) * size]
            at += size
        out[j, 0:cells, at:] = cell_pair
        for s in range(2):
            row = (2 * (j % 2) + s) * part
            out[j, cells:, s * width : s * width + gene_width] = gene_low[row : row + part]
            out[j, cells:, s * width + gene_width : (s + 1) * width] = peak_low[row : row + part]


def encode(group):
    least = jnp.min(group, axis=1, keepdims=True)
    spread = jnp.max(group, axis=1, keepdims=True) - least
    per = jnp.where(spread > 0.0, CODES / spread, 0.0)
    code = jnp.minimum(jnp.floor((group - least) * per + 0.5), CODES) - (CODES + 1) / 2
    return code.astype(jnp.int32).astype(jnp.int16), least, spread / CODES


def decode(code, least, step):
    return least + (code.astype(jnp.int32).astype(jnp.float32) + (CODES + 1) / 2) * step


def ahead_kernel(spot, gene, peak, *refs):
    links, (codes, beside), copied, sems = refs[:4], refs[4:6], refs[6:10], refs[10]
    copies = [pltpu.make_async_copy(link, to, sems.at[i]) for i, (link, to) in enumerate(zip(links, copied))]
    for copy in copies:
        copy.start()
    rank, width = codes.shape
    gene_width = gene.shape[1]
    least, step = [], []
    for b in range(width // BLOCK):
        ref, at = (gene, b * BLOCK) if b * BLOCK < gene_width else (peak, b * BLOCK - gene_width)
        code, low, per = encode(ref[:, at : at + BLOCK])
        codes[:, b * BLOCK : (b + 1) * BLOCK] = code
        least.append(low)
        step.append(per)
    pad = jnp.zeros((rank, beside.shape[1] - 2 * len(least)), jnp.float32)
    beside[:rank] = jnp.concatenate([*least, *step, pad], axis=1)
    for copy in copies:
        copy.wait()
    link_gene, link_peak, link_weight, link_count = copied
    slots = link_gene.shape[0]
    shape = (beside.shape[0] - rank, beside.shape[1])
    lane = lax.broadcasted_iota(jnp.int32, shape, 1) - spot[1] * slots
    row = lax.broadcasted_iota(jnp.int32, shape, 0)
    value = jnp.zeros(shape, jnp.float32)
    for s in range(slots):
        weight = jnp.where(s < link_count[0], link_weight[s], 0)
        for r, entry in enumerate((link_gene[s], link_peak[s], weight)):
            value = jnp.where((lane == s) & (row == r), entry.astype(jnp.float32), value)
    beside[rank:] = value


def ahead(spot, gene_factor, peak_factor, links):
    rank = gene_factor.shape[0]
    width = gene_factor.shape[1] + peak_factor.shape[1]
    anywhere = pl.BlockSpec(memory_space=pl.ANY)
    return pl.pallas_call(
        ahead_kernel,
        grid=(1,),
        in_specs=[SMEM] + [pl.BlockSpec(f.shape, lambda i: (0, 0)) for f in (gene_factor, peak_factor)] + [anywhere] * 4,
        out_specs=[VMEM, VMEM],
        out_shape=(struct(rank, width, dtype=jnp.int16), struct(rank + rank // 8, 2 * rank)),
        scratch_shapes=[pltpu.SMEM(link.shape, jnp.int32) for link in links] + [pltpu.SemaphoreType.DMA((4,))],
        compiler_params=PARAMS,
    )(spot, in_hbm(gene_factor), in_hbm(peak_factor), *links)


def twins_kernel(spot, gene, peak, codes, beside, out):
    gene_width, peak_width = gene.shape[1], peak.shape[1]
    groups = (gene_width + peak_width) // BLOCK
    at = 0
    first = spot[0] == 0
    for ref, start in ((gene, 0), (peak, gene_width)):
        size = ref.shape[1]
        for b in range(size // BLOCK):
            g = start // BLOCK + b
            mine = ref[:, b * BLOCK : (b + 1) * BLOCK]
            code = codes[:, g * BLOCK : (g + 1) * BLOCK]
            other = decode(code, beside[: mine.shape[0], g : g + 1], beside[: mine.shape[0], groups + g : groups + g + 1])
            out[:, at + b * BLOCK : at + (b + 1) * BLOCK] = jnp.where(first, mine, other)
            out[:, at + size + b * BLOCK : at + size + (b + 1) * BLOCK] = jnp.where(first, other, mine)
        at += 2 * size


def in_hbm(value):
    return pltpu.with_memory_space_constraint(value, pltpu.HBM)


def put_slots_kernel(mine, other, parcels_in, out, block, sems):
    first = mine.shape[0] - block.shape[0] // 2
    block[...] = jnp.concatenate([mine[first:], other[first:]], axis=0).astype(jnp.bfloat16)
    half, rows, lanes = out.shape
    copies = [
        pltpu.make_async_copy(
            block, out.at[j, rows - block.shape[0] : rows, lanes - block.shape[1] : lanes], sems.at[j]
        )
        for j in range(half)
    ]
    for copy in copies:
        copy.start()
    for copy in copies:
        copy.wait()


def put_slots(mine, other, parcels_value):
    rank = mine.shape[1] // 2
    return pl.pallas_call(
        put_slots_kernel,
        in_specs=[VMEM] * 3,
        out_specs=VMEM,
        out_shape=struct(*parcels_value.shape, dtype=parcels_value.dtype),
        scratch_shapes=[
            pltpu.VMEM((rank // 4, 2 * rank), jnp.bfloat16),
            pltpu.SemaphoreType.DMA((parcels_value.shape[0],)),
        ],
        input_output_aliases={2: 0},
        compiler_params=PARAMS,
    )(mine, other, parcels_value)


def parcels(rna_counts, atac_counts, cell_factor, gene_factor, peak_factor, half):
    cells = rna_counts.shape[0]
    rank = cell_factor.shape[0]
    gene_width, peak_width = gene_factor.shape[1], peak_factor.shape[1]
    rows, lanes = cells + rank // 4, 2 * (gene_width + peak_width) + 2 * rank
    each = 4
    steps = half // each

    def columns(width, side):
        return pl.BlockSpec((cells, each * width), lambda i: (0, i + side * steps))

    def whole(array):
        return pl.BlockSpec(array.shape, lambda i: (0, 0))

    return pl.pallas_call(
        parcels_kernel,
        grid=(steps,),
        in_specs=[columns(gene_width, 0), columns(gene_width, 1), columns(peak_width, 0), columns(peak_width, 1)]
        + [whole(a) for a in (cell_factor, gene_factor, peak_factor)],
        out_specs=pl.BlockSpec((each, rows, lanes), lambda i: (i, 0, 0)),
        out_shape=struct(half, rows, lanes, dtype=jnp.bfloat16),
        compiler_params=PARAMS,
    )(*(in_hbm(a) for a in (rna_counts, rna_counts, atac_counts, atac_counts, cell_factor, gene_factor, peak_factor)))


def first_sums_kernel(received, sums, gram):
    half, cells, features = received.shape[0], received.shape[1] - sums.shape[0] // 4, sums.shape[1]
    rank = sums.shape[0]
    high = jnp.concatenate([received[j, 0:cells, features : features + rank] for j in range(half)], axis=1)
    rest = jnp.concatenate([received[j, 0:cells, features + rank :] for j in range(half)], axis=1)
    counts = jnp.concatenate([received[j, 0:cells, 0:features] for j in range(half)], axis=0)
    sums[...] = jnp.dot(high, counts, preferred_element_type=jnp.float32)
    gram[...] = gram_of(high, rest)


def finish_sums(sums_value, gram_value, sums, coded, beside):
    rank, features = sums_value.shape
    least, step = [], []
    for b in range(features // BLOCK):
        group = sums_value[:, b * BLOCK : (b + 1) * BLOCK]
        sums[:, b * BLOCK : (b + 1) * BLOCK] = group
        code, low, per = encode(group)
        coded[:, b * BLOCK : (b + 1) * BLOCK] = code
        least.append(low)
        step.append(per)
    pad = jnp.zeros((rank, beside.shape[1] - rank - 2 * len(least)), jnp.float32)
    beside[...] = jnp.concatenate([gram_value, *least, *step, pad], axis=1)


def first_links_kernel(
    link_scale, widths, spot, mine, other, sums_in, gram, sums, coded, beside, table, table_sem, table_smem
):
    half = mine.shape[0]
    rank, features = sums_in.shape
    gene_width, peak_width = widths
    gene_blocks, peak_blocks = gene_width // BLOCK, peak_width // BLOCK
    width = gene_width + peak_width
    slots = sum(mine[j, :, 2 * width :].astype(jnp.float32) for j in range(half))

    def hot(row, size, value):
        ids = lax.broadcasted_iota(jnp.int32, (size, slots.shape[1]), 0).astype(jnp.float32)
        return jnp.where(slots[row : row + 1] == ids, value, 0.0).astype(jnp.bfloat16)

    table[...] = sum(
        across(hot(row, table.shape[0], slots[row + 2 : row + 3]), hot(row + 1, table.shape[1], 1.0))
        for row in (0, slots.shape[0] // 2)
    )
    copy = pltpu.make_async_copy(table, table_smem, table_sem)
    copy.start()
    copy.wait()
    side, place, core = spot[0], spot[1], spot[2]
    total = [None] * (features // BLOCK)

    def add(target, weight, block):
        term = weight * block
        total[target] = term if total[target] is None else total[target] + term

    for j in range(half):
        blocks = []
        for b in range(width // BLOCK):
            pieces = [
                ref[j, :, s * width + b * BLOCK : s * width + (b + 1) * BLOCK] for ref in (mine, other) for s in range(2)
            ]
            blocks.append(jnp.concatenate(pieces, axis=0).astype(jnp.float32))
        for b in range(gene_blocks):
            row = (side * half + j) * gene_blocks + b
            for u in range(2 * peak_blocks):
                column = (place + u // peak_blocks * half) * peak_blocks + u % peak_blocks
                add(2 * gene_blocks + u, table_smem[row, column], blocks[b])
        for b in range(peak_blocks):
            column = (side * half + j) * peak_blocks + b
            for t in range(2 * gene_blocks):
                row = (place + t // gene_blocks * half) * gene_blocks + t % gene_blocks
                add(t, table_smem[row, column], blocks[gene_blocks + b])
    links = jnp.concatenate(total, axis=1)
    ahead, behind = links[: rank // 2], links[rank // 2 :]
    first = core == 0
    links = jnp.concatenate([jnp.where(first, ahead, behind), jnp.where(first, behind, ahead)], axis=0)
    finish_sums(sums_in[...] + link_scale * links, gram[...], sums, coded, beside)


def next_sums_kernel(
    link_scale, widths, orders, spot, table, mine, other, received, to_gene, genes, sums, coded, beside
):
    half = received.shape[0]
    rank, features = sums.shape
    cells = mine.shape[1] * 2 // (2 * half)
    gene_width, peak_width = widths
    gene_blocks, peak_blocks = gene_width // BLOCK, peak_width // BLOCK
    side, place, core = spot[0], spot[1], spot[2]
    first = core == 0
    left, right = mine[...], other[...]
    even, odd = jnp.where(first, left, right), jnp.where(first, right, left)
    kept = half // 2 * cells
    high = jnp.concatenate([even[:, :kept], odd[:, :kept]], axis=1)
    rest = jnp.concatenate([even[:, kept:], odd[:, kept:]], axis=1)
    counts = jnp.concatenate([received[j, 0:cells, 0:features] for j in orders[0]], axis=0)
    products = jnp.dot(high, counts, preferred_element_type=jnp.float32)
    total = [None] * (2 * peak_blocks)
    for position, j in enumerate(orders[1]):
        for b in range(gene_blocks):
            at = (position * gene_blocks + b) * BLOCK
            block = genes[:, at : at + BLOCK].astype(jnp.float32)
            row = (side * half + j) * gene_blocks + b
            for u in range(2 * peak_blocks):
                column = (place + u // peak_blocks * half) * peak_blocks + u % peak_blocks
                term = table[row, column] * block
                total[u] = term if total[u] is None else total[u] + term
    gene_links = to_gene[...]
    nothing = jnp.zeros_like(gene_links)
    links = jnp.concatenate(
        [jnp.where(side == 0, gene_links, nothing), jnp.where(side == 0, nothing, gene_links), *total], axis=1
    )
    finish_sums(products + link_scale * links, gram_of(high, rest), sums, coded, beside)


def update_kernel(last, widths, orders, spot, table, sums, other, beside, beside_other, factors, received, *outs):
    half = received.shape[0]
    rank, features = sums.shape
    cells = received.shape[1] - rank // 4
    gene_width, peak_width = widths
    gene_blocks, peak_blocks = gene_width // BLOCK, peak_width // BLOCK
    side, place, core = spot[0], spot[1], spot[2]
    first = core == 0
    gram = beside[:, 0:rank] + beside_other[:, 0:rank]
    old = factors[...]
    below = exact(gram, old) + EPSILON
    groups = features // BLOCK
    whole = []
    for b in range(groups):
        code = other[:, b * BLOCK : (b + 1) * BLOCK]
        least = beside_other[:, rank + b : rank + b + 1]
        step = beside_other[:, rank + groups + b : rank + groups + b + 1]
        whole.append(sums[:, b * BLOCK : (b + 1) * BLOCK] + decode(code, least, step))
    whole = jnp.concatenate(whole, axis=1)
    new = old * whole / below
    low = new.astype(jnp.bfloat16)
    cell_sums = jnp.concatenate([across(low, received[j, 0:cells, 0:features]) for j in orders[0]], axis=1)
    gram_features = across(low, low)
    kept, sent, *outs = outs
    split = half // 2 * cells
    left, right = cell_sums[:, :split], cell_sums[:, split:]
    for ref, value in ((kept, jnp.where(first, left, right)), (sent, jnp.where(first, right, left))):
        ref[:, :split] = value
        ref[:, split : split + rank] = gram_features
        ref[:, split + rank :] = jnp.zeros((rank, ref.shape[1] - split - rank), jnp.float32)

    def own(at, width):
        return jnp.where(side == 0, new[:, at : at + width], new[:, at + width : at + 2 * width])

    if last:
        gene_out, peak_out = outs
        gene_out[...] = own(0, gene_width)
        peak_out[...] = own(2 * gene_width, peak_width)
        return
    factors_out, links_kept, links_sent, gene_low = outs
    factors_out[...] = new
    gene_low[...] = own(0, gene_width).astype(jnp.bfloat16)
    peaks = low[:, 2 * gene_width :].astype(jnp.float32)
    peaks = [peaks[:, u * BLOCK : (u + 1) * BLOCK] for u in range(2 * peak_blocks)]
    for position in range(half // 2):
        pair = []
        for j in (orders[1][position], orders[1][position + half // 2]):
            parts = []
            for b in range(gene_blocks):
                row = (side * half + j) * gene_blocks + b
                part = None
                for u, block in enumerate(peaks):
                    column = (place + u // peak_blocks * half) * peak_blocks + u % peak_blocks
                    term = table[row, column] * block
                    part = term if part is None else part + term
                parts.append(part)
            pair.append(jnp.concatenate(parts, axis=1))
        at = position * gene_width
        links_kept[:, at : at + gene_width] = jnp.where(first, *pair)
        links_sent[:, at : at + gene_width] = jnp.where(first, pair[1], pair[0])


def cells_kernel(order, spot, totals, received_cells, pair, own):
    rank = totals.shape[0]
    cells = own.shape[1]
    kept = cells * len(order) // 2
    place, core = spot[1], spot[2]
    first = core == 0

    def state(j):
        terms = received_cells[j].astype(jnp.float32)
        return terms[:, :rank] + terms[:, rank:]

    old = jnp.concatenate(
        [
            jnp.where(first, state(order[s]), state(order[s + len(order) // 2]))
            for s in range(len(order) // 2)
        ],
        axis=1,
    )
    new = old * totals[:, :kept] / (exact(totals[:, kept : kept + rank], old) + EPSILON)
    pair[...] = jnp.concatenate(halved(new), axis=1)
    mine = new[:, :cells]
    for s in range(1, len(order) // 2):
        mine = jnp.where(place // 2 == order[s] // 2, new[:, s * cells : (s + 1) * cells], mine)
    own[...] = mine


def shards_blocks(
    rna_counts,
    atac_counts,
    cell_factor,
    gene_factor,
    peak_factor,
    link_gene,
    link_peak,
    link_weight,
    link_count,
):
    count = lax.axis_size(AXIS)
    half = count // 2
    me = lax.axis_index(AXIS)
    side, place, core = me // half, me % half, me % 2
    spot = jnp.stack([side, place, core]).astype(jnp.int32)
    rank, cells = cell_factor.shape
    gene_width, peak_width = gene_factor.shape[1], peak_factor.shape[1]
    widths = (gene_width, peak_width)
    width = gene_width + peak_width
    features = 2 * width
    link_scale = cells * count / 4.0
    table_shape = (rna_counts.shape[1] // BLOCK, atac_counts.shape[1] // BLOCK)
    chip_bits = bits_below(half)[1:]
    cell_bits, link_bits, gene_bits = (turned(chip_bits, i % len(chip_bits)) for i in range(3))
    cell_order = layout([1] + cell_bits)
    link_order = layout([1] + link_bits)
    gene_order = layout([1] + gene_bits[::-1])

    codes, aside = ahead(spot, gene_factor, peak_factor, (link_gene, link_peak, link_weight, link_count))
    aside_other = flip(aside, half)
    codes_other = flip(codes, half)
    sent = parcels(rna_counts, atac_counts, cell_factor, gene_factor, peak_factor, half)
    sent = put_slots(aside, aside_other, sent)
    sent, codes_other = lax.optimization_barrier((sent, codes_other))
    halves = [list(range(half)), list(range(half, count))]
    received = lax.all_to_all(sent, AXIS, 0, 0, axis_index_groups=halves, tiled=True)
    factors = pl.pallas_call(
        twins_kernel,
        in_specs=[SMEM] + [VMEM] * 4,
        out_specs=VMEM,
        out_shape=struct(rank, features),
        compiler_params=PARAMS,
    )(spot, gene_factor, peak_factor, codes_other, aside_other)

    sums_shapes = (struct(rank, features), struct(rank, features, dtype=jnp.int16), struct(rank, 2 * rank))
    rows_other = flip(received[:, cells:, :features], 1)
    received = pltpu.with_memory_space_constraint(received, pltpu.VMEM)
    sums, gram = pl.pallas_call(
        first_sums_kernel,
        in_specs=[VMEM],
        out_specs=[VMEM] * 2,
        out_shape=(struct(rank, features), struct(rank, rank)),
        compiler_params=PARAMS,
    )(received)
    rows = rank // 4
    sums, coded, beside, link_table = pl.pallas_call(
        functools.partial(first_links_kernel, link_scale, widths),
        grid=(1,),
        in_specs=[
            SMEM,
            pl.BlockSpec((half, rows, features + 2 * rank), lambda i: (0, cells // rows, 0)),
            VMEM,
            VMEM,
            VMEM,
        ],
        out_specs=[VMEM] * 4,
        out_shape=(*sums_shapes, struct(*table_shape)),
        scratch_shapes=[pltpu.SemaphoreType.DMA, pltpu.SMEM(table_shape, jnp.float32)],
        compiler_params=PARAMS,
    )(spot, received, rows_other, sums, gram)

    split = half // 2 * cells
    for sweep_index in range(ROUNDS):
        last = sweep_index == ROUNDS - 1
        beside_other = flip(beside, half)
        other = flip(coded, half)
        lanes = -(-(split + rank) // BLOCK) * BLOCK
        outs = [struct(rank, lanes)] * 2
        if last:
            outs += [struct(rank, gene_width), struct(rank, peak_width)]
        else:
            outs += [struct(rank, features)] + [struct(rank, half // 2 * gene_width)] * 2
            outs += [struct(rank, gene_width, dtype=jnp.bfloat16)]
        kept, sent, *outs = pl.pallas_call(
            functools.partial(update_kernel, last, widths, (cell_order, link_order)),
            in_specs=[SMEM] * 2 + [VMEM] * 6,
            out_specs=[VMEM] * len(outs),
            out_shape=outs,
            compiler_params=PARAMS,
        )(spot, link_table, sums, other, beside, beside_other, factors, received)
        if last:
            gene_out, peak_out = outs
            totals = kept + flip(sent, 1)
            cell_sums, gram_features = totals[:, :split], totals[:, split : split + rank]
            first, second = cell_bits[:2]
            quarters = jnp.split(cell_sums, 4, axis=1)
            is_first, is_second = (me & first) != 0, (me & second) != 0

            def quarter(flip_first, flip_second):
                low, high = (
                    jnp.where(is_second ^ flip_second, quarters[2 * i + 1], quarters[2 * i]) for i in range(2)
                )
                return jnp.where(is_first ^ flip_first, high, low)

            leaving = [
                jnp.concatenate([quarter(*which), gram_features], axis=1)
                for which in ((True, False), (False, True), (True, True))
            ]
            got = [flip(value, bit) for value, bit in zip(leaving, (first, second, first | second))]
            size = quarters[0].shape[1]
            cell_sums = quarter(False, False) + (got[0][:, :size] + got[1][:, :size] + got[2][:, :size])
            gram_features = gram_features + (got[0][:, size:] + got[1][:, size:] + got[2][:, size:])
            for bit in cell_bits[2:]:
                left, right = jnp.split(cell_sums, 2, axis=1)
                clear = (me & bit) == 0
                got = flip(jnp.concatenate([jnp.where(clear, right, left), gram_features], axis=1), bit)
                cell_sums = jnp.where(clear, left, right) + got[:, : left.shape[1]]
                gram_features = gram_features + got[:, left.shape[1] :]
            cell_out = own_cells * cell_sums / (exact(gram_features, own_cells) + EPSILON)
            return cell_out, gene_out, peak_out
        factors, links_kept, links_sent, genes = outs
        totals = kept + flip(sent, 1)
        to_gene = links_kept + flip(links_sent, 1)
        for cell_bit, link_bit, gene_bit in zip(cell_bits, link_bits, gene_bits):
            left, right = jnp.split(to_gene, 2, axis=1)
            clear = (me & link_bit) == 0
            leaving, staying = jnp.where(clear, right, left), jnp.where(clear, left, right)
            totals, leaving, genes = lax.optimization_barrier((totals, leaving, genes))
            got = flip(totals, cell_bit), flip(leaving, link_bit), flip(genes, gene_bit)
            got = lax.optimization_barrier(got)
            totals = totals + got[0]
            to_gene = staying + got[1]
            genes = jnp.concatenate(in_order(gene_bit, genes, got[2]), axis=1)
        pair, own_cells = pl.pallas_call(
            functools.partial(cells_kernel, cell_order),
            grid=(1,),
            in_specs=[
                SMEM,
                VMEM,
                pl.BlockSpec((half, cells, 2 * rank), lambda i: (0, 0, features // (2 * rank))),
            ],
            out_specs=[VMEM] * 2,
            out_shape=(struct(rank, 2 * split, dtype=jnp.bfloat16), struct(rank, cells)),
            compiler_params=PARAMS,
        )(spot, totals, received)
        genes = jnp.concatenate(in_order(1, genes, flip(genes, 1)), axis=1)
        sums, coded, beside = pl.pallas_call(
            functools.partial(next_sums_kernel, link_scale, widths, (cell_order, gene_order)),
            in_specs=[SMEM] * 2 + [VMEM] * 5,
            out_specs=[VMEM] * 3,
            out_shape=sums_shapes,
            compiler_params=PARAMS,
        )(spot, link_table, pair, flip(pair, 1), received, to_gene, genes)


def shards(rna_counts, atac_counts, cell_factor, gene_factor, peak_factor, link_gene, *links):
    half = lax.axis_size(AXIS) // 2
    rank, cells = cell_factor.shape
    gene_width, peak_width = gene_factor.shape[1], peak_factor.shape[1]
    features = 2 * (gene_width + peak_width)
    in_blocks = (
        half % 8 == 0
        and rank == cells
        and 2 * rank == BLOCK
        and gene_width % BLOCK == 0
        and peak_width % BLOCK == 0
        and 2 * (features // BLOCK) <= rank
        and half * link_gene.shape[0] <= 2 * rank
        and rank % 64 == 0
        and max(rna_counts.shape[1], atac_counts.shape[1]) // BLOCK <= 256
    )
    run = shards_blocks if in_blocks else shards_any
    return run(rna_counts, atac_counts, cell_factor, gene_factor, peak_factor, link_gene, *links)


def solution(mesh):
    columns = P(None, ("groups", "cells"))
    slots = P(("groups", "cells"))
    in_specs = (P(("groups", "cells"), None),) * 2 + (columns,) * 3 + (slots,) * 4
    return jax.shard_map(
        shards, mesh=mesh, in_specs=in_specs, out_specs=(columns,) * 3, check_vma=False
    )
```

```python
import functools

import jax
import jax.numpy as jnp
from jax import lax
from jax.experimental import pallas as pl
from jax.experimental.pallas import tpu as pltpu
from jax.sharding import PartitionSpec as P

BLOCK = 128
ROUNDS = 2
EPSILON = 1e-06
CODES = 65535.0
AXIS = "cells"
PARAMS = pltpu.CompilerParams(vmem_limit_bytes=14 * 1024 * 1024)
SMEM = pl.BlockSpec(memory_space=pltpu.SMEM)
VMEM = pl.BlockSpec(memory_space=pltpu.VMEM)


def flip(value, bit):
    count = lax.axis_size(AXIS)
    return lax.ppermute(value, AXIS, [(i, i ^ bit) for i in range(count)])


def in_order(bit, mine, other):
    mine_first = (lax.axis_index(AXIS) & bit) == 0
    return jnp.where(mine_first, mine, other), jnp.where(mine_first, other, mine)


def bits_below(size):
    return [1 << b for b in range(size.bit_length() - 1)]


def own_table(link_gene, link_peak, link_weight, link_count, gene_blocks, peak_blocks):
    slot_ids = jnp.arange(link_gene.shape[0], dtype=jnp.int32)
    live_weight = jnp.where(slot_ids < link_count[0], link_weight, 0).astype(jnp.float32)
    gene_hot = (link_gene[:, None] == jnp.arange(gene_blocks, dtype=jnp.int32)[None, :]).astype(
        jnp.float32
    )
    peak_hot = (link_peak[:, None] == jnp.arange(peak_blocks, dtype=jnp.int32)[None, :]).astype(
        jnp.float32
    )
    return jnp.dot((gene_hot * live_weight[:, None]).T, peak_hot, precision=lax.Precision.HIGHEST)


def split_low(value):
    high = lax.reduce_precision(value, exponent_bits=8, mantissa_bits=7)
    return high.astype(jnp.bfloat16), (value - high).astype(jnp.bfloat16)


def gather_half(value, half):
    for bit in bits_below(half):
        value = jnp.concatenate(in_order(bit, value, flip(value, bit)), axis=1)
    return value


def scatter_half(value, half):
    for bit in reversed(bits_below(half)):
        low, high = jnp.split(value, 2, axis=1)
        clear = (lax.axis_index(AXIS) & bit) == 0
        value = jnp.where(clear, low, high) + flip(jnp.where(clear, high, low), bit)
    return value


def weigh(weights, source):
    rank = source.shape[0]
    blocks = source.astype(jnp.float32).reshape(rank, weights.shape[1], BLOCK)
    result = jnp.einsum("ksc,ts->ktc", blocks, weights, precision=lax.Precision.HIGHEST)
    return result.reshape(rank, weights.shape[0] * BLOCK)


def coupling(link_table, factors, widths):
    gene_width, peak_width = widths
    half = lax.axis_size(AXIS) // 2
    me = lax.axis_index(AXIS)
    side, place = me // half, me % half
    low = factors.astype(jnp.bfloat16)
    genes, peaks = low[:, : 2 * gene_width], low[:, 2 * gene_width :]
    own_gene = jnp.where(side == 0, genes[:, :gene_width], genes[:, gene_width:])
    side_blocks = half * gene_width // BLOCK
    peak_blocks = peak_width // BLOCK
    side_rows = lax.dynamic_slice_in_dim(link_table, side * side_blocks, side_blocks, 0)
    weights = jnp.concatenate(
        [
            lax.dynamic_slice_in_dim(side_rows, (place + s * half) * peak_blocks, peak_blocks, 1)
            for s in range(2)
        ],
        axis=1,
    )
    to_gene = scatter_half(weigh(weights, peaks), half)
    to_peak = weigh(weights.T, gather_half(own_gene, half))
    nothing = jnp.zeros_like(to_gene)
    return jnp.concatenate([*(jnp.where(side == s, to_gene, nothing) for s in range(2)), to_peak], axis=1)


def shards_any(
    rna_counts,
    atac_counts,
    cell_factor,
    gene_factor,
    peak_factor,
    link_gene,
    link_peak,
    link_weight,
    link_count,
):
    count = lax.axis_size(AXIS)
    half = count // 2
    me = lax.axis_index(AXIS)
    side = me // half
    rank, cells = cell_factor.shape
    gene_width, peak_width = gene_factor.shape[1], peak_factor.shape[1]
    features = 2 * (gene_width + peak_width)
    link_scale = cells * count / 4.0

    link_table = own_table(
        link_gene,
        link_peak,
        link_weight,
        link_count,
        rna_counts.shape[1] // BLOCK,
        atac_counts.shape[1] // BLOCK,
    )
    for bit in bits_below(count):
        link_table = link_table + flip(link_table, bit)

    def by_place(counts, width):
        return counts.reshape(cells, 2, half, width).transpose(2, 0, 1, 3).reshape(half, cells, 2 * width)

    cell_pair = jnp.concatenate([part.T for part in split_low(cell_factor)], axis=1)
    parcels = jnp.concatenate(
        [
            by_place(rna_counts, gene_width),
            by_place(atac_counts, peak_width),
            jnp.broadcast_to(cell_pair[None], (half, cells, 2 * rank)),
        ],
        axis=2,
    )
    halves = [list(range(half)), list(range(half, count))]
    received = lax.all_to_all(parcels, AXIS, 0, 0, axis_index_groups=halves, tiled=True)
    received = received.reshape(half * cells, features + 2 * rank)
    counts, cell_pair = received[:, :features], received[:, features:]

    gene_pair = in_order(half, gene_factor, flip(gene_factor, half))
    peak_pair = in_order(half, peak_factor, flip(peak_factor, half))
    factors = jnp.concatenate([*gene_pair, *peak_pair], axis=1)
    cell_low, cell_rest = cell_pair[:, :rank].T, cell_pair[:, rank:].T
    cell_state = cell_factor

    for sweep_index in range(ROUNDS):
        links = link_scale * coupling(link_table, factors, (gene_width, peak_width))
        pair = jnp.concatenate([cell_low, cell_rest], axis=0)
        squares = lax.dot_general(
            pair, pair, (((1,), (1,)), ((), ())), preferred_element_type=jnp.float32
        )
        gram_cells = (
            squares[:rank, :rank] + squares[:rank, rank:] + squares[rank:, :rank] + squares[rank:, rank:]
        )
        sums = jnp.dot(cell_low, counts, preferred_element_type=jnp.float32) + links
        gram_cells = gram_cells + flip(gram_cells, half)
        sums = sums + flip(sums, half)
        factors = (
            factors
            * sums
            / (jnp.dot(gram_cells, factors, precision=lax.Precision.HIGHEST) + EPSILON)
        )
        low = factors.astype(jnp.bfloat16)
        gram_features = lax.dot_general(
            low, low, (((1,), (1,)), ((), ())), preferred_element_type=jnp.float32
        )
        cell_sums = lax.dot_general(
            low, counts, (((1,), (1,)), ((), ())), preferred_element_type=jnp.float32
        )
        last = sweep_index == ROUNDS - 1
        if last:
            for bit in reversed(bits_below(half)):
                left, right = jnp.split(cell_sums, 2, axis=1)
                clear = (me & bit) == 0
                sent = jnp.concatenate([jnp.where(clear, right, left), gram_features], axis=1)
                got = flip(sent, bit)
                kept = cell_sums.shape[1] // 2
                cell_sums = jnp.where(clear, left, right) + got[:, :kept]
                gram_features = gram_features + got[:, kept:]
        else:
            left, right = jnp.split(cell_sums, 2, axis=1)
            clear = (me & 1) == 0
            sent = jnp.concatenate([jnp.where(clear, right, left), gram_features], axis=1)
            kept = jnp.concatenate([jnp.where(clear, left, right), gram_features], axis=1)
            for bit in bits_below(half):
                kept = kept + flip(sent, bit)
                sent = kept
            width = cell_sums.shape[1] // 2
            cell_sums, gram_features = kept[:, :width], kept[:, width:]
            low_rest = [jnp.where(clear, *jnp.split(part, 2, axis=1)) for part in (cell_low, cell_rest)]
            cell_state = low_rest[0].astype(jnp.float32) + low_rest[1].astype(jnp.float32)
        cell_state = (
            cell_state
            * cell_sums
            / (jnp.dot(gram_features, cell_state, precision=lax.Precision.HIGHEST) + EPSILON)
        )
        if not last:
            pair = jnp.concatenate(split_low(cell_state), axis=0)
            pair = jnp.concatenate(in_order(1, pair, flip(pair, 1)), axis=1)
            cell_low, cell_rest = pair[:rank], pair[rank:]
            mine = lax.dynamic_slice_in_dim(pair, (me % half) * cells, cells, 1).astype(jnp.float32)
            cell_state = mine[:rank] + mine[rank:]

    def own(first, width):
        return jnp.where(side == 0, factors[:, first : first + width], factors[:, first + width : first + 2 * width])

    return cell_state, own(0, gene_width), own(2 * gene_width, peak_width)


def layout(bits):
    size = 1 << len(bits)
    return [
        sum(bit for i, bit in enumerate(bits) if position >> (len(bits) - 1 - i) & 1)
        for position in range(size)
    ]


def turned(bits, by):
    return bits[by:] + bits[:by]


def across(left, right):
    return lax.dot_general(left, right, (((1,), (1,)), ((), ())), preferred_element_type=jnp.float32)


def exact(left, right):
    return lax.dot_general(
        left,
        right,
        (((1,), (0,)), ((), ())),
        precision=lax.Precision.HIGHEST,
        preferred_element_type=jnp.float32,
    )


def halved(value):
    high = value.astype(jnp.bfloat16)
    return high, (value - high.astype(jnp.float32)).astype(jnp.bfloat16)


def struct(*shape, dtype=jnp.float32):
    return jax.ShapeDtypeStruct(shape, dtype)


def gram_of(high, rest):
    pair = jnp.concatenate([high, rest], axis=0)
    squares = across(pair, pair)
    rank = high.shape[0]
    return (squares[:rank, :rank] + squares[rank:, rank:]) + (squares[:rank, rank:] + squares[rank:, :rank])


def parcels_kernel(spot, rna_0, rna_1, atac_0, atac_1, cell, gene, peak, *refs):
    links, out, copied, slots, sems = refs[:4], refs[4], refs[5:9], refs[9], refs[10]

    @pl.when(pl.program_id(0) == 0)
    def _():
        copies = [pltpu.make_async_copy(link, to, sems.at[i]) for i, (link, to) in enumerate(zip(links, copied))]
        for copy in copies:
            copy.start()
        for copy in copies:
            copy.wait()
        link_gene, link_peak, link_weight, link_count = copied
        count = link_gene.shape[0]
        lane = lax.broadcasted_iota(jnp.int32, slots.shape, 1) - spot[1] * count
        row = lax.broadcasted_iota(jnp.int32, slots.shape, 0)
        value = jnp.zeros(slots.shape, jnp.float32)
        for s in range(count):
            weight = jnp.where(s < link_count[0], link_weight[s], 0)
            for r, entry in enumerate((link_gene[s], link_peak[s], weight)):
                value = jnp.where((lane == s) & (row == r), entry.astype(jnp.float32), value)
        slots[...] = value.astype(jnp.bfloat16)

    rank = cell.shape[0]
    cells = rna_0.shape[0]
    gene_width, peak_width = gene.shape[1], peak.shape[1]
    width = gene_width + peak_width
    cell_pair = jnp.concatenate(halved(cell[...]), axis=1)
    gene_low = gene[...].astype(jnp.bfloat16)
    peak_low = peak[...].astype(jnp.bfloat16)
    part = rank // 4
    for j in range(out.shape[0]):
        at = 0
        for source, size in ((rna_0, gene_width), (rna_1, gene_width), (atac_0, peak_width), (atac_1, peak_width)):
            out[j, 0:cells, at : at + size] = source[:, j * size : (j + 1) * size]
            at += size
        out[j, 0:cells, at:] = cell_pair
        for s in range(2):
            row = (2 * (j % 2) + s) * part
            out[j, cells:, s * width : s * width + gene_width] = gene_low[row : row + part]
            out[j, cells:, s * width + gene_width : (s + 1) * width] = peak_low[row : row + part]
        out[j, cells:, 2 * width :] = slots[...]


def encode(group):
    least = jnp.min(group, axis=1, keepdims=True)
    spread = jnp.max(group, axis=1, keepdims=True) - least
    per = jnp.where(spread > 0.0, CODES / spread, 0.0)
    code = jnp.minimum(jnp.floor((group - least) * per + 0.5), CODES) - (CODES + 1) / 2
    return code.astype(jnp.int32).astype(jnp.int16), least, spread / CODES


def decode(code, least, step):
    return least + (code.astype(jnp.int32).astype(jnp.float32) + (CODES + 1) / 2) * step


def codes_kernel(gene, peak, codes, bounds):
    rank, width = codes.shape
    gene_width = gene.shape[1]
    least, step = [], []
    for b in range(width // BLOCK):
        ref, at = (gene, b * BLOCK) if b * BLOCK < gene_width else (peak, b * BLOCK - gene_width)
        code, low, per = encode(ref[:, at : at + BLOCK])
        codes[:, b * BLOCK : (b + 1) * BLOCK] = code
        least.append(low)
        step.append(per)
    pad = jnp.zeros((rank, bounds.shape[1] - 2 * len(least)), jnp.float32)
    bounds[...] = jnp.concatenate([*least, *step, pad], axis=1)


def table_kernel(received_slots, bounds, out):
    rank = bounds.shape[0]
    out[:rank] = bounds[...]
    slots = sum(received_slots[j].astype(jnp.float32) for j in range(received_slots.shape[0]))

    def hot(row, size, value):
        ids = lax.broadcasted_iota(jnp.int32, (size, slots.shape[1]), 0).astype(jnp.float32)
        return jnp.where(slots[row : row + 1] == ids, value, 0.0).astype(jnp.bfloat16)

    out[rank:] = across(hot(0, out.shape[0] - rank, slots[2:3]), hot(1, out.shape[1], 1.0))


def twins_kernel(spot, gene, peak, codes, beside, out):
    gene_width, peak_width = gene.shape[1], peak.shape[1]
    groups = (gene_width + peak_width) // BLOCK
    at = 0
    first = spot[0] == 0
    for ref, start in ((gene, 0), (peak, gene_width)):
        size = ref.shape[1]
        for b in range(size // BLOCK):
            g = start // BLOCK + b
            mine = ref[:, b * BLOCK : (b + 1) * BLOCK]
            code = codes[:, g * BLOCK : (g + 1) * BLOCK]
            other = decode(code, beside[: mine.shape[0], g : g + 1], beside[: mine.shape[0], groups + g : groups + g + 1])
            out[:, at + b * BLOCK : at + (b + 1) * BLOCK] = jnp.where(first, mine, other)
            out[:, at + size + b * BLOCK : at + size + (b + 1) * BLOCK] = jnp.where(first, other, mine)
        at += 2 * size


def in_hbm(value):
    return pltpu.with_memory_space_constraint(value, pltpu.HBM)


def parcels(spot, rna_counts, atac_counts, cell_factor, gene_factor, peak_factor, links, half):
    cells = rna_counts.shape[0]
    rank = cell_factor.shape[0]
    gene_width, peak_width = gene_factor.shape[1], peak_factor.shape[1]
    rows, lanes = cells + rank // 4, 2 * (gene_width + peak_width) + 2 * rank
    each = 4
    steps = half // each

    def columns(width, side):
        return pl.BlockSpec((cells, each * width), lambda i: (0, i + side * steps))

    def whole(array):
        return pl.BlockSpec(array.shape, lambda i: (0, 0))

    return pl.pallas_call(
        parcels_kernel,
        grid=(steps,),
        in_specs=[SMEM, columns(gene_width, 0), columns(gene_width, 1), columns(peak_width, 0), columns(peak_width, 1)]
        + [whole(a) for a in (cell_factor, gene_factor, peak_factor)]
        + [pl.BlockSpec(memory_space=pl.ANY)] * 4,
        out_specs=pl.BlockSpec((each, rows, lanes), lambda i: (i, 0, 0)),
        out_shape=struct(half, rows, lanes, dtype=jnp.bfloat16),
        scratch_shapes=[pltpu.SMEM(link.shape, jnp.int32) for link in links]
        + [pltpu.VMEM((rank // 4, 2 * rank), jnp.bfloat16), pltpu.SemaphoreType.DMA((4,))],
        compiler_params=PARAMS,
    )(
        spot,
        *(in_hbm(a) for a in (rna_counts, rna_counts, atac_counts, atac_counts, cell_factor, gene_factor, peak_factor)),
        *(in_hbm(a) for a in links[:-1]),
        links[-1],
    )


def first_sums_kernel(order, received, sums, gram, state):
    rank, features = sums.shape
    cells = received.shape[1] - rank // 4
    high = jnp.concatenate([received[j, 0:cells, features : features + rank] for j in order], axis=1)
    rest = jnp.concatenate([received[j, 0:cells, features + rank :] for j in order], axis=1)
    counts = jnp.concatenate([received[j, 0:cells, 0:features] for j in order], axis=0)
    sums[...] = jnp.dot(high, counts, preferred_element_type=jnp.float32)
    gram[...] = gram_of(high, rest)
    state[...] = high.astype(jnp.float32) + rest.astype(jnp.float32)


def finish_sums(sums_value, gram_value, sums, coded, beside):
    rank, features = sums_value.shape
    least, step = [], []
    for b in range(features // BLOCK):
        group = sums_value[:, b * BLOCK : (b + 1) * BLOCK]
        sums[:, b * BLOCK : (b + 1) * BLOCK] = group
        code, low, per = encode(group)
        coded[:, b * BLOCK : (b + 1) * BLOCK] = code
        least.append(low)
        step.append(per)
    pad = jnp.zeros((rank, beside.shape[1] - rank - 2 * len(least)), jnp.float32)
    beside[...] = jnp.concatenate([gram_value, *least, *step, pad], axis=1)


def first_links_kernel(
    link_scale, widths, spot, mine, other, aside, aside_other, sums_in, gram, sums, coded, beside, table, sem, table_smem
):
    half = mine.shape[0]
    rank, features = sums_in.shape
    gene_width, peak_width = widths
    gene_blocks, peak_blocks = gene_width // BLOCK, peak_width // BLOCK
    width = gene_width + peak_width
    table[...] = aside[rank:] + aside_other[rank:]
    copy = pltpu.make_async_copy(table, table_smem, sem)
    copy.start()
    copy.wait()
    side, place, core = spot[0], spot[1], spot[2]
    total = [None] * (features // BLOCK)

    def add(target, weight, block):
        term = weight * block
        total[target] = term if total[target] is None else total[target] + term

    for j in range(half):
        blocks = []
        for b in range(width // BLOCK):
            pieces = [
                ref[j, :, s * width + b * BLOCK : s * width + (b + 1) * BLOCK] for ref in (mine, other) for s in range(2)
            ]
            blocks.append(jnp.concatenate(pieces, axis=0).astype(jnp.float32))
        for b in range(gene_blocks):
            row = (side * half + j) * gene_blocks + b
            for u in range(2 * peak_blocks):
                column = (place + u // peak_blocks * half) * peak_blocks + u % peak_blocks
                add(2 * gene_blocks + u, table_smem[row, column], blocks[b])
        for b in range(peak_blocks):
            column = (side * half + j) * peak_blocks + b
            for t in range(2 * gene_blocks):
                row = (place + t // gene_blocks * half) * gene_blocks + t % gene_blocks
                add(t, table_smem[row, column], blocks[gene_blocks + b])
    links = jnp.concatenate(total, axis=1)
    ahead, behind = links[: rank // 2], links[rank // 2 :]
    first = core == 0
    links = jnp.concatenate([jnp.where(first, ahead, behind), jnp.where(first, behind, ahead)], axis=0)
    finish_sums(sums_in[...] + link_scale * links, gram[...], sums, coded, beside)


def gram_rows(gram, lanes):
    rank = gram.shape[0]
    rows = rank * rank // lanes
    return jnp.concatenate([gram[b * rows : (b + 1) * rows] for b in range(rank // rows)], axis=1)


def gram_back(rows_value, rank):
    return jnp.concatenate(
        [rows_value[:, b * rank : (b + 1) * rank] for b in range(rows_value.shape[1] // rank)], axis=0
    )


def next_sums_kernel(
    link_scale, widths, orders, spot, table, mine, other, state, received, to_gene, genes, sums, coded, beside, state_out, own
):
    half = received.shape[0]
    rank, features = sums.shape
    cells = own.shape[1]
    gene_width, peak_width = widths
    gene_blocks, peak_blocks = gene_width // BLOCK, peak_width // BLOCK
    side, place, core = spot[0], spot[1], spot[2]
    first = core == 0
    old = state[...]
    left, right = mine[:rank], other[:rank]
    products = jnp.concatenate([jnp.where(first, left, right), jnp.where(first, right, left)], axis=1)
    new = old * products / (exact(gram_back(mine[rank:], rank), old) + EPSILON)
    state_out[...] = new
    mine_now = new[:, :cells]
    for position in range(1, half):
        at = position * cells
        mine_now = jnp.where(place == orders[0][position], new[:, at : at + cells], mine_now)
    own[...] = mine_now
    high, rest = halved(new)
    counts = jnp.concatenate([received[j, 0:cells, 0:features] for j in orders[0]], axis=0)
    products = jnp.dot(high, counts, preferred_element_type=jnp.float32)
    total = [None] * (2 * peak_blocks)
    for position, j in enumerate(orders[1]):
        for b in range(gene_blocks):
            at = (position * gene_blocks + b) * BLOCK
            block = genes[:, at : at + BLOCK].astype(jnp.float32)
            row = (side * half + j) * gene_blocks + b
            for u in range(2 * peak_blocks):
                column = (place + u // peak_blocks * half) * peak_blocks + u % peak_blocks
                term = table[row, column] * block
                total[u] = term if total[u] is None else total[u] + term
    gene_links = to_gene[...]
    nothing = jnp.zeros_like(gene_links)
    links = jnp.concatenate(
        [jnp.where(side == 0, gene_links, nothing), jnp.where(side == 0, nothing, gene_links), *total], axis=1
    )
    finish_sums(products + link_scale * links, gram_of(high, rest), sums, coded, beside)


def update_kernel(last, widths, orders, spot, table, sums, other, beside, beside_other, factors, received, *outs):
    half = received.shape[0]
    rank, features = sums.shape
    cells = received.shape[1] - rank // 4
    gene_width, peak_width = widths
    gene_blocks, peak_blocks = gene_width // BLOCK, peak_width // BLOCK
    side, place, core = spot[0], spot[1], spot[2]
    first = core == 0
    gram = beside[:, 0:rank] + beside_other[:, 0:rank]
    old = factors[...]
    below = exact(gram, old) + EPSILON
    groups = features // BLOCK
    whole = []
    for b in range(groups):
        code = other[:, b * BLOCK : (b + 1) * BLOCK]
        least = beside_other[:, rank + b : rank + b + 1]
        step = beside_other[:, rank + groups + b : rank + groups + b + 1]
        whole.append(sums[:, b * BLOCK : (b + 1) * BLOCK] + decode(code, least, step))
    whole = jnp.concatenate(whole, axis=1)
    new = old * whole / below
    low = new.astype(jnp.bfloat16)
    cell_sums = jnp.concatenate([across(low, received[j, 0:cells, 0:features]) for j in orders[0]], axis=1)
    gram_features = across(low, low)
    kept, sent, *outs = outs
    split = half // 2 * cells
    left, right = cell_sums[:, :split], cell_sums[:, split:]
    for ref, value in ((kept, jnp.where(first, left, right)), (sent, jnp.where(first, right, left))):
        ref[:rank] = value
        ref[rank:] = gram_rows(gram_features, split)

    def own(at, width):
        return jnp.where(side == 0, new[:, at : at + width], new[:, at + width : at + 2 * width])

    if last:
        gene_out, peak_out = outs
        gene_out[...] = own(0, gene_width)
        peak_out[...] = own(2 * gene_width, peak_width)
        return
    factors_out, links_kept, links_sent, gene_low = outs
    factors_out[...] = new
    gene_low[...] = own(0, gene_width).astype(jnp.bfloat16)
    peaks = low[:, 2 * gene_width :].astype(jnp.float32)
    peaks = [peaks[:, u * BLOCK : (u + 1) * BLOCK] for u in range(2 * peak_blocks)]
    for position in range(half // 2):
        pair = []
        for j in (orders[1][position], orders[1][position + half // 2]):
            parts = []
            for b in range(gene_blocks):
                row = (side * half + j) * gene_blocks + b
                part = None
                for u, block in enumerate(peaks):
                    column = (place + u // peak_blocks * half) * peak_blocks + u % peak_blocks
                    term = table[row, column] * block
                    part = term if part is None else part + term
                parts.append(part)
            pair.append(jnp.concatenate(parts, axis=1))
        at = position * gene_width
        links_kept[:, at : at + gene_width] = jnp.where(first, *pair)
        links_sent[:, at : at + gene_width] = jnp.where(first, pair[1], pair[0])


def last_cells_kernel(spot, mine, other, old, out):
    rank, cells = out.shape
    totals = mine[:rank] + other[:rank]
    gram = mine[rank:] + other[rank:]
    lanes = totals.shape[1]
    rows = rank * rank // (4 * lanes)
    gram = jnp.concatenate(
        [gram[i * rows : (i + 1) * rows, b * rank : (b + 1) * rank] for i in range(4) for b in range(lanes // rank)],
        axis=0,
    )
    own = totals[:, :cells]
    for position in range(1, lanes // cells):
        own = jnp.where(spot[3] == position, totals[:, position * cells : (position + 1) * cells], own)
    out[...] = old[...] * own / (exact(gram, old[...]) + EPSILON)


def shards_blocks(
    rna_counts,
    atac_counts,
    cell_factor,
    gene_factor,
    peak_factor,
    link_gene,
    link_peak,
    link_weight,
    link_count,
):
    count = lax.axis_size(AXIS)
    half = count // 2
    me = lax.axis_index(AXIS)
    side, place, core = me // half, me % half, me % 2
    chip_bits = bits_below(half)[1:]
    cell_bits, link_bits, gene_bits = (turned(chip_bits, i % len(chip_bits)) for i in range(3))
    tail = sum(
        jnp.where((me & bit) != 0, 1 << i, 0) for i, bit in enumerate(reversed(cell_bits[2:]))
    )
    spot = jnp.stack([side, place, core, tail]).astype(jnp.int32)
    rank, cells = cell_factor.shape
    gene_width, peak_width = gene_factor.shape[1], peak_factor.shape[1]
    widths = (gene_width, peak_width)
    width = gene_width + peak_width
    features = 2 * width
    link_scale = cells * count / 4.0
    table_shape = (rna_counts.shape[1] // BLOCK, atac_counts.shape[1] // BLOCK)
    cell_order = layout([1] + cell_bits)
    link_order = layout([1] + link_bits)
    gene_order = layout([1] + gene_bits[::-1])

    links = (link_gene, link_peak, link_weight, link_count)
    sent = parcels(spot, rna_counts, atac_counts, cell_factor, gene_factor, peak_factor, links, half)
    halves = [list(range(half)), list(range(half, count))]
    received = lax.all_to_all(sent, AXIS, 0, 0, axis_index_groups=halves, tiled=True)
    rows_other = flip(received[:, cells:, :features], 1)
    received = pltpu.with_memory_space_constraint(received, pltpu.VMEM)
    codes, bounds = pl.pallas_call(
        codes_kernel,
        in_specs=[VMEM] * 2,
        out_specs=[VMEM] * 2,
        out_shape=(struct(rank, width, dtype=jnp.int16), struct(rank, 2 * rank)),
        compiler_params=PARAMS,
    )(gene_factor, peak_factor)
    rows = rank // 4
    aside = pl.pallas_call(
        table_kernel,
        grid=(1,),
        in_specs=[
            pl.BlockSpec((half, rows, 2 * rank), lambda i: (0, cells // rows, features // (2 * rank))),
            VMEM,
        ],
        out_specs=VMEM,
        out_shape=struct(rank + table_shape[0], table_shape[1]),
        compiler_params=PARAMS,
    )(received, bounds)
    aside_other = flip(aside, half)
    codes_other = flip(codes, half)
    sums_shapes = (struct(rank, features), struct(rank, features, dtype=jnp.int16), struct(rank, 2 * rank))
    sums, gram, state = pl.pallas_call(
        functools.partial(first_sums_kernel, cell_order),
        in_specs=[VMEM],
        out_specs=[VMEM] * 3,
        out_shape=(struct(rank, features), struct(rank, rank), struct(rank, half * cells)),
        compiler_params=PARAMS,
    )(received)
    sums, coded, beside, link_table = pl.pallas_call(
        functools.partial(first_links_kernel, link_scale, widths),
        grid=(1,),
        in_specs=[
            SMEM,
            pl.BlockSpec((half, rows, features + 2 * rank), lambda i: (0, cells // rows, 0)),
            VMEM,
            VMEM,
            VMEM,
            VMEM,
            VMEM,
        ],
        out_specs=[VMEM] * 4,
        out_shape=(*sums_shapes, struct(*table_shape)),
        scratch_shapes=[pltpu.SemaphoreType.DMA, pltpu.SMEM(table_shape, jnp.float32)],
        compiler_params=PARAMS,
    )(spot, received, rows_other, aside, aside_other, sums, gram)

    beside, codes_other = lax.optimization_barrier((beside, codes_other))
    factors = pl.pallas_call(
        twins_kernel,
        in_specs=[SMEM] + [VMEM] * 4,
        out_specs=VMEM,
        out_shape=struct(rank, features),
        compiler_params=PARAMS,
    )(spot, gene_factor, peak_factor, codes_other, aside_other)

    split = half // 2 * cells
    for sweep_index in range(ROUNDS):
        last = sweep_index == ROUNDS - 1
        beside_other = flip(beside, half)
        other = flip(coded, half)
        outs = [struct(rank + rank * rank // split, split)] * 2
        if last:
            outs += [struct(rank, gene_width), struct(rank, peak_width)]
        else:
            outs += [struct(rank, features)] + [struct(rank, half // 2 * gene_width)] * 2
            outs += [struct(rank, gene_width, dtype=jnp.bfloat16)]
        kept, sent, *outs = pl.pallas_call(
            functools.partial(update_kernel, last, widths, (cell_order, link_order)),
            in_specs=[SMEM] * 2 + [VMEM] * 6,
            out_specs=[VMEM] * len(outs),
            out_shape=outs,
            compiler_params=PARAMS,
        )(spot, link_table, sums, other, beside, beside_other, factors, received)
        if last:
            gene_out, peak_out = outs
            totals = kept + flip(sent, 1)
            first, second = cell_bits[:2]
            quarters = jnp.split(totals[:rank], 4, axis=1)
            gram_part = jnp.concatenate(jnp.split(totals[rank:], 4, axis=1), axis=0)
            is_first, is_second = (me & first) != 0, (me & second) != 0

            def quarter(flip_first, flip_second):
                low, high = (
                    jnp.where(is_second ^ flip_second, quarters[2 * i + 1], quarters[2 * i]) for i in range(2)
                )
                return jnp.concatenate([jnp.where(is_first ^ flip_first, high, low), gram_part], axis=0)

            got = [
                flip(quarter(*which), bit)
                for which, bit in (((True, False), first), ((False, True), second), ((True, True), first | second))
            ]
            totals = quarter(False, False) + (got[0] + got[1] + got[2])
            for bit in cell_bits[2:-1]:
                totals = totals + flip(totals, bit)
            cell_out = pl.pallas_call(
                last_cells_kernel,
                in_specs=[SMEM] + [VMEM] * 3,
                out_specs=VMEM,
                out_shape=struct(rank, cells),
                compiler_params=PARAMS,
            )(spot, totals, flip(totals, cell_bits[-1]), own_cells)
            return cell_out, gene_out, peak_out
        factors, links_kept, links_sent, genes = outs
        totals = kept + flip(sent, 1)
        to_gene = links_kept + flip(links_sent, 1)
        for cell_bit, link_bit, gene_bit in zip(cell_bits, link_bits, gene_bits):
            left, right = jnp.split(to_gene, 2, axis=1)
            clear = (me & link_bit) == 0
            leaving, staying = jnp.where(clear, right, left), jnp.where(clear, left, right)
            totals, leaving, genes = lax.optimization_barrier((totals, leaving, genes))
            got = flip(totals, cell_bit), flip(leaving, link_bit), flip(genes, gene_bit)
            got = lax.optimization_barrier(got)
            totals = totals + got[0]
            to_gene = staying + got[1]
            genes = jnp.concatenate(in_order(gene_bit, genes, got[2]), axis=1)
        genes = jnp.concatenate(in_order(1, genes, flip(genes, 1)), axis=1)
        sums, coded, beside, state, own_cells = pl.pallas_call(
            functools.partial(next_sums_kernel, link_scale, widths, (cell_order, gene_order)),
            in_specs=[SMEM] * 2 + [VMEM] * 6,
            out_specs=[VMEM] * 5,
            out_shape=(*sums_shapes, struct(rank, half * cells), struct(rank, cells)),
            compiler_params=PARAMS,
        )(spot, link_table, totals, flip(totals, 1), state, received, to_gene, genes)


def shards(rna_counts, atac_counts, cell_factor, gene_factor, peak_factor, link_gene, *links):
    half = lax.axis_size(AXIS) // 2
    rank, cells = cell_factor.shape
    gene_width, peak_width = gene_factor.shape[1], peak_factor.shape[1]
    features = 2 * (gene_width + peak_width)
    in_blocks = (
        half % 16 == 0
        and rank == cells
        and 2 * rank == BLOCK
        and gene_width % BLOCK == 0
        and peak_width % BLOCK == 0
        and 2 * (features // BLOCK) <= rank
        and half * link_gene.shape[0] <= 2 * rank
        and rank % 64 == 0
        and atac_counts.shape[1] // BLOCK == 2 * rank
        and max(rna_counts.shape[1], atac_counts.shape[1]) // BLOCK <= 256
    )
    run = shards_blocks if in_blocks else shards_any
    return run(rna_counts, atac_counts, cell_factor, gene_factor, peak_factor, link_gene, *links)


def solution(mesh):
    columns = P(None, ("groups", "cells"))
    slots = P(("groups", "cells"))
    in_specs = (P(("groups", "cells"), None),) * 2 + (columns,) * 3 + (slots,) * 4
    return jax.shard_map(
        shards, mesh=mesh, in_specs=in_specs, out_specs=(columns,) * 3, check_vma=False
    )
```

```python
import functools

import jax
import jax.numpy as jnp
from jax import lax
from jax.experimental import pallas as pl
from jax.experimental.pallas import tpu as pltpu
from jax.sharding import PartitionSpec as P

BLOCK = 128
ROUNDS = 2
EPSILON = 1e-06
CODES = 65535.0
AXIS = "cells"
PARAMS = pltpu.CompilerParams(vmem_limit_bytes=14 * 1024 * 1024)
SMEM = pl.BlockSpec(memory_space=pltpu.SMEM)
VMEM = pl.BlockSpec(memory_space=pltpu.VMEM)


def flip(value, bit):
    count = lax.axis_size(AXIS)
    return lax.ppermute(value, AXIS, [(i, i ^ bit) for i in range(count)])


def in_order(bit, mine, other):
    mine_first = (lax.axis_index(AXIS) & bit) == 0
    return jnp.where(mine_first, mine, other), jnp.where(mine_first, other, mine)


def bits_below(size):
    return [1 << b for b in range(size.bit_length() - 1)]


def own_table(link_gene, link_peak, link_weight, link_count, gene_blocks, peak_blocks):
    slot_ids = jnp.arange(link_gene.shape[0], dtype=jnp.int32)
    live_weight = jnp.where(slot_ids < link_count[0], link_weight, 0).astype(jnp.float32)
    gene_hot = (link_gene[:, None] == jnp.arange(gene_blocks, dtype=jnp.int32)[None, :]).astype(
        jnp.float32
    )
    peak_hot = (link_peak[:, None] == jnp.arange(peak_blocks, dtype=jnp.int32)[None, :]).astype(
        jnp.float32
    )
    return jnp.dot((gene_hot * live_weight[:, None]).T, peak_hot, precision=lax.Precision.HIGHEST)


def split_low(value):
    high = lax.reduce_precision(value, exponent_bits=8, mantissa_bits=7)
    return high.astype(jnp.bfloat16), (value - high).astype(jnp.bfloat16)


def gather_half(value, half):
    for bit in bits_below(half):
        value = jnp.concatenate(in_order(bit, value, flip(value, bit)), axis=1)
    return value


def scatter_half(value, half):
    for bit in reversed(bits_below(half)):
        low, high = jnp.split(value, 2, axis=1)
        clear = (lax.axis_index(AXIS) & bit) == 0
        value = jnp.where(clear, low, high) + flip(jnp.where(clear, high, low), bit)
    return value


def weigh(weights, source):
    rank = source.shape[0]
    blocks = source.astype(jnp.float32).reshape(rank, weights.shape[1], BLOCK)
    result = jnp.einsum("ksc,ts->ktc", blocks, weights, precision=lax.Precision.HIGHEST)
    return result.reshape(rank, weights.shape[0] * BLOCK)


def coupling(link_table, factors, widths):
    gene_width, peak_width = widths
    half = lax.axis_size(AXIS) // 2
    me = lax.axis_index(AXIS)
    side, place = me // half, me % half
    low = factors.astype(jnp.bfloat16)
    genes, peaks = low[:, : 2 * gene_width], low[:, 2 * gene_width :]
    own_gene = jnp.where(side == 0, genes[:, :gene_width], genes[:, gene_width:])
    side_blocks = half * gene_width // BLOCK
    peak_blocks = peak_width // BLOCK
    side_rows = lax.dynamic_slice_in_dim(link_table, side * side_blocks, side_blocks, 0)
    weights = jnp.concatenate(
        [
            lax.dynamic_slice_in_dim(side_rows, (place + s * half) * peak_blocks, peak_blocks, 1)
            for s in range(2)
        ],
        axis=1,
    )
    to_gene = scatter_half(weigh(weights, peaks), half)
    to_peak = weigh(weights.T, gather_half(own_gene, half))
    nothing = jnp.zeros_like(to_gene)
    return jnp.concatenate([*(jnp.where(side == s, to_gene, nothing) for s in range(2)), to_peak], axis=1)


def shards_any(
    rna_counts,
    atac_counts,
    cell_factor,
    gene_factor,
    peak_factor,
    link_gene,
    link_peak,
    link_weight,
    link_count,
):
    count = lax.axis_size(AXIS)
    half = count // 2
    me = lax.axis_index(AXIS)
    side = me // half
    rank, cells = cell_factor.shape
    gene_width, peak_width = gene_factor.shape[1], peak_factor.shape[1]
    features = 2 * (gene_width + peak_width)
    link_scale = cells * count / 4.0

    link_table = own_table(
        link_gene,
        link_peak,
        link_weight,
        link_count,
        rna_counts.shape[1] // BLOCK,
        atac_counts.shape[1] // BLOCK,
    )
    for bit in bits_below(count):
        link_table = link_table + flip(link_table, bit)

    def by_place(counts, width):
        return counts.reshape(cells, 2, half, width).transpose(2, 0, 1, 3).reshape(half, cells, 2 * width)

    cell_pair = jnp.concatenate([part.T for part in split_low(cell_factor)], axis=1)
    parcels = jnp.concatenate(
        [
            by_place(rna_counts, gene_width),
            by_place(atac_counts, peak_width),
            jnp.broadcast_to(cell_pair[None], (half, cells, 2 * rank)),
        ],
        axis=2,
    )
    halves = [list(range(half)), list(range(half, count))]
    received = lax.all_to_all(parcels, AXIS, 0, 0, axis_index_groups=halves, tiled=True)
    received = received.reshape(half * cells, features + 2 * rank)
    counts, cell_pair = received[:, :features], received[:, features:]

    gene_pair = in_order(half, gene_factor, flip(gene_factor, half))
    peak_pair = in_order(half, peak_factor, flip(peak_factor, half))
    factors = jnp.concatenate([*gene_pair, *peak_pair], axis=1)
    cell_low, cell_rest = cell_pair[:, :rank].T, cell_pair[:, rank:].T
    cell_state = cell_factor

    for sweep_index in range(ROUNDS):
        links = link_scale * coupling(link_table, factors, (gene_width, peak_width))
        pair = jnp.concatenate([cell_low, cell_rest], axis=0)
        squares = lax.dot_general(
            pair, pair, (((1,), (1,)), ((), ())), preferred_element_type=jnp.float32
        )
        gram_cells = (
            squares[:rank, :rank] + squares[:rank, rank:] + squares[rank:, :rank] + squares[rank:, rank:]
        )
        sums = jnp.dot(cell_low, counts, preferred_element_type=jnp.float32) + links
        gram_cells = gram_cells + flip(gram_cells, half)
        sums = sums + flip(sums, half)
        factors = (
            factors
            * sums
            / (jnp.dot(gram_cells, factors, precision=lax.Precision.HIGHEST) + EPSILON)
        )
        low = factors.astype(jnp.bfloat16)
        gram_features = lax.dot_general(
            low, low, (((1,), (1,)), ((), ())), preferred_element_type=jnp.float32
        )
        cell_sums = lax.dot_general(
            low, counts, (((1,), (1,)), ((), ())), preferred_element_type=jnp.float32
        )
        last = sweep_index == ROUNDS - 1
        if last:
            for bit in reversed(bits_below(half)):
                left, right = jnp.split(cell_sums, 2, axis=1)
                clear = (me & bit) == 0
                sent = jnp.concatenate([jnp.where(clear, right, left), gram_features], axis=1)
                got = flip(sent, bit)
                kept = cell_sums.shape[1] // 2
                cell_sums = jnp.where(clear, left, right) + got[:, :kept]
                gram_features = gram_features + got[:, kept:]
        else:
            left, right = jnp.split(cell_sums, 2, axis=1)
            clear = (me & 1) == 0
            sent = jnp.concatenate([jnp.where(clear, right, left), gram_features], axis=1)
            kept = jnp.concatenate([jnp.where(clear, left, right), gram_features], axis=1)
            for bit in bits_below(half):
                kept = kept + flip(sent, bit)
                sent = kept
            width = cell_sums.shape[1] // 2
            cell_sums, gram_features = kept[:, :width], kept[:, width:]
            low_rest = [jnp.where(clear, *jnp.split(part, 2, axis=1)) for part in (cell_low, cell_rest)]
            cell_state = low_rest[0].astype(jnp.float32) + low_rest[1].astype(jnp.float32)
        cell_state = (
            cell_state
            * cell_sums
            / (jnp.dot(gram_features, cell_state, precision=lax.Precision.HIGHEST) + EPSILON)
        )
        if not last:
            pair = jnp.concatenate(split_low(cell_state), axis=0)
            pair = jnp.concatenate(in_order(1, pair, flip(pair, 1)), axis=1)
            cell_low, cell_rest = pair[:rank], pair[rank:]
            mine = lax.dynamic_slice_in_dim(pair, (me % half) * cells, cells, 1).astype(jnp.float32)
            cell_state = mine[:rank] + mine[rank:]

    def own(first, width):
        return jnp.where(side == 0, factors[:, first : first + width], factors[:, first + width : first + 2 * width])

    return cell_state, own(0, gene_width), own(2 * gene_width, peak_width)


def layout(bits):
    size = 1 << len(bits)
    return [
        sum(bit for i, bit in enumerate(bits) if position >> (len(bits) - 1 - i) & 1)
        for position in range(size)
    ]


def turned(bits, by):
    return bits[by:] + bits[:by]


def across(left, right):
    return lax.dot_general(left, right, (((1,), (1,)), ((), ())), preferred_element_type=jnp.float32)


def exact(left, right):
    return lax.dot_general(
        left,
        right,
        (((1,), (0,)), ((), ())),
        precision=lax.Precision.HIGHEST,
        preferred_element_type=jnp.float32,
    )


def halved(value):
    high = value.astype(jnp.bfloat16)
    return high, (value - high.astype(jnp.float32)).astype(jnp.bfloat16)


def struct(*shape, dtype=jnp.float32):
    return jax.ShapeDtypeStruct(shape, dtype)


def gram_of(high, rest):
    pair = jnp.concatenate([high, rest], axis=0)
    squares = across(pair, pair)
    rank = high.shape[0]
    return (squares[:rank, :rank] + squares[rank:, rank:]) + (squares[:rank, rank:] + squares[rank:, :rank])


def parcels_kernel(spot, rna_0, rna_1, atac_0, atac_1, cell, gene, peak, *refs):
    links, out, copied, slots, sems = refs[:4], refs[4], refs[5:9], refs[9], refs[10]

    copies = [pltpu.make_async_copy(link, to, sems.at[i]) for i, (link, to) in enumerate(zip(links, copied))]

    @pl.when(pl.program_id(0) == 0)
    def _():
        for copy in copies:
            copy.start()

    rank = cell.shape[0]
    cells = rna_0.shape[0]
    gene_width, peak_width = gene.shape[1], peak.shape[1]
    width = gene_width + peak_width
    cell_pair = jnp.concatenate(halved(cell[...]), axis=1)
    gene_low = gene[...].astype(jnp.bfloat16)
    peak_low = peak[...].astype(jnp.bfloat16)
    part = rank // 4
    for j in range(out.shape[0]):
        at = 0
        for source, size in ((rna_0, gene_width), (rna_1, gene_width), (atac_0, peak_width), (atac_1, peak_width)):
            out[j, 0:cells, at : at + size] = source[:, j * size : (j + 1) * size]
            at += size
        out[j, 0:cells, at:] = cell_pair
        for s in range(2):
            row = (2 * (j % 2) + s) * part
            out[j, cells:, s * width : s * width + gene_width] = gene_low[row : row + part]
            out[j, cells:, s * width + gene_width : (s + 1) * width] = peak_low[row : row + part]

    @pl.when(pl.program_id(0) == 0)
    def _():
        for copy in copies:
            copy.wait()
        link_gene, link_peak, link_weight, link_count = copied
        count = link_gene.shape[0]
        lane = lax.broadcasted_iota(jnp.int32, slots.shape, 1) - spot[1] * count
        row = lax.broadcasted_iota(jnp.int32, slots.shape, 0)
        value = jnp.zeros(slots.shape, jnp.float32)
        for s in range(count):
            weight = jnp.where(s < link_count[0], link_weight[s], 0)
            for r, entry in enumerate((link_gene[s], link_peak[s], weight)):
                value = jnp.where((lane == s) & (row == r), entry.astype(jnp.float32), value)
        slots[...] = value.astype(jnp.bfloat16)

    for j in range(out.shape[0]):
        out[j, cells:, 2 * width :] = slots[...]


def encode(group):
    least = jnp.min(group, axis=1, keepdims=True)
    spread = jnp.max(group, axis=1, keepdims=True) - least
    per = jnp.where(spread > 0.0, CODES / spread, 0.0)
    code = jnp.minimum(jnp.floor((group - least) * per + 0.5), CODES) - (CODES + 1) / 2
    return code.astype(jnp.int32).astype(jnp.int16), least, spread / CODES


def decode(code, least, step):
    return least + (code.astype(jnp.int32).astype(jnp.float32) + (CODES + 1) / 2) * step


def codes_kernel(gene, peak, codes, bounds):
    rank, width = codes.shape
    gene_width = gene.shape[1]
    least, step = [], []
    for b in range(width // BLOCK):
        ref, at = (gene, b * BLOCK) if b * BLOCK < gene_width else (peak, b * BLOCK - gene_width)
        code, low, per = encode(ref[:, at : at + BLOCK])
        codes[:, b * BLOCK : (b + 1) * BLOCK] = code
        least.append(low)
        step.append(per)
    pad = jnp.zeros((rank, bounds.shape[1] - 2 * len(least)), jnp.float32)
    bounds[...] = jnp.concatenate([*least, *step, pad], axis=1)


def table_kernel(received_slots, bounds, out):
    rank = bounds.shape[0]
    out[:rank] = bounds[...]
    slots = sum(received_slots[j].astype(jnp.float32) for j in range(received_slots.shape[0]))

    def hot(row, size, value):
        ids = lax.broadcasted_iota(jnp.int32, (size, slots.shape[1]), 0).astype(jnp.float32)
        return jnp.where(slots[row : row + 1] == ids, value, 0.0).astype(jnp.bfloat16)

    out[rank:] = across(hot(0, out.shape[0] - rank, slots[2:3]), hot(1, out.shape[1], 1.0))


def twins_kernel(spot, gene, peak, codes, beside, out):
    gene_width, peak_width = gene.shape[1], peak.shape[1]
    groups = (gene_width + peak_width) // BLOCK
    at = 0
    first = spot[0] == 0
    for ref, start in ((gene, 0), (peak, gene_width)):
        size = ref.shape[1]
        for b in range(size // BLOCK):
            g = start // BLOCK + b
            mine = ref[:, b * BLOCK : (b + 1) * BLOCK]
            code = codes[:, g * BLOCK : (g + 1) * BLOCK]
            other = decode(code, beside[: mine.shape[0], g : g + 1], beside[: mine.shape[0], groups + g : groups + g + 1])
            out[:, at + b * BLOCK : at + (b + 1) * BLOCK] = jnp.where(first, mine, other)
            out[:, at + size + b * BLOCK : at + size + (b + 1) * BLOCK] = jnp.where(first, other, mine)
        at += 2 * size


def in_hbm(value):
    return pltpu.with_memory_space_constraint(value, pltpu.HBM)


def parcels(spot, rna_counts, atac_counts, cell_factor, gene_factor, peak_factor, links, half):
    cells = rna_counts.shape[0]
    rank = cell_factor.shape[0]
    gene_width, peak_width = gene_factor.shape[1], peak_factor.shape[1]
    rows, lanes = cells + rank // 4, 2 * (gene_width + peak_width) + 2 * rank
    each = 4
    steps = half // each

    def columns(width, side):
        return pl.BlockSpec((cells, each * width), lambda i: (0, i + side * steps))

    def whole(array):
        return pl.BlockSpec(array.shape, lambda i: (0, 0))

    return pl.pallas_call(
        parcels_kernel,
        grid=(steps,),
        in_specs=[SMEM, columns(gene_width, 0), columns(gene_width, 1), columns(peak_width, 0), columns(peak_width, 1)]
        + [whole(a) for a in (cell_factor, gene_factor, peak_factor)]
        + [pl.BlockSpec(memory_space=pl.ANY)] * 4,
        out_specs=pl.BlockSpec((each, rows, lanes), lambda i: (i, 0, 0)),
        out_shape=struct(half, rows, lanes, dtype=jnp.bfloat16),
        scratch_shapes=[pltpu.SMEM(link.shape, jnp.int32) for link in links]
        + [pltpu.VMEM((rank // 4, 2 * rank), jnp.bfloat16), pltpu.SemaphoreType.DMA((4,))],
        compiler_params=PARAMS,
    )(
        spot,
        *(in_hbm(a) for a in (rna_counts, rna_counts, atac_counts, atac_counts, cell_factor, gene_factor, peak_factor)),
        *(in_hbm(a) for a in links[:-1]),
        links[-1],
    )


def first_sums_kernel(order, received, sums, gram, state):
    rank, features = sums.shape
    cells = received.shape[1] - rank // 4
    high = jnp.concatenate([received[j, 0:cells, features : features + rank] for j in order], axis=1)
    rest = jnp.concatenate([received[j, 0:cells, features + rank :] for j in order], axis=1)
    counts = jnp.concatenate([received[j, 0:cells, 0:features] for j in order], axis=0)
    sums[...] = jnp.dot(high, counts, preferred_element_type=jnp.float32)
    gram[...] = gram_of(high, rest)
    state[...] = high.astype(jnp.float32) + rest.astype(jnp.float32)


def finish_sums(sums_value, gram_value, sums, coded, beside):
    rank, features = sums_value.shape
    least, step = [], []
    for b in range(features // BLOCK):
        group = sums_value[:, b * BLOCK : (b + 1) * BLOCK]
        sums[:, b * BLOCK : (b + 1) * BLOCK] = group
        code, low, per = encode(group)
        coded[:, b * BLOCK : (b + 1) * BLOCK] = code
        least.append(low)
        step.append(per)
    pad = jnp.zeros((rank, beside.shape[1] - rank - 2 * len(least)), jnp.float32)
    beside[...] = jnp.concatenate([gram_value, *least, *step, pad], axis=1)


def first_links_kernel(
    link_scale, widths, spot, mine, other, aside, aside_other, sums_in, gram, sums, coded, beside, table, sem, table_smem
):
    half = mine.shape[0]
    rank, features = sums_in.shape
    gene_width, peak_width = widths
    gene_blocks, peak_blocks = gene_width // BLOCK, peak_width // BLOCK
    width = gene_width + peak_width
    table[...] = aside[rank:] + aside_other[rank:]
    copy = pltpu.make_async_copy(table, table_smem, sem)
    copy.start()
    copy.wait()
    side, place, core = spot[0], spot[1], spot[2]
    total = [None] * (features // BLOCK)

    def add(target, weight, block):
        term = weight * block
        total[target] = term if total[target] is None else total[target] + term

    for j in range(half):
        blocks = []
        for b in range(width // BLOCK):
            pieces = [
                ref[j, :, s * width + b * BLOCK : s * width + (b + 1) * BLOCK] for ref in (mine, other) for s in range(2)
            ]
            blocks.append(jnp.concatenate(pieces, axis=0).astype(jnp.float32))
        for b in range(gene_blocks):
            row = (side * half + j) * gene_blocks + b
            for u in range(2 * peak_blocks):
                column = (place + u // peak_blocks * half) * peak_blocks + u % peak_blocks
                add(2 * gene_blocks + u, table_smem[row, column], blocks[b])
        for b in range(peak_blocks):
            column = (side * half + j) * peak_blocks + b
            for t in range(2 * gene_blocks):
                row = (place + t // gene_blocks * half) * gene_blocks + t % gene_blocks
                add(t, table_smem[row, column], blocks[gene_blocks + b])
    links = jnp.concatenate(total, axis=1)
    ahead, behind = links[: rank // 2], links[rank // 2 :]
    first = core == 0
    links = jnp.concatenate([jnp.where(first, ahead, behind), jnp.where(first, behind, ahead)], axis=0)
    finish_sums(sums_in[...] + link_scale * links, gram[...], sums, coded, beside)


def fetch(received, order, counts, sems):
    cells, features = counts.shape[0] // len(order), counts.shape[1]
    copies = [
        pltpu.make_async_copy(
            received.at[j, pl.ds(0, cells), pl.ds(0, features)], counts.at[pl.ds(i * cells, cells)], sems.at[i]
        )
        for i, j in enumerate(order)
    ]
    for copy in copies:
        copy.start()
    return copies


def gram_rows(gram, lanes):
    rank = gram.shape[0]
    rows = rank * rank // lanes
    return jnp.concatenate([gram[b * rows : (b + 1) * rows] for b in range(rank // rows)], axis=1)


def gram_back(rows_value, rank):
    return jnp.concatenate(
        [rows_value[:, b * rank : (b + 1) * rank] for b in range(rows_value.shape[1] // rank)], axis=0
    )


def next_sums_kernel(
    link_scale, widths, orders, spot, table, mine, other, state, received, to_gene, genes, *refs
):
    sums, coded, beside, state_out, own, counts, sems = refs
    copies = fetch(received, orders[0], counts, sems)
    half = received.shape[0]
    rank, features = sums.shape
    cells = own.shape[1]
    gene_width, peak_width = widths
    gene_blocks, peak_blocks = gene_width // BLOCK, peak_width // BLOCK
    side, place, core = spot[0], spot[1], spot[2]
    first = core == 0
    old = state[...]
    left, right = mine[:rank], other[:rank]
    products = jnp.concatenate([jnp.where(first, left, right), jnp.where(first, right, left)], axis=1)
    new = old * products / (exact(gram_back(mine[rank:], rank), old) + EPSILON)
    state_out[...] = new
    mine_now = new[:, :cells]
    for position in range(1, half):
        at = position * cells
        mine_now = jnp.where(place == orders[0][position], new[:, at : at + cells], mine_now)
    own[...] = mine_now
    high, rest = halved(new)
    total = [None] * (2 * peak_blocks)
    for position, j in enumerate(orders[1]):
        for b in range(gene_blocks):
            at = (position * gene_blocks + b) * BLOCK
            block = genes[:, at : at + BLOCK].astype(jnp.float32)
            row = (side * half + j) * gene_blocks + b
            for u in range(2 * peak_blocks):
                column = (place + u // peak_blocks * half) * peak_blocks + u % peak_blocks
                term = table[row, column] * block
                total[u] = term if total[u] is None else total[u] + term
    gene_links = to_gene[...]
    nothing = jnp.zeros_like(gene_links)
    links = jnp.concatenate(
        [jnp.where(side == 0, gene_links, nothing), jnp.where(side == 0, nothing, gene_links), *total], axis=1
    )
    gram = gram_of(high, rest)
    for copy in copies:
        copy.wait()
    products = jnp.dot(high, counts[...], preferred_element_type=jnp.float32)
    finish_sums(products + link_scale * links, gram, sums, coded, beside)


def update_kernel(last, widths, orders, spot, table, sums, other, beside, beside_other, factors, received, *outs):
    half = received.shape[0]
    rank, features = sums.shape
    cells = received.shape[1] - rank // 4
    if last:
        *outs, counts, sems = outs
        copies = fetch(received, orders[0], counts, sems)
    gene_width, peak_width = widths
    gene_blocks, peak_blocks = gene_width // BLOCK, peak_width // BLOCK
    side, place, core = spot[0], spot[1], spot[2]
    first = core == 0
    gram = beside[:, 0:rank] + beside_other[:, 0:rank]
    old = factors[...]
    below = exact(gram, old) + EPSILON
    groups = features // BLOCK
    whole = []
    for b in range(groups):
        code = other[:, b * BLOCK : (b + 1) * BLOCK]
        least = beside_other[:, rank + b : rank + b + 1]
        step = beside_other[:, rank + groups + b : rank + groups + b + 1]
        whole.append(sums[:, b * BLOCK : (b + 1) * BLOCK] + decode(code, least, step))
    whole = jnp.concatenate(whole, axis=1)
    new = old * whole / below
    low = new.astype(jnp.bfloat16)
    if last:
        for copy in copies:
            copy.wait()
        cell_sums = across(low, counts[...])
    else:
        cell_sums = jnp.concatenate([across(low, received[j, 0:cells, 0:features]) for j in orders[0]], axis=1)
    gram_features = across(low, low)
    kept, sent, *outs = outs
    split = half // 2 * cells
    left, right = cell_sums[:, :split], cell_sums[:, split:]
    for ref, value in ((kept, jnp.where(first, left, right)), (sent, jnp.where(first, right, left))):
        ref[:rank] = value
        ref[rank:] = gram_rows(gram_features, split)

    def own(at, width):
        return jnp.where(side == 0, new[:, at : at + width], new[:, at + width : at + 2 * width])

    if last:
        gene_out, peak_out = outs
        gene_out[...] = own(0, gene_width)
        peak_out[...] = own(2 * gene_width, peak_width)
        return
    factors_out, links_kept, links_sent, gene_low = outs
    factors_out[...] = new
    gene_low[...] = own(0, gene_width).astype(jnp.bfloat16)
    peaks = low[:, 2 * gene_width :].astype(jnp.float32)
    peaks = [peaks[:, u * BLOCK : (u + 1) * BLOCK] for u in range(2 * peak_blocks)]
    for position in range(half // 2):
        pair = []
        for j in (orders[1][position], orders[1][position + half // 2]):
            parts = []
            for b in range(gene_blocks):
                row = (side * half + j) * gene_blocks + b
                part = None
                for u, block in enumerate(peaks):
                    column = (place + u // peak_blocks * half) * peak_blocks + u % peak_blocks
                    term = table[row, column] * block
                    part = term if part is None else part + term
                parts.append(part)
            pair.append(jnp.concatenate(parts, axis=1))
        at = position * gene_width
        links_kept[:, at : at + gene_width] = jnp.where(first, *pair)
        links_sent[:, at : at + gene_width] = jnp.where(first, pair[1], pair[0])


def last_cells_kernel(spot, mine, other, old, out):
    rank, cells = out.shape
    totals = mine[:rank] + other[:rank]
    gram = mine[rank:] + other[rank:]
    lanes = totals.shape[1]
    rows = rank * rank // (4 * lanes)
    gram = jnp.concatenate(
        [gram[i * rows : (i + 1) * rows, b * rank : (b + 1) * rank] for i in range(4) for b in range(lanes // rank)],
        axis=0,
    )
    own = totals[:, :cells]
    for position in range(1, lanes // cells):
        own = jnp.where(spot[3] == position, totals[:, position * cells : (position + 1) * cells], own)
    out[...] = old[...] * own / (exact(gram, old[...]) + EPSILON)


def shards_blocks(
    rna_counts,
    atac_counts,
    cell_factor,
    gene_factor,
    peak_factor,
    link_gene,
    link_peak,
    link_weight,
    link_count,
):
    count = lax.axis_size(AXIS)
    half = count // 2
    me = lax.axis_index(AXIS)
    side, place, core = me // half, me % half, me % 2
    chip_bits = bits_below(half)[1:]
    cell_bits, link_bits, gene_bits = (turned(chip_bits, i % len(chip_bits)) for i in range(3))
    tail = sum(
        jnp.where((me & bit) != 0, 1 << i, 0) for i, bit in enumerate(reversed(cell_bits[2:]))
    )
    spot = jnp.stack([side, place, core, tail]).astype(jnp.int32)
    rank, cells = cell_factor.shape
    gene_width, peak_width = gene_factor.shape[1], peak_factor.shape[1]
    widths = (gene_width, peak_width)
    width = gene_width + peak_width
    features = 2 * width
    link_scale = cells * count / 4.0
    table_shape = (rna_counts.shape[1] // BLOCK, atac_counts.shape[1] // BLOCK)
    cell_order = layout([1] + cell_bits)
    link_order = layout([1] + link_bits)
    gene_order = layout([1] + gene_bits[::-1])

    links = (link_gene, link_peak, link_weight, link_count)
    sent = parcels(spot, rna_counts, atac_counts, cell_factor, gene_factor, peak_factor, links, half)
    halves = [list(range(half)), list(range(half, count))]
    received = lax.all_to_all(sent, AXIS, 0, 0, axis_index_groups=halves, tiled=True)
    rows_other = flip(received[:, cells:, :features], 1)
    received_here = pltpu.with_memory_space_constraint(received, pltpu.VMEM)
    codes, bounds = pl.pallas_call(
        codes_kernel,
        in_specs=[VMEM] * 2,
        out_specs=[VMEM] * 2,
        out_shape=(struct(rank, width, dtype=jnp.int16), struct(rank, 2 * rank)),
        compiler_params=PARAMS,
    )(gene_factor, peak_factor)
    rows = rank // 4
    aside = pl.pallas_call(
        table_kernel,
        grid=(1,),
        in_specs=[
            pl.BlockSpec((half, rows, 2 * rank), lambda i: (0, cells // rows, features // (2 * rank))),
            VMEM,
        ],
        out_specs=VMEM,
        out_shape=struct(rank + table_shape[0], table_shape[1]),
        compiler_params=PARAMS,
    )(received_here, bounds)
    aside_other = flip(aside, half)
    codes_other = flip(codes, half)
    aside_other, codes_other = lax.optimization_barrier((aside_other, codes_other))
    sums_shapes = (struct(rank, features), struct(rank, features, dtype=jnp.int16), struct(rank, 2 * rank))
    sums, gram, state = pl.pallas_call(
        functools.partial(first_sums_kernel, cell_order),
        in_specs=[VMEM],
        out_specs=[VMEM] * 3,
        out_shape=(struct(rank, features), struct(rank, rank), struct(rank, half * cells)),
        compiler_params=PARAMS,
    )(received_here)
    sums, coded, beside, link_table = pl.pallas_call(
        functools.partial(first_links_kernel, link_scale, widths),
        grid=(1,),
        in_specs=[
            SMEM,
            pl.BlockSpec((half, rows, features + 2 * rank), lambda i: (0, cells // rows, 0)),
            VMEM,
            VMEM,
            VMEM,
            VMEM,
            VMEM,
        ],
        out_specs=[VMEM] * 4,
        out_shape=(*sums_shapes, struct(*table_shape)),
        scratch_shapes=[pltpu.SemaphoreType.DMA, pltpu.SMEM(table_shape, jnp.float32)],
        compiler_params=PARAMS,
    )(spot, received_here, rows_other, aside, aside_other, sums, gram)

    factors = pl.pallas_call(
        twins_kernel,
        in_specs=[SMEM] + [VMEM] * 4,
        out_specs=VMEM,
        out_shape=struct(rank, features),
        compiler_params=PARAMS,
    )(spot, gene_factor, peak_factor, codes_other, aside_other)

    split = half // 2 * cells
    anywhere = pl.BlockSpec(memory_space=pl.ANY)
    fetched = [pltpu.VMEM((half * cells, features), jnp.bfloat16), pltpu.SemaphoreType.DMA((half,))]
    for sweep_index in range(ROUNDS):
        last = sweep_index == ROUNDS - 1
        beside_other = flip(beside, half)
        other = flip(coded, half)
        outs = [struct(rank + rank * rank // split, split)] * 2
        if last:
            outs += [struct(rank, gene_width), struct(rank, peak_width)]
        else:
            outs += [struct(rank, features)] + [struct(rank, half // 2 * gene_width)] * 2
            outs += [struct(rank, gene_width, dtype=jnp.bfloat16)]
        kept, sent, *outs = pl.pallas_call(
            functools.partial(update_kernel, last, widths, (cell_order, link_order)),
            in_specs=[SMEM] * 2 + [VMEM] * 5 + [anywhere if last else VMEM],
            out_specs=[VMEM] * len(outs),
            out_shape=outs,
            scratch_shapes=fetched if last else [],
            compiler_params=PARAMS,
        )(spot, link_table, sums, other, beside, beside_other, factors, in_hbm(received) if last else received_here)
        if last:
            gene_out, peak_out = outs
            totals = kept + flip(sent, 1)
            first, second = cell_bits[:2]
            quarters = jnp.split(totals[:rank], 4, axis=1)
            gram_part = jnp.concatenate(jnp.split(totals[rank:], 4, axis=1), axis=0)
            is_first, is_second = (me & first) != 0, (me & second) != 0

            def quarter(flip_first, flip_second):
                low, high = (
                    jnp.where(is_second ^ flip_second, quarters[2 * i + 1], quarters[2 * i]) for i in range(2)
                )
                return jnp.concatenate([jnp.where(is_first ^ flip_first, high, low), gram_part], axis=0)

            got = [
                flip(quarter(*which), bit)
                for which, bit in (((True, False), first), ((False, True), second), ((True, True), first | second))
            ]
            totals = quarter(False, False) + (got[0] + got[1] + got[2])
            for bit in cell_bits[2:-1]:
                totals = totals + flip(totals, bit)
            cell_out = pl.pallas_call(
                last_cells_kernel,
                in_specs=[SMEM] + [VMEM] * 3,
                out_specs=VMEM,
                out_shape=struct(rank, cells),
                compiler_params=PARAMS,
            )(spot, totals, flip(totals, cell_bits[-1]), own_cells)
            return cell_out, gene_out, peak_out
        factors, links_kept, links_sent, genes = outs
        totals = kept + flip(sent, 1)
        to_gene = links_kept + flip(links_sent, 1)
        for cell_bit, link_bit, gene_bit in zip(cell_bits, link_bits, gene_bits):
            left, right = jnp.split(to_gene, 2, axis=1)
            clear = (me & link_bit) == 0
            leaving, staying = jnp.where(clear, right, left), jnp.where(clear, left, right)
            totals, leaving, genes = lax.optimization_barrier((totals, leaving, genes))
            got = flip(totals, cell_bit), flip(leaving, link_bit), flip(genes, gene_bit)
            got = lax.optimization_barrier(got)
            totals = totals + got[0]
            to_gene = staying + got[1]
            genes = jnp.concatenate(in_order(gene_bit, genes, got[2]), axis=1)
        genes = jnp.concatenate(in_order(1, genes, flip(genes, 1)), axis=1)
        sums, coded, beside, state, own_cells = pl.pallas_call(
            functools.partial(next_sums_kernel, link_scale, widths, (cell_order, gene_order)),
            in_specs=[SMEM] * 2 + [VMEM] * 3 + [anywhere] + [VMEM] * 2,
            out_specs=[VMEM] * 5,
            scratch_shapes=fetched,
            out_shape=(*sums_shapes, struct(rank, half * cells), struct(rank, cells)),
            compiler_params=PARAMS,
        )(spot, link_table, totals, flip(totals, 1), state, in_hbm(received), to_gene, genes)


def shards(rna_counts, atac_counts, cell_factor, gene_factor, peak_factor, link_gene, *links):
    half = lax.axis_size(AXIS) // 2
    rank, cells = cell_factor.shape
    gene_width, peak_width = gene_factor.shape[1], peak_factor.shape[1]
    features = 2 * (gene_width + peak_width)
    in_blocks = (
        half % 16 == 0
        and rank == cells
        and 2 * rank == BLOCK
        and gene_width % BLOCK == 0
        and peak_width % BLOCK == 0
        and 2 * (features // BLOCK) <= rank
        and half * link_gene.shape[0] <= 2 * rank
        and rank % 64 == 0
        and atac_counts.shape[1] // BLOCK == 2 * rank
        and max(rna_counts.shape[1], atac_counts.shape[1]) // BLOCK <= 256
    )
    run = shards_blocks if in_blocks else shards_any
    return run(rna_counts, atac_counts, cell_factor, gene_factor, peak_factor, link_gene, *links)


def solution(mesh):
    columns = P(None, ("groups", "cells"))
    slots = P(("groups", "cells"))
    in_specs = (P(("groups", "cells"), None),) * 2 + (columns,) * 3 + (slots,) * 4
    return jax.shard_map(
        shards, mesh=mesh, in_specs=in_specs, out_specs=(columns,) * 3, check_vma=False
    )
```

```python
import functools

import jax
import jax.numpy as jnp
from jax import lax
from jax.experimental import pallas as pl
from jax.experimental.pallas import tpu as pltpu
from jax.sharding import PartitionSpec as P

BLOCK = 128
ROUNDS = 2
EPSILON = 1e-06
CODES = 65535.0
AXIS = "cells"
PARAMS = pltpu.CompilerParams(vmem_limit_bytes=14 * 1024 * 1024)
SMEM = pl.BlockSpec(memory_space=pltpu.SMEM)
VMEM = pl.BlockSpec(memory_space=pltpu.VMEM)


def flip(value, bit):
    count = lax.axis_size(AXIS)
    return lax.ppermute(value, AXIS, [(i, i ^ bit) for i in range(count)])


def in_order(bit, mine, other):
    mine_first = (lax.axis_index(AXIS) & bit) == 0
    return jnp.where(mine_first, mine, other), jnp.where(mine_first, other, mine)


def bits_below(size):
    return [1 << b for b in range(size.bit_length() - 1)]


def own_table(link_gene, link_peak, link_weight, link_count, gene_blocks, peak_blocks):
    slot_ids = jnp.arange(link_gene.shape[0], dtype=jnp.int32)
    live_weight = jnp.where(slot_ids < link_count[0], link_weight, 0).astype(jnp.float32)
    gene_hot = (link_gene[:, None] == jnp.arange(gene_blocks, dtype=jnp.int32)[None, :]).astype(
        jnp.float32
    )
    peak_hot = (link_peak[:, None] == jnp.arange(peak_blocks, dtype=jnp.int32)[None, :]).astype(
        jnp.float32
    )
    return jnp.dot((gene_hot * live_weight[:, None]).T, peak_hot, precision=lax.Precision.HIGHEST)


def split_low(value):
    high = lax.reduce_precision(value, exponent_bits=8, mantissa_bits=7)
    return high.astype(jnp.bfloat16), (value - high).astype(jnp.bfloat16)


def gather_half(value, half):
    for bit in bits_below(half):
        value = jnp.concatenate(in_order(bit, value, flip(value, bit)), axis=1)
    return value


def scatter_half(value, half):
    for bit in reversed(bits_below(half)):
        low, high = jnp.split(value, 2, axis=1)
        clear = (lax.axis_index(AXIS) & bit) == 0
        value = jnp.where(clear, low, high) + flip(jnp.where(clear, high, low), bit)
    return value


def weigh(weights, source):
    rank = source.shape[0]
    blocks = source.astype(jnp.float32).reshape(rank, weights.shape[1], BLOCK)
    result = jnp.einsum("ksc,ts->ktc", blocks, weights, precision=lax.Precision.HIGHEST)
    return result.reshape(rank, weights.shape[0] * BLOCK)


def coupling(link_table, factors, widths):
    gene_width, peak_width = widths
    half = lax.axis_size(AXIS) // 2
    me = lax.axis_index(AXIS)
    side, place = me // half, me % half
    low = factors.astype(jnp.bfloat16)
    genes, peaks = low[:, : 2 * gene_width], low[:, 2 * gene_width :]
    own_gene = jnp.where(side == 0, genes[:, :gene_width], genes[:, gene_width:])
    side_blocks = half * gene_width // BLOCK
    peak_blocks = peak_width // BLOCK
    side_rows = lax.dynamic_slice_in_dim(link_table, side * side_blocks, side_blocks, 0)
    weights = jnp.concatenate(
        [
            lax.dynamic_slice_in_dim(side_rows, (place + s * half) * peak_blocks, peak_blocks, 1)
            for s in range(2)
        ],
        axis=1,
    )
    to_gene = scatter_half(weigh(weights, peaks), half)
    to_peak = weigh(weights.T, gather_half(own_gene, half))
    nothing = jnp.zeros_like(to_gene)
    return jnp.concatenate([*(jnp.where(side == s, to_gene, nothing) for s in range(2)), to_peak], axis=1)


def shards_any(
    rna_counts,
    atac_counts,
    cell_factor,
    gene_factor,
    peak_factor,
    link_gene,
    link_peak,
    link_weight,
    link_count,
):
    count = lax.axis_size(AXIS)
    half = count // 2
    me = lax.axis_index(AXIS)
    side = me // half
    rank, cells = cell_factor.shape
    gene_width, peak_width = gene_factor.shape[1], peak_factor.shape[1]
    features = 2 * (gene_width + peak_width)
    link_scale = cells * count / 4.0

    link_table = own_table(
        link_gene,
        link_peak,
        link_weight,
        link_count,
        rna_counts.shape[1] // BLOCK,
        atac_counts.shape[1] // BLOCK,
    )
    for bit in bits_below(count):
        link_table = link_table + flip(link_table, bit)

    def by_place(counts, width):
        return counts.reshape(cells, 2, half, width).transpose(2, 0, 1, 3).reshape(half, cells, 2 * width)

    cell_pair = jnp.concatenate([part.T for part in split_low(cell_factor)], axis=1)
    parcels = jnp.concatenate(
        [
            by_place(rna_counts, gene_width),
            by_place(atac_counts, peak_width),
            jnp.broadcast_to(cell_pair[None], (half, cells, 2 * rank)),
        ],
        axis=2,
    )
    halves = [list(range(half)), list(range(half, count))]
    received = lax.all_to_all(parcels, AXIS, 0, 0, axis_index_groups=halves, tiled=True)
    received = received.reshape(half * cells, features + 2 * rank)
    counts, cell_pair = received[:, :features], received[:, features:]

    gene_pair = in_order(half, gene_factor, flip(gene_factor, half))
    peak_pair = in_order(half, peak_factor, flip(peak_factor, half))
    factors = jnp.concatenate([*gene_pair, *peak_pair], axis=1)
    cell_low, cell_rest = cell_pair[:, :rank].T, cell_pair[:, rank:].T
    cell_state = cell_factor

    for sweep_index in range(ROUNDS):
        links = link_scale * coupling(link_table, factors, (gene_width, peak_width))
        pair = jnp.concatenate([cell_low, cell_rest], axis=0)
        squares = lax.dot_general(
            pair, pair, (((1,), (1,)), ((), ())), preferred_element_type=jnp.float32
        )
        gram_cells = (
            squares[:rank, :rank] + squares[:rank, rank:] + squares[rank:, :rank] + squares[rank:, rank:]
        )
        sums = jnp.dot(cell_low, counts, preferred_element_type=jnp.float32) + links
        gram_cells = gram_cells + flip(gram_cells, half)
        sums = sums + flip(sums, half)
        factors = (
            factors
            * sums
            / (jnp.dot(gram_cells, factors, precision=lax.Precision.HIGHEST) + EPSILON)
        )
        low = factors.astype(jnp.bfloat16)
        gram_features = lax.dot_general(
            low, low, (((1,), (1,)), ((), ())), preferred_element_type=jnp.float32
        )
        cell_sums = lax.dot_general(
            low, counts, (((1,), (1,)), ((), ())), preferred_element_type=jnp.float32
        )
        last = sweep_index == ROUNDS - 1
        if last:
            for bit in reversed(bits_below(half)):
                left, right = jnp.split(cell_sums, 2, axis=1)
                clear = (me & bit) == 0
                sent = jnp.concatenate([jnp.where(clear, right, left), gram_features], axis=1)
                got = flip(sent, bit)
                kept = cell_sums.shape[1] // 2
                cell_sums = jnp.where(clear, left, right) + got[:, :kept]
                gram_features = gram_features + got[:, kept:]
        else:
            left, right = jnp.split(cell_sums, 2, axis=1)
            clear = (me & 1) == 0
            sent = jnp.concatenate([jnp.where(clear, right, left), gram_features], axis=1)
            kept = jnp.concatenate([jnp.where(clear, left, right), gram_features], axis=1)
            for bit in bits_below(half):
                kept = kept + flip(sent, bit)
                sent = kept
            width = cell_sums.shape[1] // 2
            cell_sums, gram_features = kept[:, :width], kept[:, width:]
            low_rest = [jnp.where(clear, *jnp.split(part, 2, axis=1)) for part in (cell_low, cell_rest)]
            cell_state = low_rest[0].astype(jnp.float32) + low_rest[1].astype(jnp.float32)
        cell_state = (
            cell_state
            * cell_sums
            / (jnp.dot(gram_features, cell_state, precision=lax.Precision.HIGHEST) + EPSILON)
        )
        if not last:
            pair = jnp.concatenate(split_low(cell_state), axis=0)
            pair = jnp.concatenate(in_order(1, pair, flip(pair, 1)), axis=1)
            cell_low, cell_rest = pair[:rank], pair[rank:]
            mine = lax.dynamic_slice_in_dim(pair, (me % half) * cells, cells, 1).astype(jnp.float32)
            cell_state = mine[:rank] + mine[rank:]

    def own(first, width):
        return jnp.where(side == 0, factors[:, first : first + width], factors[:, first + width : first + 2 * width])

    return cell_state, own(0, gene_width), own(2 * gene_width, peak_width)


def layout(bits):
    size = 1 << len(bits)
    return [
        sum(bit for i, bit in enumerate(bits) if position >> (len(bits) - 1 - i) & 1)
        for position in range(size)
    ]


def turned(bits, by):
    return bits[by:] + bits[:by]


def across(left, right):
    return lax.dot_general(left, right, (((1,), (1,)), ((), ())), preferred_element_type=jnp.float32)


def exact(left, right):
    return lax.dot_general(
        left,
        right,
        (((1,), (0,)), ((), ())),
        precision=lax.Precision.HIGHEST,
        preferred_element_type=jnp.float32,
    )


def halved(value):
    high = value.astype(jnp.bfloat16)
    return high, (value - high.astype(jnp.float32)).astype(jnp.bfloat16)


def struct(*shape, dtype=jnp.float32):
    return jax.ShapeDtypeStruct(shape, dtype)


def gram_of(high, rest):
    pair = jnp.concatenate([high, rest], axis=0)
    squares = across(pair, pair)
    rank = high.shape[0]
    return (squares[:rank, :rank] + squares[rank:, rank:]) + (squares[:rank, rank:] + squares[rank:, :rank])


def parcels_kernel(spot, rna_0, rna_1, atac_0, atac_1, cell, gene, peak, *refs):
    links, out, copied, slots, sems = refs[:4], refs[4], refs[5:9], refs[9], refs[10]

    copies = [pltpu.make_async_copy(link, to, sems.at[i]) for i, (link, to) in enumerate(zip(links, copied))]

    @pl.when(pl.program_id(0) == 0)
    def _():
        for copy in copies:
            copy.start()

    rank = cell.shape[0]
    cells = rna_0.shape[0]
    gene_width, peak_width = gene.shape[1], peak.shape[1]
    width = gene_width + peak_width
    cell_pair = jnp.concatenate(halved(cell[...]), axis=1)
    gene_low = gene[...].astype(jnp.bfloat16)
    peak_low = peak[...].astype(jnp.bfloat16)
    part = rank // 4
    for j in range(out.shape[0]):
        at = 0
        for source, size in ((rna_0, gene_width), (rna_1, gene_width), (atac_0, peak_width), (atac_1, peak_width)):
            out[j, 0:cells, at : at + size] = source[:, j * size : (j + 1) * size]
            at += size
        out[j, 0:cells, at:] = cell_pair
        for s in range(2):
            row = (2 * (j % 2) + s) * part
            out[j, cells:, s * width : s * width + gene_width] = gene_low[row : row + part]
            out[j, cells:, s * width + gene_width : (s + 1) * width] = peak_low[row : row + part]

    @pl.when(pl.program_id(0) == 0)
    def _():
        for copy in copies:
            copy.wait()
        link_gene, link_peak, link_weight, link_count = copied
        count = link_gene.shape[0]
        lane = lax.broadcasted_iota(jnp.int32, slots.shape, 1) - spot[1] * count
        row = lax.broadcasted_iota(jnp.int32, slots.shape, 0)
        value = jnp.zeros(slots.shape, jnp.float32)
        for s in range(count):
            weight = jnp.where(s < link_count[0], link_weight[s], 0)
            for r, entry in enumerate((link_gene[s], link_peak[s], weight)):
                value = jnp.where((lane == s) & (row == r), entry.astype(jnp.float32), value)
        slots[...] = value.astype(jnp.bfloat16)

    for j in range(out.shape[0]):
        out[j, cells:, 2 * width :] = slots[...]


def encode(group):
    least = jnp.min(group, axis=1, keepdims=True)
    spread = jnp.max(group, axis=1, keepdims=True) - least
    per = jnp.where(spread > 0.0, CODES / spread, 0.0)
    code = jnp.minimum(jnp.floor((group - least) * per + 0.5), CODES) - (CODES + 1) / 2
    return code.astype(jnp.int32).astype(jnp.int16), least, spread / CODES


def decode(code, least, step):
    return least + (code.astype(jnp.int32).astype(jnp.float32) + (CODES + 1) / 2) * step


def codes_kernel(gene, peak, codes, bounds):
    rank, width = codes.shape
    gene_width = gene.shape[1]
    least, step = [], []
    for b in range(width // BLOCK):
        ref, at = (gene, b * BLOCK) if b * BLOCK < gene_width else (peak, b * BLOCK - gene_width)
        code, low, per = encode(ref[:, at : at + BLOCK])
        codes[:, b * BLOCK : (b + 1) * BLOCK] = code
        least.append(low)
        step.append(per)
    pad = jnp.zeros((rank, 2 * rank - 2 * len(least)), jnp.float32)
    columns = jnp.concatenate([*least, *step, pad], axis=1)
    square = jnp.concatenate([columns, jnp.zeros_like(columns)], axis=0)
    bounds[...] = square.T[: bounds.shape[0]]


def table_kernel(received_slots, bounds, out):
    above = bounds.shape[0]
    out[:above] = bounds[...]
    slots = sum(received_slots[j].astype(jnp.float32) for j in range(received_slots.shape[0]))

    def hot(row, size, value):
        ids = lax.broadcasted_iota(jnp.int32, (size, slots.shape[1]), 0).astype(jnp.float32)
        return jnp.where(slots[row : row + 1] == ids, value, 0.0).astype(jnp.bfloat16)

    out[above:] = across(hot(0, out.shape[0] - above, slots[2:3]), hot(1, out.shape[1], 1.0))


def twins_kernel(spot, gene, peak, codes, beside, out):
    gene_width, peak_width = gene.shape[1], peak.shape[1]
    groups = (gene_width + peak_width) // BLOCK
    lanes = beside.shape[1]
    above = -(-2 * groups // 8) * 8
    square = jnp.concatenate([beside[:above], jnp.zeros((lanes - above, lanes), jnp.float32)], axis=0)
    bounds = square.T[: gene.shape[0]]
    at = 0
    first = spot[0] == 0
    for ref, start in ((gene, 0), (peak, gene_width)):
        size = ref.shape[1]
        for b in range(size // BLOCK):
            g = start // BLOCK + b
            mine = ref[:, b * BLOCK : (b + 1) * BLOCK]
            code = codes[:, g * BLOCK : (g + 1) * BLOCK]
            other = decode(code, bounds[:, g : g + 1], bounds[:, groups + g : groups + g + 1])
            out[:, at + b * BLOCK : at + (b + 1) * BLOCK] = jnp.where(first, mine, other)
            out[:, at + size + b * BLOCK : at + size + (b + 1) * BLOCK] = jnp.where(first, other, mine)
        at += 2 * size


def in_hbm(value):
    return pltpu.with_memory_space_constraint(value, pltpu.HBM)


def parcels(spot, rna_counts, atac_counts, cell_factor, gene_factor, peak_factor, links, half):
    cells = rna_counts.shape[0]
    rank = cell_factor.shape[0]
    gene_width, peak_width = gene_factor.shape[1], peak_factor.shape[1]
    rows, lanes = cells + rank // 4, 2 * (gene_width + peak_width) + 2 * rank
    each = 4
    steps = half // each

    def columns(width, side):
        return pl.BlockSpec((cells, each * width), lambda i: (0, i + side * steps))

    def whole(array):
        return pl.BlockSpec(array.shape, lambda i: (0, 0))

    return pl.pallas_call(
        parcels_kernel,
        grid=(steps,),
        in_specs=[SMEM, columns(gene_width, 0), columns(gene_width, 1), columns(peak_width, 0), columns(peak_width, 1)]
        + [whole(a) for a in (cell_factor, gene_factor, peak_factor)]
        + [pl.BlockSpec(memory_space=pl.ANY)] * 4,
        out_specs=pl.BlockSpec((each, rows, lanes), lambda i: (i, 0, 0)),
        out_shape=struct(half, rows, lanes, dtype=jnp.bfloat16),
        scratch_shapes=[pltpu.SMEM(link.shape, jnp.int32) for link in links]
        + [pltpu.VMEM((rank // 4, 2 * rank), jnp.bfloat16), pltpu.SemaphoreType.DMA((4,))],
        compiler_params=PARAMS,
    )(
        spot,
        *(in_hbm(a) for a in (rna_counts, rna_counts, atac_counts, atac_counts, cell_factor, gene_factor, peak_factor)),
        *(in_hbm(a) for a in links[:-1]),
        links[-1],
    )


def first_sums_kernel(order, received, sums, gram, state):
    rank, features = sums.shape
    cells = received.shape[1] - rank // 4
    high = jnp.concatenate([received[j, 0:cells, features : features + rank] for j in order], axis=1)
    rest = jnp.concatenate([received[j, 0:cells, features + rank :] for j in order], axis=1)
    counts = jnp.concatenate([received[j, 0:cells, 0:features] for j in order], axis=0)
    sums[...] = jnp.dot(high, counts, preferred_element_type=jnp.float32)
    gram[...] = gram_of(high, rest)
    state[...] = high.astype(jnp.float32) + rest.astype(jnp.float32)


def finish_sums(sums_value, gram_value, sums, coded, beside):
    rank, features = sums_value.shape
    least, step = [], []
    for b in range(features // BLOCK):
        group = sums_value[:, b * BLOCK : (b + 1) * BLOCK]
        sums[:, b * BLOCK : (b + 1) * BLOCK] = group
        code, low, per = encode(group)
        coded[:, b * BLOCK : (b + 1) * BLOCK] = code
        least.append(low)
        step.append(per)
    pad = jnp.zeros((rank, beside.shape[1] - rank - 2 * len(least)), jnp.float32)
    beside[...] = jnp.concatenate([gram_value, *least, *step, pad], axis=1)


def first_links_kernel(
    link_scale, widths, spot, mine, other, aside, aside_other, sums_in, gram, sums, coded, beside, table, sem, table_smem
):
    half = mine.shape[0]
    rank, features = sums_in.shape
    gene_width, peak_width = widths
    gene_blocks, peak_blocks = gene_width // BLOCK, peak_width // BLOCK
    width = gene_width + peak_width
    above = aside.shape[0] - table.shape[0]
    table[...] = aside[above:] + aside_other[above:]
    copy = pltpu.make_async_copy(table, table_smem, sem)
    copy.start()
    copy.wait()
    side, place, core = spot[0], spot[1], spot[2]
    total = [None] * (features // BLOCK)

    def add(target, weight, block):
        term = weight * block
        total[target] = term if total[target] is None else total[target] + term

    for j in range(half):
        blocks = []
        for b in range(width // BLOCK):
            pieces = [
                ref[j, :, s * width + b * BLOCK : s * width + (b + 1) * BLOCK] for ref in (mine, other) for s in range(2)
            ]
            blocks.append(jnp.concatenate(pieces, axis=0).astype(jnp.float32))
        for b in range(gene_blocks):
            row = (side * half + j) * gene_blocks + b
            for u in range(2 * peak_blocks):
                column = (place + u // peak_blocks * half) * peak_blocks + u % peak_blocks
                add(2 * gene_blocks + u, table_smem[row, column], blocks[b])
        for b in range(peak_blocks):
            column = (side * half + j) * peak_blocks + b
            for t in range(2 * gene_blocks):
                row = (place + t // gene_blocks * half) * gene_blocks + t % gene_blocks
                add(t, table_smem[row, column], blocks[gene_blocks + b])
    links = jnp.concatenate(total, axis=1)
    ahead, behind = links[: rank // 2], links[rank // 2 :]
    first = core == 0
    links = jnp.concatenate([jnp.where(first, ahead, behind), jnp.where(first, behind, ahead)], axis=0)
    finish_sums(sums_in[...] + link_scale * links, gram[...], sums, coded, beside)


def gram_rows(gram, lanes):
    rank = gram.shape[0]
    rows = rank * rank // lanes
    return jnp.concatenate([gram[b * rows : (b + 1) * rows] for b in range(rank // rows)], axis=1)


def gram_back(rows_value, rank):
    return jnp.concatenate(
        [rows_value[:, b * rank : (b + 1) * rank] for b in range(rows_value.shape[1] // rank)], axis=0
    )


def step_kernel(link_bit, gene_bit, spot, totals, totals_got, staying, staying_got, *refs):
    if gene_bit:
        genes, genes_got, *refs = refs
    received, totals_out, *outs = refs
    totals_out[...] = totals[...] + totals_got[...]
    to_gene = staying[...] + staying_got[...]
    if gene_bit:
        genes_out, *outs = outs
        width = genes.shape[1]
        clear = (spot[1] // gene_bit) % 2 == 0
        left, right = genes[...].astype(jnp.float32), genes_got[...].astype(jnp.float32)
        genes_out[:, :width] = jnp.where(clear, left, right).astype(jnp.bfloat16)
        genes_out[:, width:] = jnp.where(clear, right, left).astype(jnp.bfloat16)
    if link_bit:
        clear = (spot[1] // link_bit) % 2 == 0
        width = to_gene.shape[1] // 2
        left, right = to_gene[:, :width], to_gene[:, width:]
        outs[0][...] = jnp.where(clear, left, right)
        outs[1][...] = jnp.where(clear, right, left)
    else:
        outs[0][...] = to_gene


def step(spot, received, link_bit, gene_bit, totals, staying, genes=None):
    rank, width = staying[0].shape
    outs = [struct(*totals[0].shape)]
    if gene_bit:
        outs += [struct(rank, 2 * genes[0].shape[1], dtype=jnp.bfloat16)]
    outs += [struct(rank, width // 2)] * 2 if link_bit else [struct(rank, width)]
    values = [*totals, *staying, *(genes if gene_bit else ()), received]
    return pl.pallas_call(
        functools.partial(step_kernel, link_bit, gene_bit),
        in_specs=[SMEM] + [VMEM] * len(values),
        out_specs=[VMEM] * len(outs),
        out_shape=outs,
        compiler_params=PARAMS,
    )(spot, *values)


def next_sums_kernel(
    link_scale, widths, orders, spot, table, mine, other, state, received, to_gene, genes_mine, genes_other, *refs
):
    sums, coded, beside, state_out, own = refs
    half = received.shape[0]
    rank, features = sums.shape
    cells = own.shape[1]
    gene_width, peak_width = widths
    gene_blocks, peak_blocks = gene_width // BLOCK, peak_width // BLOCK
    side, place, core = spot[0], spot[1], spot[2]
    first = core == 0
    old = state[...]
    left, right = mine[:rank], other[:rank]
    products = jnp.concatenate([jnp.where(first, left, right), jnp.where(first, right, left)], axis=1)
    new = old * products / (exact(gram_back(mine[rank:], rank), old) + EPSILON)
    state_out[...] = new
    mine_now = new[:, :cells]
    for position in range(1, half):
        at = position * cells
        mine_now = jnp.where(place == orders[0][position], new[:, at : at + cells], mine_now)
    own[...] = mine_now
    high, rest = halved(new)
    mine_low, other_low = genes_mine[...].astype(jnp.float32), genes_other[...].astype(jnp.float32)
    genes = jnp.concatenate(
        [jnp.where(first, mine_low, other_low), jnp.where(first, other_low, mine_low)], axis=1
    )
    total = [None] * (2 * peak_blocks)
    for position, j in enumerate(orders[1]):
        for b in range(gene_blocks):
            at = (position * gene_blocks + b) * BLOCK
            block = genes[:, at : at + BLOCK]
            row = (side * half + j) * gene_blocks + b
            for u in range(2 * peak_blocks):
                column = (place + u // peak_blocks * half) * peak_blocks + u % peak_blocks
                term = table[row, column] * block
                total[u] = term if total[u] is None else total[u] + term
    gene_links = to_gene[...]
    nothing = jnp.zeros_like(gene_links)
    links = jnp.concatenate(
        [jnp.where(side == 0, gene_links, nothing), jnp.where(side == 0, nothing, gene_links), *total], axis=1
    )
    counts = jnp.concatenate([received[j, 0:cells, 0:features] for j in orders[0]], axis=0)
    products = jnp.dot(high, counts, preferred_element_type=jnp.float32)
    finish_sums(products + link_scale * links, gram_of(high, rest), sums, coded, beside)


def update_kernel(last, widths, orders, spot, table, sums, other, beside, beside_other, factors, received, *outs):
    half = received.shape[0]
    rank, features = sums.shape
    cells = received.shape[1] - rank // 4
    gene_width, peak_width = widths
    gene_blocks, peak_blocks = gene_width // BLOCK, peak_width // BLOCK
    side, place, core = spot[0], spot[1], spot[2]
    first = core == 0
    gram = beside[:, 0:rank] + beside_other[:, 0:rank]
    old = factors[...]
    below = exact(gram, old) + EPSILON
    groups = features // BLOCK
    whole = []
    for b in range(groups):
        code = other[:, b * BLOCK : (b + 1) * BLOCK]
        least = beside_other[:, rank + b : rank + b + 1]
        step = beside_other[:, rank + groups + b : rank + groups + b + 1]
        whole.append(sums[:, b * BLOCK : (b + 1) * BLOCK] + decode(code, least, step))
    whole = jnp.concatenate(whole, axis=1)
    new = old * whole / below
    low = new.astype(jnp.bfloat16)
    cell_sums = jnp.concatenate([across(low, received[j, 0:cells, 0:features]) for j in orders[0]], axis=1)
    gram_features = across(low, low)
    kept, sent, *outs = outs
    split = half // 2 * cells
    left, right = cell_sums[:, :split], cell_sums[:, split:]
    for ref, value in ((kept, jnp.where(first, left, right)), (sent, jnp.where(first, right, left))):
        ref[:rank] = value
        ref[rank:] = gram_rows(gram_features, split)

    def own(at, width):
        return jnp.where(side == 0, new[:, at : at + width], new[:, at + width : at + 2 * width])

    if last:
        gene_out, peak_out = outs
        gene_out[...] = own(0, gene_width)
        peak_out[...] = own(2 * gene_width, peak_width)
        return
    factors_out, links_kept, links_sent, gene_low = outs
    factors_out[...] = new
    gene_low[...] = own(0, gene_width).astype(jnp.bfloat16)
    peaks = low[:, 2 * gene_width :].astype(jnp.float32)
    peaks = [peaks[:, u * BLOCK : (u + 1) * BLOCK] for u in range(2 * peak_blocks)]
    for position in range(half // 2):
        pair = []
        for j in (orders[1][position], orders[1][position + half // 2]):
            parts = []
            for b in range(gene_blocks):
                row = (side * half + j) * gene_blocks + b
                part = None
                for u, block in enumerate(peaks):
                    column = (place + u // peak_blocks * half) * peak_blocks + u % peak_blocks
                    term = table[row, column] * block
                    part = term if part is None else part + term
                parts.append(part)
            pair.append(jnp.concatenate(parts, axis=1))
        at = position * gene_width
        links_kept[:, at : at + gene_width] = jnp.where(first, *pair)
        links_sent[:, at : at + gene_width] = jnp.where(first, pair[1], pair[0])


def last_cells_kernel(spot, mine, other, old, out):
    rank, cells = out.shape
    totals = mine[:rank] + other[:rank]
    gram = mine[rank:] + other[rank:]
    lanes = totals.shape[1]
    rows = rank * rank // (4 * lanes)
    gram = jnp.concatenate(
        [gram[i * rows : (i + 1) * rows, b * rank : (b + 1) * rank] for i in range(4) for b in range(lanes // rank)],
        axis=0,
    )
    own = totals[:, :cells]
    for position in range(1, lanes // cells):
        own = jnp.where(spot[3] == position, totals[:, position * cells : (position + 1) * cells], own)
    out[...] = old[...] * own / (exact(gram, old[...]) + EPSILON)


def shards_blocks(
    rna_counts,
    atac_counts,
    cell_factor,
    gene_factor,
    peak_factor,
    link_gene,
    link_peak,
    link_weight,
    link_count,
):
    count = lax.axis_size(AXIS)
    half = count // 2
    me = lax.axis_index(AXIS)
    side, place, core = me // half, me % half, me % 2
    chip_bits = bits_below(half)[1:]
    cell_bits, link_bits, gene_bits = (turned(chip_bits, i % len(chip_bits)) for i in range(3))
    tail = sum(
        jnp.where((me & bit) != 0, 1 << i, 0) for i, bit in enumerate(reversed(cell_bits[2:]))
    )
    spot = jnp.stack([side, place, core, tail]).astype(jnp.int32)
    rank, cells = cell_factor.shape
    gene_width, peak_width = gene_factor.shape[1], peak_factor.shape[1]
    widths = (gene_width, peak_width)
    width = gene_width + peak_width
    features = 2 * width
    link_scale = cells * count / 4.0
    table_shape = (rna_counts.shape[1] // BLOCK, atac_counts.shape[1] // BLOCK)
    cell_order = layout([1] + cell_bits)
    link_order = layout([1] + link_bits)
    gene_order = layout([1] + gene_bits[::-1])

    links = (link_gene, link_peak, link_weight, link_count)
    sent = parcels(spot, rna_counts, atac_counts, cell_factor, gene_factor, peak_factor, links, half)
    halves = [list(range(half)), list(range(half, count))]
    received = lax.all_to_all(sent, AXIS, 0, 0, axis_index_groups=halves, tiled=True)
    rows_other = flip(received[:, cells:, :features], 1)
    received_here = pltpu.with_memory_space_constraint(received, pltpu.VMEM)
    above = -(-2 * width // BLOCK // 8) * 8
    codes, bounds = pl.pallas_call(
        codes_kernel,
        in_specs=[VMEM] * 2,
        out_specs=[VMEM] * 2,
        out_shape=(struct(rank, width, dtype=jnp.int16), struct(above, 2 * rank)),
        compiler_params=PARAMS,
    )(gene_factor, peak_factor)
    rows = rank // 4
    aside = pl.pallas_call(
        table_kernel,
        grid=(1,),
        in_specs=[
            pl.BlockSpec((half, rows, 2 * rank), lambda i: (0, cells // rows, features // (2 * rank))),
            VMEM,
        ],
        out_specs=VMEM,
        out_shape=struct(above + table_shape[0], table_shape[1]),
        compiler_params=PARAMS,
    )(received_here, bounds)
    aside_other = flip(aside, half)
    sums_shapes = (struct(rank, features), struct(rank, features, dtype=jnp.int16), struct(rank, 2 * rank))
    sums, gram, state = pl.pallas_call(
        functools.partial(first_sums_kernel, cell_order),
        in_specs=[VMEM],
        out_specs=[VMEM] * 3,
        out_shape=(struct(rank, features), struct(rank, rank), struct(rank, half * cells)),
        compiler_params=PARAMS,
    )(received_here)
    codes, sums = lax.optimization_barrier((codes, sums))
    codes_other = flip(codes, half)
    sums, coded, beside, link_table = pl.pallas_call(
        functools.partial(first_links_kernel, link_scale, widths),
        grid=(1,),
        in_specs=[
            SMEM,
            pl.BlockSpec((half, rows, features + 2 * rank), lambda i: (0, cells // rows, 0)),
            VMEM,
            VMEM,
            VMEM,
            VMEM,
            VMEM,
        ],
        out_specs=[VMEM] * 4,
        out_shape=(*sums_shapes, struct(*table_shape)),
        scratch_shapes=[pltpu.SemaphoreType.DMA, pltpu.SMEM(table_shape, jnp.float32)],
        compiler_params=PARAMS,
    )(spot, received_here, rows_other, aside, aside_other, sums, gram)

    coded, beside, codes_other = lax.optimization_barrier((coded, beside, codes_other))
    factors = pl.pallas_call(
        twins_kernel,
        in_specs=[SMEM] + [VMEM] * 4,
        out_specs=VMEM,
        out_shape=struct(rank, features),
        compiler_params=PARAMS,
    )(spot, gene_factor, peak_factor, codes_other, aside_other)

    split = half // 2 * cells
    for sweep_index in range(ROUNDS):
        last = sweep_index == ROUNDS - 1
        beside_other = flip(beside, half)
        other = flip(coded, half)
        outs = [struct(rank + rank * rank // split, split)] * 2
        if last:
            outs += [struct(rank, gene_width), struct(rank, peak_width)]
        else:
            outs += [struct(rank, features)] + [struct(rank, half // 2 * gene_width)] * 2
            outs += [struct(rank, gene_width, dtype=jnp.bfloat16)]
        kept, sent, *outs = pl.pallas_call(
            functools.partial(update_kernel, last, widths, (cell_order, link_order)),
            in_specs=[SMEM] * 2 + [VMEM] * 6,
            out_specs=[VMEM] * len(outs),
            out_shape=outs,
            compiler_params=PARAMS,
        )(spot, link_table, sums, other, beside, beside_other, factors, received_here)
        if last:
            gene_out, peak_out = outs
            totals = kept + flip(sent, 1)
            first, second = cell_bits[:2]
            quarters = jnp.split(totals[:rank], 4, axis=1)
            gram_part = jnp.concatenate(jnp.split(totals[rank:], 4, axis=1), axis=0)
            is_first, is_second = (me & first) != 0, (me & second) != 0

            def quarter(flip_first, flip_second):
                low, high = (
                    jnp.where(is_second ^ flip_second, quarters[2 * i + 1], quarters[2 * i]) for i in range(2)
                )
                return jnp.concatenate([jnp.where(is_first ^ flip_first, high, low), gram_part], axis=0)

            got = [
                flip(quarter(*which), bit)
                for which, bit in (((True, False), first), ((False, True), second), ((True, True), first | second))
            ]
            totals = quarter(False, False) + (got[0] + got[1] + got[2])
            for bit in cell_bits[2:-1]:
                totals = totals + flip(totals, bit)
            cell_out = pl.pallas_call(
                last_cells_kernel,
                in_specs=[SMEM] + [VMEM] * 3,
                out_specs=VMEM,
                out_shape=struct(rank, cells),
                compiler_params=PARAMS,
            )(spot, totals, flip(totals, cell_bits[-1]), own_cells)
            return cell_out, gene_out, peak_out
        factors, links_kept, links_sent, genes = outs
        totals, staying, leaving = step(
            spot, received_here, link_bits[0], 0, (kept, flip(sent, 1)), (links_kept, flip(links_sent, 1))
        )
        for i, bits in enumerate(zip(cell_bits, link_bits, gene_bits)):
            going = lax.optimization_barrier((totals, leaving, genes))
            got = lax.optimization_barrier(tuple(flip(value, bit) for value, bit in zip(going, bits)))
            next_bit = link_bits[i + 1] if i + 1 < len(link_bits) else 0
            totals, genes, staying, *leaving = step(
                spot, received_here, next_bit, bits[2], (totals, got[0]), (staying, got[1]), (genes, got[2])
            )
            leaving = leaving[0] if next_bit else None
        to_gene = staying
        sums, coded, beside, state, own_cells = pl.pallas_call(
            functools.partial(next_sums_kernel, link_scale, widths, (cell_order, gene_order)),
            in_specs=[SMEM] * 2 + [VMEM] * 7,
            out_specs=[VMEM] * 5,
            out_shape=(*sums_shapes, struct(rank, half * cells), struct(rank, cells)),
            compiler_params=PARAMS,
        )(spot, link_table, totals, flip(totals, 1), state, received_here, to_gene, genes, flip(genes, 1))


def shards(rna_counts, atac_counts, cell_factor, gene_factor, peak_factor, link_gene, *links):
    half = lax.axis_size(AXIS) // 2
    rank, cells = cell_factor.shape
    gene_width, peak_width = gene_factor.shape[1], peak_factor.shape[1]
    features = 2 * (gene_width + peak_width)
    in_blocks = (
        half % 16 == 0
        and rank == cells
        and 2 * rank == BLOCK
        and gene_width % BLOCK == 0
        and peak_width % BLOCK == 0
        and 2 * (features // BLOCK) <= rank
        and half * link_gene.shape[0] <= 2 * rank
        and rank % 64 == 0
        and atac_counts.shape[1] // BLOCK == 2 * rank
        and max(rna_counts.shape[1], atac_counts.shape[1]) // BLOCK <= 256
    )
    run = shards_blocks if in_blocks else shards_any
    return run(rna_counts, atac_counts, cell_factor, gene_factor, peak_factor, link_gene, *links)


def solution(mesh):
    columns = P(None, ("groups", "cells"))
    slots = P(("groups", "cells"))
    in_specs = (P(("groups", "cells"), None),) * 2 + (columns,) * 3 + (slots,) * 4
    return jax.shard_map(
        shards, mesh=mesh, in_specs=in_specs, out_specs=(columns,) * 3, check_vma=False
    )
```

```python
import functools

import jax
import jax.numpy as jnp
from jax import lax
from jax.experimental import pallas as pl
from jax.experimental.pallas import tpu as pltpu
from jax.sharding import PartitionSpec as P

BLOCK = 128
ROUNDS = 2
EPSILON = 1e-06
CODES = 65535.0
DIGIT = 32768.0
TINY = 1e-30
AXIS = "cells"
PARAMS = pltpu.CompilerParams(vmem_limit_bytes=14 * 1024 * 1024)
SMEM = pl.BlockSpec(memory_space=pltpu.SMEM)
VMEM = pl.BlockSpec(memory_space=pltpu.VMEM)


def flip(value, bit):
    count = lax.axis_size(AXIS)
    return lax.ppermute(value, AXIS, [(i, i ^ bit) for i in range(count)])


def in_order(bit, mine, other):
    mine_first = (lax.axis_index(AXIS) & bit) == 0
    return jnp.where(mine_first, mine, other), jnp.where(mine_first, other, mine)


def bits_below(size):
    return [1 << b for b in range(size.bit_length() - 1)]


def own_table(link_gene, link_peak, link_weight, link_count, gene_blocks, peak_blocks):
    slot_ids = jnp.arange(link_gene.shape[0], dtype=jnp.int32)
    live_weight = jnp.where(slot_ids < link_count[0], link_weight, 0).astype(jnp.float32)
    gene_hot = (link_gene[:, None] == jnp.arange(gene_blocks, dtype=jnp.int32)[None, :]).astype(
        jnp.float32
    )
    peak_hot = (link_peak[:, None] == jnp.arange(peak_blocks, dtype=jnp.int32)[None, :]).astype(
        jnp.float32
    )
    return jnp.dot((gene_hot * live_weight[:, None]).T, peak_hot, precision=lax.Precision.HIGHEST)


def split_low(value):
    high = lax.reduce_precision(value, exponent_bits=8, mantissa_bits=7)
    return high.astype(jnp.bfloat16), (value - high).astype(jnp.bfloat16)


def gather_half(value, half):
    for bit in bits_below(half):
        value = jnp.concatenate(in_order(bit, value, flip(value, bit)), axis=1)
    return value


def scatter_half(value, half):
    for bit in reversed(bits_below(half)):
        low, high = jnp.split(value, 2, axis=1)
        clear = (lax.axis_index(AXIS) & bit) == 0
        value = jnp.where(clear, low, high) + flip(jnp.where(clear, high, low), bit)
    return value


def weigh(weights, source):
    rank = source.shape[0]
    blocks = source.astype(jnp.float32).reshape(rank, weights.shape[1], BLOCK)
    result = jnp.einsum("ksc,ts->ktc", blocks, weights, precision=lax.Precision.HIGHEST)
    return result.reshape(rank, weights.shape[0] * BLOCK)


def coupling(link_table, factors, widths):
    gene_width, peak_width = widths
    half = lax.axis_size(AXIS) // 2
    me = lax.axis_index(AXIS)
    side, place = me // half, me % half
    low = factors.astype(jnp.bfloat16)
    genes, peaks = low[:, : 2 * gene_width], low[:, 2 * gene_width :]
    own_gene = jnp.where(side == 0, genes[:, :gene_width], genes[:, gene_width:])
    side_blocks = half * gene_width // BLOCK
    peak_blocks = peak_width // BLOCK
    side_rows = lax.dynamic_slice_in_dim(link_table, side * side_blocks, side_blocks, 0)
    weights = jnp.concatenate(
        [
            lax.dynamic_slice_in_dim(side_rows, (place + s * half) * peak_blocks, peak_blocks, 1)
            for s in range(2)
        ],
        axis=1,
    )
    to_gene = scatter_half(weigh(weights, peaks), half)
    to_peak = weigh(weights.T, gather_half(own_gene, half))
    nothing = jnp.zeros_like(to_gene)
    return jnp.concatenate([*(jnp.where(side == s, to_gene, nothing) for s in range(2)), to_peak], axis=1)


def shards_any(
    rna_counts,
    atac_counts,
    cell_factor,
    gene_factor,
    peak_factor,
    link_gene,
    link_peak,
    link_weight,
    link_count,
):
    count = lax.axis_size(AXIS)
    half = count // 2
    me = lax.axis_index(AXIS)
    side = me // half
    rank, cells = cell_factor.shape
    gene_width, peak_width = gene_factor.shape[1], peak_factor.shape[1]
    features = 2 * (gene_width + peak_width)
    link_scale = cells * count / 4.0

    link_table = own_table(
        link_gene,
        link_peak,
        link_weight,
        link_count,
        rna_counts.shape[1] // BLOCK,
        atac_counts.shape[1] // BLOCK,
    )
    for bit in bits_below(count):
        link_table = link_table + flip(link_table, bit)

    def by_place(counts, width):
        return counts.reshape(cells, 2, half, width).transpose(2, 0, 1, 3).reshape(half, cells, 2 * width)

    cell_pair = jnp.concatenate([part.T for part in split_low(cell_factor)], axis=1)
    parcels = jnp.concatenate(
        [
            by_place(rna_counts, gene_width),
            by_place(atac_counts, peak_width),
            jnp.broadcast_to(cell_pair[None], (half, cells, 2 * rank)),
        ],
        axis=2,
    )
    halves = [list(range(half)), list(range(half, count))]
    received = lax.all_to_all(parcels, AXIS, 0, 0, axis_index_groups=halves, tiled=True)
    received = received.reshape(half * cells, features + 2 * rank)
    counts, cell_pair = received[:, :features], received[:, features:]

    gene_pair = in_order(half, gene_factor, flip(gene_factor, half))
    peak_pair = in_order(half, peak_factor, flip(peak_factor, half))
    factors = jnp.concatenate([*gene_pair, *peak_pair], axis=1)
    cell_low, cell_rest = cell_pair[:, :rank].T, cell_pair[:, rank:].T
    cell_state = cell_factor

    for sweep_index in range(ROUNDS):
        links = link_scale * coupling(link_table, factors, (gene_width, peak_width))
        pair = jnp.concatenate([cell_low, cell_rest], axis=0)
        squares = lax.dot_general(
            pair, pair, (((1,), (1,)), ((), ())), preferred_element_type=jnp.float32
        )
        gram_cells = (
            squares[:rank, :rank] + squares[:rank, rank:] + squares[rank:, :rank] + squares[rank:, rank:]
        )
        sums = jnp.dot(cell_low, counts, preferred_element_type=jnp.float32) + links
        gram_cells = gram_cells + flip(gram_cells, half)
        sums = sums + flip(sums, half)
        factors = (
            factors
            * sums
            / (jnp.dot(gram_cells, factors, precision=lax.Precision.HIGHEST) + EPSILON)
        )
        low = factors.astype(jnp.bfloat16)
        gram_features = lax.dot_general(
            low, low, (((1,), (1,)), ((), ())), preferred_element_type=jnp.float32
        )
        cell_sums = lax.dot_general(
            low, counts, (((1,), (1,)), ((), ())), preferred_element_type=jnp.float32
        )
        last = sweep_index == ROUNDS - 1
        if last:
            for bit in reversed(bits_below(half)):
                left, right = jnp.split(cell_sums, 2, axis=1)
                clear = (me & bit) == 0
                sent = jnp.concatenate([jnp.where(clear, right, left), gram_features], axis=1)
                got = flip(sent, bit)
                kept = cell_sums.shape[1] // 2
                cell_sums = jnp.where(clear, left, right) + got[:, :kept]
                gram_features = gram_features + got[:, kept:]
        else:
            left, right = jnp.split(cell_sums, 2, axis=1)
            clear = (me & 1) == 0
            sent = jnp.concatenate([jnp.where(clear, right, left), gram_features], axis=1)
            kept = jnp.concatenate([jnp.where(clear, left, right), gram_features], axis=1)
            for bit in bits_below(half):
                kept = kept + flip(sent, bit)
                sent = kept
            width = cell_sums.shape[1] // 2
            cell_sums, gram_features = kept[:, :width], kept[:, width:]
            low_rest = [jnp.where(clear, *jnp.split(part, 2, axis=1)) for part in (cell_low, cell_rest)]
            cell_state = low_rest[0].astype(jnp.float32) + low_rest[1].astype(jnp.float32)
        cell_state = (
            cell_state
            * cell_sums
            / (jnp.dot(gram_features, cell_state, precision=lax.Precision.HIGHEST) + EPSILON)
        )
        if not last:
            pair = jnp.concatenate(split_low(cell_state), axis=0)
            pair = jnp.concatenate(in_order(1, pair, flip(pair, 1)), axis=1)
            cell_low, cell_rest = pair[:rank], pair[rank:]
            mine = lax.dynamic_slice_in_dim(pair, (me % half) * cells, cells, 1).astype(jnp.float32)
            cell_state = mine[:rank] + mine[rank:]

    def own(first, width):
        return jnp.where(side == 0, factors[:, first : first + width], factors[:, first + width : first + 2 * width])

    return cell_state, own(0, gene_width), own(2 * gene_width, peak_width)


def layout(bits):
    size = 1 << len(bits)
    return [
        sum(bit for i, bit in enumerate(bits) if position >> (len(bits) - 1 - i) & 1)
        for position in range(size)
    ]


def turned(bits, by):
    return bits[by:] + bits[:by]


def across(left, right):
    return lax.dot_general(left, right, (((1,), (1,)), ((), ())), preferred_element_type=jnp.float32)


def exact(left, right):
    return lax.dot_general(
        left,
        right,
        (((1,), (0,)), ((), ())),
        precision=lax.Precision.HIGHEST,
        preferred_element_type=jnp.float32,
    )


def halved(value):
    high = value.astype(jnp.bfloat16)
    return high, (value - high.astype(jnp.float32)).astype(jnp.bfloat16)


def struct(*shape, dtype=jnp.float32):
    return jax.ShapeDtypeStruct(shape, dtype)


def gram_of(high, rest):
    pair = jnp.concatenate([high, rest], axis=0)
    squares = across(pair, pair)
    rank = high.shape[0]
    return (squares[:rank, :rank] + squares[rank:, rank:]) + (squares[:rank, rank:] + squares[rank:, :rank])


def parcels_kernel(spot, rna_0, rna_1, atac_0, atac_1, cell, gene, peak, *refs):
    links, out, copied, slots, sems = refs[:4], refs[4], refs[5:9], refs[9], refs[10]

    copies = [pltpu.make_async_copy(link, to, sems.at[i]) for i, (link, to) in enumerate(zip(links, copied))]

    @pl.when(pl.program_id(0) == 0)
    def _():
        for copy in copies:
            copy.start()

    rank = cell.shape[0]
    cells = rna_0.shape[0]
    gene_width, peak_width = gene.shape[1], peak.shape[1]
    width = gene_width + peak_width
    cell_pair = jnp.concatenate(halved(cell[...]), axis=1)
    gene_low = gene[...].astype(jnp.bfloat16)
    peak_low = peak[...].astype(jnp.bfloat16)
    part = rank // 4
    for j in range(out.shape[0]):
        at = 0
        for source, size in ((rna_0, gene_width), (rna_1, gene_width), (atac_0, peak_width), (atac_1, peak_width)):
            out[j, 0:cells, at : at + size] = source[:, j * size : (j + 1) * size]
            at += size
        out[j, 0:cells, at:] = cell_pair
        for s in range(2):
            row = (2 * (j % 2) + s) * part
            out[j, cells:, s * width : s * width + gene_width] = gene_low[row : row + part]
            out[j, cells:, s * width + gene_width : (s + 1) * width] = peak_low[row : row + part]

    @pl.when(pl.program_id(0) == 0)
    def _():
        for copy in copies:
            copy.wait()
        link_gene, link_peak, link_weight, link_count = copied
        count = link_gene.shape[0]
        lane = lax.broadcasted_iota(jnp.int32, slots.shape, 1) - spot[1] * count
        row = lax.broadcasted_iota(jnp.int32, slots.shape, 0)
        value = jnp.zeros(slots.shape, jnp.float32)
        for s in range(count):
            weight = jnp.where(s < link_count[0], link_weight[s], 0)
            for r, entry in enumerate((link_gene[s], link_peak[s], weight)):
                value = jnp.where((lane == s) & (row == r), entry.astype(jnp.float32), value)
        slots[...] = value.astype(jnp.bfloat16)

    for j in range(out.shape[0]):
        out[j, cells:, 2 * width :] = slots[...]


def encode(group):
    least = jnp.min(group, axis=1, keepdims=True)
    spread = jnp.max(group, axis=1, keepdims=True) - least
    per = jnp.where(spread > 0.0, CODES / spread, 0.0)
    code = jnp.minimum(jnp.floor((group - least) * per + 0.5), CODES) - (CODES + 1) / 2
    return code.astype(jnp.int32).astype(jnp.int16), least, spread / CODES


def decode(code, least, step):
    return least + (code.astype(jnp.int32).astype(jnp.float32) + (CODES + 1) / 2) * step


def codes_kernel(gene, peak, codes, bounds):
    rank, width = codes.shape
    gene_width = gene.shape[1]
    least, step = [], []
    for b in range(width // BLOCK):
        ref, at = (gene, b * BLOCK) if b * BLOCK < gene_width else (peak, b * BLOCK - gene_width)
        code, low, per = encode(ref[:, at : at + BLOCK])
        codes[:, b * BLOCK : (b + 1) * BLOCK] = code
        least.append(low)
        step.append(per)
    pad = jnp.zeros((rank, 2 * rank - 2 * len(least)), jnp.float32)
    columns = jnp.concatenate([*least, *step, pad], axis=1)
    square = jnp.concatenate([columns, jnp.zeros_like(columns)], axis=0)
    bounds[...] = square.T[: bounds.shape[0]]


def table_kernel(received_slots, bounds, out):
    above = bounds.shape[0]
    out[:above] = bounds[...]
    slots = sum(received_slots[j].astype(jnp.float32) for j in range(received_slots.shape[0]))

    def hot(row, size, value):
        ids = lax.broadcasted_iota(jnp.int32, (size, slots.shape[1]), 0).astype(jnp.float32)
        return jnp.where(slots[row : row + 1] == ids, value, 0.0).astype(jnp.bfloat16)

    out[above:] = across(hot(0, out.shape[0] - above, slots[2:3]), hot(1, out.shape[1], 1.0))


def twins_kernel(spot, gene, peak, codes, beside, out):
    gene_width, peak_width = gene.shape[1], peak.shape[1]
    groups = (gene_width + peak_width) // BLOCK
    lanes = beside.shape[1]
    above = -(-2 * groups // 8) * 8
    square = jnp.concatenate([beside[:above], jnp.zeros((lanes - above, lanes), jnp.float32)], axis=0)
    bounds = square.T[: gene.shape[0]]
    at = 0
    first = spot[0] == 0
    for ref, start in ((gene, 0), (peak, gene_width)):
        size = ref.shape[1]
        for b in range(size // BLOCK):
            g = start // BLOCK + b
            mine = ref[:, b * BLOCK : (b + 1) * BLOCK]
            code = codes[:, g * BLOCK : (g + 1) * BLOCK]
            other = decode(code, bounds[:, g : g + 1], bounds[:, groups + g : groups + g + 1])
            out[:, at + b * BLOCK : at + (b + 1) * BLOCK] = jnp.where(first, mine, other)
            out[:, at + size + b * BLOCK : at + size + (b + 1) * BLOCK] = jnp.where(first, other, mine)
        at += 2 * size


def in_hbm(value):
    return pltpu.with_memory_space_constraint(value, pltpu.HBM)


def parcels(spot, rna_counts, atac_counts, cell_factor, gene_factor, peak_factor, links, half):
    cells = rna_counts.shape[0]
    rank = cell_factor.shape[0]
    gene_width, peak_width = gene_factor.shape[1], peak_factor.shape[1]
    rows, lanes = cells + rank // 4, 2 * (gene_width + peak_width) + 2 * rank
    each = 4
    steps = half // each

    def columns(width, side):
        return pl.BlockSpec((cells, each * width), lambda i: (0, i + side * steps))

    def whole(array):
        return pl.BlockSpec(array.shape, lambda i: (0, 0))

    return pl.pallas_call(
        parcels_kernel,
        grid=(steps,),
        in_specs=[SMEM, columns(gene_width, 0), columns(gene_width, 1), columns(peak_width, 0), columns(peak_width, 1)]
        + [whole(a) for a in (cell_factor, gene_factor, peak_factor)]
        + [pl.BlockSpec(memory_space=pl.ANY)] * 4,
        out_specs=pl.BlockSpec((each, rows, lanes), lambda i: (i, 0, 0)),
        out_shape=struct(half, rows, lanes, dtype=jnp.bfloat16),
        scratch_shapes=[pltpu.SMEM(link.shape, jnp.int32) for link in links]
        + [pltpu.VMEM((rank // 4, 2 * rank), jnp.bfloat16), pltpu.SemaphoreType.DMA((4,))],
        compiler_params=PARAMS,
    )(
        spot,
        *(in_hbm(a) for a in (rna_counts, rna_counts, atac_counts, atac_counts, cell_factor, gene_factor, peak_factor)),
        *(in_hbm(a) for a in links[:-1]),
        links[-1],
    )


def first_sums_kernel(order, received, sums, gram, state):
    rank, features = sums.shape
    cells = received.shape[1] - rank // 4
    high = jnp.concatenate([received[j, 0:cells, features : features + rank] for j in order], axis=1)
    rest = jnp.concatenate([received[j, 0:cells, features + rank :] for j in order], axis=1)
    counts = jnp.concatenate([received[j, 0:cells, 0:features] for j in order], axis=0)
    sums[...] = jnp.dot(high, counts, preferred_element_type=jnp.float32)
    gram[...] = gram_of(high, rest)
    state[...] = high.astype(jnp.float32) + rest.astype(jnp.float32)


def digits(values):
    top = jnp.maximum(jnp.max(values, axis=1, keepdims=True), TINY)
    power = jnp.floor(jnp.log2(top)) + 1.0
    scaled = values * jnp.exp2(-power) * DIGIT
    high = jnp.minimum(jnp.floor(scaled), DIGIT - 1)
    low = jnp.clip(jnp.floor((scaled - high) * DIGIT), 0.0, DIGIT - 1)
    return [high, low, power]


def from_digits(high, low, power):
    return (high + low / DIGIT) / DIGIT * jnp.exp2(power)


def finish_sums(sums_value, gram_value, sums, message):
    rank, features = sums_value.shape
    least, top = [], []
    for b in range(features // BLOCK):
        group = sums_value[:, b * BLOCK : (b + 1) * BLOCK]
        sums[:, b * BLOCK : (b + 1) * BLOCK] = group
        code, low, per = encode(group)
        message[:, b * BLOCK : (b + 1) * BLOCK] = code
        least.append(low)
        top.append(low + per * CODES)
    beside = digits(gram_value) + digits(jnp.concatenate(least + top, axis=1))
    size = sum(part.shape[1] for part in beside)
    beside.append(jnp.zeros((rank, message.shape[1] - features - size), jnp.float32))
    message[:, features:] = jnp.concatenate(beside, axis=1).astype(jnp.int32).astype(jnp.int16)


def read_beside(message, features, rank):
    groups = features // BLOCK
    beside = message[:, features:].astype(jnp.int32).astype(jnp.float32)
    parts, at = [], 0
    for size in (rank, rank, 1, 2 * groups, 2 * groups, 1):
        parts.append(beside[:, at : at + size])
        at += size
    return from_digits(*parts[:3]), from_digits(*parts[3:])


def first_links_kernel(
    link_scale, widths, spot, mine, other, aside, aside_other, sums_in, gram, sums, message, table, sem, table_smem
):
    half = mine.shape[0]
    rank, features = sums_in.shape
    gene_width, peak_width = widths
    gene_blocks, peak_blocks = gene_width // BLOCK, peak_width // BLOCK
    width = gene_width + peak_width
    above = aside.shape[0] - table.shape[0]
    table[...] = aside[above:] + aside_other[above:]
    copy = pltpu.make_async_copy(table, table_smem, sem)
    copy.start()
    copy.wait()
    side, place, core = spot[0], spot[1], spot[2]
    total = [None] * (features // BLOCK)

    def add(target, weight, block):
        term = weight * block
        total[target] = term if total[target] is None else total[target] + term

    for j in range(half):
        blocks = []
        for b in range(width // BLOCK):
            pieces = [
                ref[j, :, s * width + b * BLOCK : s * width + (b + 1) * BLOCK] for ref in (mine, other) for s in range(2)
            ]
            blocks.append(jnp.concatenate(pieces, axis=0).astype(jnp.float32))
        for b in range(gene_blocks):
            row = (side * half + j) * gene_blocks + b
            for u in range(2 * peak_blocks):
                column = (place + u // peak_blocks * half) * peak_blocks + u % peak_blocks
                add(2 * gene_blocks + u, table_smem[row, column], blocks[b])
        for b in range(peak_blocks):
            column = (side * half + j) * peak_blocks + b
            for t in range(2 * gene_blocks):
                row = (place + t // gene_blocks * half) * gene_blocks + t % gene_blocks
                add(t, table_smem[row, column], blocks[gene_blocks + b])
    links = jnp.concatenate(total, axis=1)
    ahead, behind = links[: rank // 2], links[rank // 2 :]
    first = core == 0
    links = jnp.concatenate([jnp.where(first, ahead, behind), jnp.where(first, behind, ahead)], axis=0)
    finish_sums(sums_in[...] + link_scale * links, gram[...], sums, message)


def gram_rows(gram, lanes):
    rank = gram.shape[0]
    rows = rank * rank // lanes
    return jnp.concatenate([gram[b * rows : (b + 1) * rows] for b in range(rank // rows)], axis=1)


def gram_back(rows_value, rank):
    return jnp.concatenate(
        [rows_value[:, b * rank : (b + 1) * rank] for b in range(rows_value.shape[1] // rank)], axis=0
    )


def step_kernel(link_bit, gene_bit, spot, totals, totals_got, staying, staying_got, *refs):
    if gene_bit:
        genes, genes_got, *refs = refs
    received, totals_out, *outs = refs
    totals_out[...] = totals[...] + totals_got[...]
    to_gene = staying[...] + staying_got[...]
    if gene_bit:
        genes_out, *outs = outs
        width = genes.shape[1]
        clear = (spot[1] // gene_bit) % 2 == 0
        left, right = genes[...].astype(jnp.float32), genes_got[...].astype(jnp.float32)
        genes_out[:, :width] = jnp.where(clear, left, right).astype(jnp.bfloat16)
        genes_out[:, width:] = jnp.where(clear, right, left).astype(jnp.bfloat16)
    if link_bit:
        clear = (spot[1] // link_bit) % 2 == 0
        width = to_gene.shape[1] // 2
        left, right = to_gene[:, :width], to_gene[:, width:]
        outs[0][...] = jnp.where(clear, left, right)
        outs[1][...] = jnp.where(clear, right, left)
    else:
        outs[0][...] = to_gene


def step(spot, received, link_bit, gene_bit, totals, staying, genes=None):
    rank, width = staying[0].shape
    outs = [struct(*totals[0].shape)]
    if gene_bit:
        outs += [struct(rank, 2 * genes[0].shape[1], dtype=jnp.bfloat16)]
    outs += [struct(rank, width // 2)] * 2 if link_bit else [struct(rank, width)]
    values = [*totals, *staying, *(genes if gene_bit else ()), received]
    return pl.pallas_call(
        functools.partial(step_kernel, link_bit, gene_bit),
        in_specs=[SMEM] + [VMEM] * len(values),
        out_specs=[VMEM] * len(outs),
        out_shape=outs,
        compiler_params=PARAMS,
    )(spot, *values)


def next_sums_kernel(
    link_scale, widths, orders, spot, table, mine, other, state, received, to_gene, genes_mine, genes_other, *refs
):
    sums, message, gram, state_out, own = refs
    half = received.shape[0]
    rank, features = sums.shape
    cells = own.shape[1]
    gene_width, peak_width = widths
    gene_blocks, peak_blocks = gene_width // BLOCK, peak_width // BLOCK
    side, place, core = spot[0], spot[1], spot[2]
    first = core == 0
    old = state[...]
    left, right = mine[:rank], other[:rank]
    products = jnp.concatenate([jnp.where(first, left, right), jnp.where(first, right, left)], axis=1)
    new = old * products / (exact(gram_back(mine[rank:], rank), old) + EPSILON)
    state_out[...] = new
    mine_now = new[:, :cells]
    for position in range(1, half):
        at = position * cells
        mine_now = jnp.where(place == orders[0][position], new[:, at : at + cells], mine_now)
    own[...] = mine_now
    high, rest = halved(new)
    mine_low, other_low = genes_mine[...].astype(jnp.float32), genes_other[...].astype(jnp.float32)
    genes = jnp.concatenate(
        [jnp.where(first, mine_low, other_low), jnp.where(first, other_low, mine_low)], axis=1
    )
    total = [None] * (2 * peak_blocks)
    for position, j in enumerate(orders[1]):
        for b in range(gene_blocks):
            at = (position * gene_blocks + b) * BLOCK
            block = genes[:, at : at + BLOCK]
            row = (side * half + j) * gene_blocks + b
            for u in range(2 * peak_blocks):
                column = (place + u // peak_blocks * half) * peak_blocks + u % peak_blocks
                term = table[row, column] * block
                total[u] = term if total[u] is None else total[u] + term
    gene_links = to_gene[...]
    nothing = jnp.zeros_like(gene_links)
    links = jnp.concatenate(
        [jnp.where(side == 0, gene_links, nothing), jnp.where(side == 0, nothing, gene_links), *total], axis=1
    )
    counts = jnp.concatenate([received[j, 0:cells, 0:features] for j in orders[0]], axis=0)
    products = jnp.dot(high, counts, preferred_element_type=jnp.float32)
    gram[...] = gram_of(high, rest)
    finish_sums(products + link_scale * links, gram[...], sums, message)


def update_kernel(last, widths, orders, spot, table, sums, gram_mine, other, factors, received, *outs):
    half = received.shape[0]
    rank, features = sums.shape
    cells = received.shape[1] - rank // 4
    gene_width, peak_width = widths
    gene_blocks, peak_blocks = gene_width // BLOCK, peak_width // BLOCK
    side, place, core = spot[0], spot[1], spot[2]
    first = core == 0
    gram_other, bounds = read_beside(other, features, rank)
    gram = gram_mine[...] + gram_other
    old = factors[...]
    below = exact(gram, old) + EPSILON
    groups = features // BLOCK
    whole = []
    for b in range(groups):
        code = other[:, b * BLOCK : (b + 1) * BLOCK]
        least = bounds[:, b : b + 1]
        step = (bounds[:, groups + b : groups + b + 1] - least) / CODES
        whole.append(sums[:, b * BLOCK : (b + 1) * BLOCK] + decode(code, least, step))
    whole = jnp.concatenate(whole, axis=1)
    new = old * whole / below
    low = new.astype(jnp.bfloat16)
    cell_sums = jnp.concatenate([across(low, received[j, 0:cells, 0:features]) for j in orders[0]], axis=1)
    gram_features = across(low, low)
    kept, sent, *outs = outs
    split = half // 2 * cells
    left, right = cell_sums[:, :split], cell_sums[:, split:]
    for ref, value in ((kept, jnp.where(first, left, right)), (sent, jnp.where(first, right, left))):
        ref[:rank] = value
        ref[rank:] = gram_rows(gram_features, split)

    def own(at, width):
        return jnp.where(side == 0, new[:, at : at + width], new[:, at + width : at + 2 * width])

    if last:
        gene_out, peak_out = outs
        gene_out[...] = own(0, gene_width)
        peak_out[...] = own(2 * gene_width, peak_width)
        return
    factors_out, links_kept, links_sent, gene_low = outs
    factors_out[...] = new
    gene_low[...] = own(0, gene_width).astype(jnp.bfloat16)
    peaks = low[:, 2 * gene_width :].astype(jnp.float32)
    peaks = [peaks[:, u * BLOCK : (u + 1) * BLOCK] for u in range(2 * peak_blocks)]
    for position in range(half // 2):
        pair = []
        for j in (orders[1][position], orders[1][position + half // 2]):
            parts = []
            for b in range(gene_blocks):
                row = (side * half + j) * gene_blocks + b
                part = None
                for u, block in enumerate(peaks):
                    column = (place + u // peak_blocks * half) * peak_blocks + u % peak_blocks
                    term = table[row, column] * block
                    part = term if part is None else part + term
                parts.append(part)
            pair.append(jnp.concatenate(parts, axis=1))
        at = position * gene_width
        links_kept[:, at : at + gene_width] = jnp.where(first, *pair)
        links_sent[:, at : at + gene_width] = jnp.where(first, pair[1], pair[0])


def last_cells_kernel(spot, mine, other, old, out):
    rank, cells = out.shape
    totals = mine[:rank] + other[:rank]
    gram = mine[rank:] + other[rank:]
    lanes = totals.shape[1]
    rows = rank * rank // (4 * lanes)
    gram = jnp.concatenate(
        [gram[i * rows : (i + 1) * rows, b * rank : (b + 1) * rank] for i in range(4) for b in range(lanes // rank)],
        axis=0,
    )
    own = totals[:, :cells]
    for position in range(1, lanes // cells):
        own = jnp.where(spot[3] == position, totals[:, position * cells : (position + 1) * cells], own)
    out[...] = old[...] * own / (exact(gram, old[...]) + EPSILON)


def shards_blocks(
    rna_counts,
    atac_counts,
    cell_factor,
    gene_factor,
    peak_factor,
    link_gene,
    link_peak,
    link_weight,
    link_count,
):
    count = lax.axis_size(AXIS)
    half = count // 2
    me = lax.axis_index(AXIS)
    side, place, core = me // half, me % half, me % 2
    chip_bits = bits_below(half)[1:]
    cell_bits, link_bits, gene_bits = (turned(chip_bits, i % len(chip_bits)) for i in range(3))
    tail = sum(
        jnp.where((me & bit) != 0, 1 << i, 0) for i, bit in enumerate(reversed(cell_bits[2:]))
    )
    spot = jnp.stack([side, place, core, tail]).astype(jnp.int32)
    rank, cells = cell_factor.shape
    gene_width, peak_width = gene_factor.shape[1], peak_factor.shape[1]
    widths = (gene_width, peak_width)
    width = gene_width + peak_width
    features = 2 * width
    link_scale = cells * count / 4.0
    table_shape = (rna_counts.shape[1] // BLOCK, atac_counts.shape[1] // BLOCK)
    cell_order = layout([1] + cell_bits)
    link_order = layout([1] + link_bits)
    gene_order = layout([1] + gene_bits[::-1])

    links = (link_gene, link_peak, link_weight, link_count)
    sent = parcels(spot, rna_counts, atac_counts, cell_factor, gene_factor, peak_factor, links, half)
    halves = [list(range(half)), list(range(half, count))]
    received = lax.all_to_all(sent, AXIS, 0, 0, axis_index_groups=halves, tiled=True)
    rows_other = flip(received[:, cells:, :features], 1)
    received_here = pltpu.with_memory_space_constraint(received, pltpu.VMEM)
    above = -(-2 * width // BLOCK // 8) * 8
    codes, bounds = pl.pallas_call(
        codes_kernel,
        in_specs=[VMEM] * 2,
        out_specs=[VMEM] * 2,
        out_shape=(struct(rank, width, dtype=jnp.int16), struct(above, 2 * rank)),
        compiler_params=PARAMS,
    )(gene_factor, peak_factor)
    rows = rank // 4
    aside = pl.pallas_call(
        table_kernel,
        grid=(1,),
        in_specs=[
            pl.BlockSpec((half, rows, 2 * rank), lambda i: (0, cells // rows, features // (2 * rank))),
            VMEM,
        ],
        out_specs=VMEM,
        out_shape=struct(above + table_shape[0], table_shape[1]),
        compiler_params=PARAMS,
    )(received_here, bounds)
    aside_other = flip(aside, half)
    sums_shapes = (struct(rank, features), struct(rank, features + 4 * rank, dtype=jnp.int16))
    sums, gram, state = pl.pallas_call(
        functools.partial(first_sums_kernel, cell_order),
        in_specs=[VMEM],
        out_specs=[VMEM] * 3,
        out_shape=(struct(rank, features), struct(rank, rank), struct(rank, half * cells)),
        compiler_params=PARAMS,
    )(received_here)
    codes, sums, aside_other = lax.optimization_barrier((codes, sums, aside_other))
    codes_other = flip(codes, half)
    sums, message, link_table = pl.pallas_call(
        functools.partial(first_links_kernel, link_scale, widths),
        grid=(1,),
        in_specs=[
            SMEM,
            pl.BlockSpec((half, rows, features + 2 * rank), lambda i: (0, cells // rows, 0)),
            VMEM,
            VMEM,
            VMEM,
            VMEM,
            VMEM,
        ],
        out_specs=[VMEM] * 3,
        out_shape=(*sums_shapes, struct(*table_shape)),
        scratch_shapes=[pltpu.SemaphoreType.DMA, pltpu.SMEM(table_shape, jnp.float32)],
        compiler_params=PARAMS,
    )(spot, received_here, rows_other, aside, aside_other, sums, gram)

    message, codes_other = lax.optimization_barrier((message, codes_other))
    factors = pl.pallas_call(
        twins_kernel,
        in_specs=[SMEM] + [VMEM] * 4,
        out_specs=VMEM,
        out_shape=struct(rank, features),
        compiler_params=PARAMS,
    )(spot, gene_factor, peak_factor, codes_other, aside_other)

    split = half // 2 * cells
    for sweep_index in range(ROUNDS):
        last = sweep_index == ROUNDS - 1
        other = flip(message, half)
        outs = [struct(rank + rank * rank // split, split)] * 2
        if last:
            outs += [struct(rank, gene_width), struct(rank, peak_width)]
        else:
            outs += [struct(rank, features)] + [struct(rank, half // 2 * gene_width)] * 2
            outs += [struct(rank, gene_width, dtype=jnp.bfloat16)]
        kept, sent, *outs = pl.pallas_call(
            functools.partial(update_kernel, last, widths, (cell_order, link_order)),
            in_specs=[SMEM] * 2 + [VMEM] * 5,
            out_specs=[VMEM] * len(outs),
            out_shape=outs,
            compiler_params=PARAMS,
        )(spot, link_table, sums, gram, other, factors, received_here)
        if last:
            gene_out, peak_out = outs
            totals = kept + flip(sent, 1)
            first, second = cell_bits[:2]
            quarters = jnp.split(totals[:rank], 4, axis=1)
            gram_part = jnp.concatenate(jnp.split(totals[rank:], 4, axis=1), axis=0)
            is_first, is_second = (me & first) != 0, (me & second) != 0

            def quarter(flip_first, flip_second):
                low, high = (
                    jnp.where(is_second ^ flip_second, quarters[2 * i + 1], quarters[2 * i]) for i in range(2)
                )
                return jnp.concatenate([jnp.where(is_first ^ flip_first, high, low), gram_part], axis=0)

            got = [
                flip(quarter(*which), bit)
                for which, bit in (((True, False), first), ((False, True), second), ((True, True), first | second))
            ]
            totals = quarter(False, False) + (got[0] + got[1] + got[2])
            for bit in cell_bits[2:-1]:
                totals = totals + flip(totals, bit)
            cell_out = pl.pallas_call(
                last_cells_kernel,
                in_specs=[SMEM] + [VMEM] * 3,
                out_specs=VMEM,
                out_shape=struct(rank, cells),
                compiler_params=PARAMS,
            )(spot, totals, flip(totals, cell_bits[-1]), own_cells)
            return cell_out, gene_out, peak_out
        factors, links_kept, links_sent, genes = outs
        totals, staying, leaving = step(
            spot, received_here, link_bits[0], 0, (kept, flip(sent, 1)), (links_kept, flip(links_sent, 1))
        )
        for i, bits in enumerate(zip(cell_bits, link_bits, gene_bits)):
            going = lax.optimization_barrier((totals, leaving, genes))
            got = lax.optimization_barrier(tuple(flip(value, bit) for value, bit in zip(going, bits)))
            next_bit = link_bits[i + 1] if i + 1 < len(link_bits) else 0
            totals, genes, staying, *leaving = step(
                spot, received_here, next_bit, bits[2], (totals, got[0]), (staying, got[1]), (genes, got[2])
            )
            leaving = leaving[0] if next_bit else None
        to_gene = staying
        sums, message, gram, state, own_cells = pl.pallas_call(
            functools.partial(next_sums_kernel, link_scale, widths, (cell_order, gene_order)),
            in_specs=[SMEM] * 2 + [VMEM] * 7,
            out_specs=[VMEM] * 5,
            out_shape=(*sums_shapes, struct(rank, rank), struct(rank, half * cells), struct(rank, cells)),
            compiler_params=PARAMS,
        )(spot, link_table, totals, flip(totals, 1), state, received_here, to_gene, genes, flip(genes, 1))


def shards(rna_counts, atac_counts, cell_factor, gene_factor, peak_factor, link_gene, *links):
    half = lax.axis_size(AXIS) // 2
    rank, cells = cell_factor.shape
    gene_width, peak_width = gene_factor.shape[1], peak_factor.shape[1]
    features = 2 * (gene_width + peak_width)
    in_blocks = (
        half % 16 == 0
        and rank == cells
        and 2 * rank == BLOCK
        and gene_width % BLOCK == 0
        and peak_width % BLOCK == 0
        and 4 * (features // BLOCK) + 2 <= 2 * rank
        and half * link_gene.shape[0] <= 2 * rank
        and rank % 64 == 0
        and atac_counts.shape[1] // BLOCK == 2 * rank
        and max(rna_counts.shape[1], atac_counts.shape[1]) // BLOCK <= 256
    )
    run = shards_blocks if in_blocks else shards_any
    return run(rna_counts, atac_counts, cell_factor, gene_factor, peak_factor, link_gene, *links)


def solution(mesh):
    columns = P(None, ("groups", "cells"))
    slots = P(("groups", "cells"))
    in_specs = (P(("groups", "cells"), None),) * 2 + (columns,) * 3 + (slots,) * 4
    return jax.shard_map(
        shards, mesh=mesh, in_specs=in_specs, out_specs=(columns,) * 3, check_vma=False
    )
```

```python
import functools

import jax
import jax.numpy as jnp
from jax import lax
from jax.experimental import pallas as pl
from jax.experimental.pallas import tpu as pltpu
from jax.sharding import PartitionSpec as P

BLOCK = 128
ROUNDS = 2
EPSILON = 1e-06
CODES = 65535.0
DIGIT = 32768.0
UNITS = 16384.0
TINY = 1e-30
AXIS = "cells"
PARAMS = pltpu.CompilerParams(vmem_limit_bytes=14 * 1024 * 1024)
SMEM = pl.BlockSpec(memory_space=pltpu.SMEM)
VMEM = pl.BlockSpec(memory_space=pltpu.VMEM)


def flip(value, bit):
    count = lax.axis_size(AXIS)
    return lax.ppermute(value, AXIS, [(i, i ^ bit) for i in range(count)])


def in_order(bit, mine, other):
    mine_first = (lax.axis_index(AXIS) & bit) == 0
    return jnp.where(mine_first, mine, other), jnp.where(mine_first, other, mine)


def bits_below(size):
    return [1 << b for b in range(size.bit_length() - 1)]


def own_table(link_gene, link_peak, link_weight, link_count, gene_blocks, peak_blocks):
    slot_ids = jnp.arange(link_gene.shape[0], dtype=jnp.int32)
    live_weight = jnp.where(slot_ids < link_count[0], link_weight, 0).astype(jnp.float32)
    gene_hot = (link_gene[:, None] == jnp.arange(gene_blocks, dtype=jnp.int32)[None, :]).astype(
        jnp.float32
    )
    peak_hot = (link_peak[:, None] == jnp.arange(peak_blocks, dtype=jnp.int32)[None, :]).astype(
        jnp.float32
    )
    return jnp.dot((gene_hot * live_weight[:, None]).T, peak_hot, precision=lax.Precision.HIGHEST)


def split_low(value):
    high = lax.reduce_precision(value, exponent_bits=8, mantissa_bits=7)
    return high.astype(jnp.bfloat16), (value - high).astype(jnp.bfloat16)


def gather_half(value, half):
    for bit in bits_below(half):
        value = jnp.concatenate(in_order(bit, value, flip(value, bit)), axis=1)
    return value


def scatter_half(value, half):
    for bit in reversed(bits_below(half)):
        low, high = jnp.split(value, 2, axis=1)
        clear = (lax.axis_index(AXIS) & bit) == 0
        value = jnp.where(clear, low, high) + flip(jnp.where(clear, high, low), bit)
    return value


def weigh(weights, source):
    rank = source.shape[0]
    blocks = source.astype(jnp.float32).reshape(rank, weights.shape[1], BLOCK)
    result = jnp.einsum("ksc,ts->ktc", blocks, weights, precision=lax.Precision.HIGHEST)
    return result.reshape(rank, weights.shape[0] * BLOCK)


def coupling(link_table, factors, widths):
    gene_width, peak_width = widths
    half = lax.axis_size(AXIS) // 2
    me = lax.axis_index(AXIS)
    side, place = me // half, me % half
    low = factors.astype(jnp.bfloat16)
    genes, peaks = low[:, : 2 * gene_width], low[:, 2 * gene_width :]
    own_gene = jnp.where(side == 0, genes[:, :gene_width], genes[:, gene_width:])
    side_blocks = half * gene_width // BLOCK
    peak_blocks = peak_width // BLOCK
    side_rows = lax.dynamic_slice_in_dim(link_table, side * side_blocks, side_blocks, 0)
    weights = jnp.concatenate(
        [
            lax.dynamic_slice_in_dim(side_rows, (place + s * half) * peak_blocks, peak_blocks, 1)
            for s in range(2)
        ],
        axis=1,
    )
    to_gene = scatter_half(weigh(weights, peaks), half)
    to_peak = weigh(weights.T, gather_half(own_gene, half))
    nothing = jnp.zeros_like(to_gene)
    return jnp.concatenate([*(jnp.where(side == s, to_gene, nothing) for s in range(2)), to_peak], axis=1)


def shards_any(
    rna_counts,
    atac_counts,
    cell_factor,
    gene_factor,
    peak_factor,
    link_gene,
    link_peak,
    link_weight,
    link_count,
):
    count = lax.axis_size(AXIS)
    half = count // 2
    me = lax.axis_index(AXIS)
    side = me // half
    rank, cells = cell_factor.shape
    gene_width, peak_width = gene_factor.shape[1], peak_factor.shape[1]
    features = 2 * (gene_width + peak_width)
    link_scale = cells * count / 4.0

    link_table = own_table(
        link_gene,
        link_peak,
        link_weight,
        link_count,
        rna_counts.shape[1] // BLOCK,
        atac_counts.shape[1] // BLOCK,
    )
    for bit in bits_below(count):
        link_table = link_table + flip(link_table, bit)

    def by_place(counts, width):
        return counts.reshape(cells, 2, half, width).transpose(2, 0, 1, 3).reshape(half, cells, 2 * width)

    cell_pair = jnp.concatenate([part.T for part in split_low(cell_factor)], axis=1)
    parcels = jnp.concatenate(
        [
            by_place(rna_counts, gene_width),
            by_place(atac_counts, peak_width),
            jnp.broadcast_to(cell_pair[None], (half, cells, 2 * rank)),
        ],
        axis=2,
    )
    halves = [list(range(half)), list(range(half, count))]
    received = lax.all_to_all(parcels, AXIS, 0, 0, axis_index_groups=halves, tiled=True)
    received = received.reshape(half * cells, features + 2 * rank)
    counts, cell_pair = received[:, :features], received[:, features:]

    gene_pair = in_order(half, gene_factor, flip(gene_factor, half))
    peak_pair = in_order(half, peak_factor, flip(peak_factor, half))
    factors = jnp.concatenate([*gene_pair, *peak_pair], axis=1)
    cell_low, cell_rest = cell_pair[:, :rank].T, cell_pair[:, rank:].T
    cell_state = cell_factor

    for sweep_index in range(ROUNDS):
        links = link_scale * coupling(link_table, factors, (gene_width, peak_width))
        pair = jnp.concatenate([cell_low, cell_rest], axis=0)
        squares = lax.dot_general(
            pair, pair, (((1,), (1,)), ((), ())), preferred_element_type=jnp.float32
        )
        gram_cells = (
            squares[:rank, :rank] + squares[:rank, rank:] + squares[rank:, :rank] + squares[rank:, rank:]
        )
        sums = jnp.dot(cell_low, counts, preferred_element_type=jnp.float32) + links
        gram_cells = gram_cells + flip(gram_cells, half)
        sums = sums + flip(sums, half)
        factors = (
            factors
            * sums
            / (jnp.dot(gram_cells, factors, precision=lax.Precision.HIGHEST) + EPSILON)
        )
        low = factors.astype(jnp.bfloat16)
        gram_features = lax.dot_general(
            low, low, (((1,), (1,)), ((), ())), preferred_element_type=jnp.float32
        )
        cell_sums = lax.dot_general(
            low, counts, (((1,), (1,)), ((), ())), preferred_element_type=jnp.float32
        )
        last = sweep_index == ROUNDS - 1
        if last:
            for bit in reversed(bits_below(half)):
                left, right = jnp.split(cell_sums, 2, axis=1)
                clear = (me & bit) == 0
                sent = jnp.concatenate([jnp.where(clear, right, left), gram_features], axis=1)
                got = flip(sent, bit)
                kept = cell_sums.shape[1] // 2
                cell_sums = jnp.where(clear, left, right) + got[:, :kept]
                gram_features = gram_features + got[:, kept:]
        else:
            left, right = jnp.split(cell_sums, 2, axis=1)
            clear = (me & 1) == 0
            sent = jnp.concatenate([jnp.where(clear, right, left), gram_features], axis=1)
            kept = jnp.concatenate([jnp.where(clear, left, right), gram_features], axis=1)
            for bit in bits_below(half):
                kept = kept + flip(sent, bit)
                sent = kept
            width = cell_sums.shape[1] // 2
            cell_sums, gram_features = kept[:, :width], kept[:, width:]
            low_rest = [jnp.where(clear, *jnp.split(part, 2, axis=1)) for part in (cell_low, cell_rest)]
            cell_state = low_rest[0].astype(jnp.float32) + low_rest[1].astype(jnp.float32)
        cell_state = (
            cell_state
            * cell_sums
            / (jnp.dot(gram_features, cell_state, precision=lax.Precision.HIGHEST) + EPSILON)
        )
        if not last:
            pair = jnp.concatenate(split_low(cell_state), axis=0)
            pair = jnp.concatenate(in_order(1, pair, flip(pair, 1)), axis=1)
            cell_low, cell_rest = pair[:rank], pair[rank:]
            mine = lax.dynamic_slice_in_dim(pair, (me % half) * cells, cells, 1).astype(jnp.float32)
            cell_state = mine[:rank] + mine[rank:]

    def own(first, width):
        return jnp.where(side == 0, factors[:, first : first + width], factors[:, first + width : first + 2 * width])

    return cell_state, own(0, gene_width), own(2 * gene_width, peak_width)


def layout(bits):
    size = 1 << len(bits)
    return [
        sum(bit for i, bit in enumerate(bits) if position >> (len(bits) - 1 - i) & 1)
        for position in range(size)
    ]


def turned(bits, by):
    return bits[by:] + bits[:by]


def across(left, right):
    return lax.dot_general(left, right, (((1,), (1,)), ((), ())), preferred_element_type=jnp.float32)


def halved(value):
    high = value.astype(jnp.bfloat16)
    return high, (value - high.astype(jnp.float32)).astype(jnp.bfloat16)


def exact(left, right):
    left_high, left_low = halved(left)
    right_high, right_low = halved(right)
    return jnp.dot(
        jnp.concatenate([left_low, left_low, left_high, left_high], axis=1),
        jnp.concatenate([right_low, right_high, right_low, right_high], axis=0),
        preferred_element_type=jnp.float32,
    )


def struct(*shape, dtype=jnp.float32):
    return jax.ShapeDtypeStruct(shape, dtype)


def gram_of(high, rest):
    pair = jnp.concatenate([high, rest], axis=0)
    squares = across(pair, pair)
    rank = high.shape[0]
    return (squares[:rank, :rank] + squares[rank:, rank:]) + (squares[:rank, rank:] + squares[rank:, :rank])


def parcels_kernel(spot, rna_0, rna_1, atac_0, atac_1, cell, gene, peak, *refs):
    links, out, copied, slots, sems = refs[:4], refs[4], refs[5:9], refs[9], refs[10]

    copies = [pltpu.make_async_copy(link, to, sems.at[i]) for i, (link, to) in enumerate(zip(links, copied))]

    @pl.when(pl.program_id(0) == 0)
    def _():
        for copy in copies:
            copy.start()

    rank = cell.shape[0]
    cells = rna_0.shape[0]
    gene_width, peak_width = gene.shape[1], peak.shape[1]
    width = gene_width + peak_width
    cell_pair = jnp.concatenate(halved(cell[...]), axis=1)
    gene_low = gene[...].astype(jnp.bfloat16)
    peak_low = peak[...].astype(jnp.bfloat16)
    part = rank // 4
    each = rna_0.shape[1] // gene_width
    base = pl.program_id(0) * each
    for j in range(each):
        at = 0
        for source, size in ((rna_0, gene_width), (rna_1, gene_width), (atac_0, peak_width), (atac_1, peak_width)):
            out[base + j, 0:cells, at : at + size] = source[:, j * size : (j + 1) * size]
            at += size
        out[base + j, 0:cells, at:] = cell_pair
        for s in range(2):
            row = (2 * (j % 2) + s) * part
            out[base + j, cells:, s * width : s * width + gene_width] = gene_low[row : row + part]
            out[base + j, cells:, s * width + gene_width : (s + 1) * width] = peak_low[row : row + part]

    @pl.when(pl.program_id(0) == 0)
    def _():
        for copy in copies:
            copy.wait()
        link_gene, link_peak, link_weight, link_count = copied
        count = link_gene.shape[0]
        lane = lax.broadcasted_iota(jnp.int32, slots.shape, 1) - spot[1] * count
        row = lax.broadcasted_iota(jnp.int32, slots.shape, 0)
        value = jnp.zeros(slots.shape, jnp.float32)
        for s in range(count):
            weight = jnp.where(s < link_count[0], link_weight[s], 0)
            for r, entry in enumerate((link_gene[s], link_peak[s], weight)):
                value = jnp.where((lane == s) & (row == r), entry.astype(jnp.float32), value)
        slots[...] = value.astype(jnp.bfloat16)

    for j in range(each):
        out[base + j, cells:, 2 * width :] = slots[...]


def power_of(top):
    return jnp.floor(jnp.log2(jnp.maximum(top, TINY))) + 1.0


def encode(value):
    groups = [value[:, at : at + BLOCK] for at in range(0, value.shape[1], BLOCK)]
    least = [jnp.min(group, axis=1, keepdims=True) for group in groups]
    most = [jnp.max(group, axis=1, keepdims=True) for group in groups]
    power = power_of(functools.reduce(jnp.maximum, most))
    unit, per_unit = jnp.exp2(power) / UNITS, jnp.exp2(-power) * UNITS
    least = [jnp.floor(low * per_unit) for low in least]
    most = [jnp.ceil(high * per_unit) for high in most]
    codes = []
    for group, low, high in zip(groups, least, most):
        spread = (high - low) * unit
        per = jnp.where(spread > 0.0, CODES / spread, 0.0)
        code = jnp.clip(jnp.floor((group - low * unit) * per + 0.5), 0.0, CODES) - (CODES + 1) / 2
        codes.append(code.astype(jnp.int32).astype(jnp.int16))
    return codes, [*least, *most, power]


def decode(code, least, most, power):
    steps = code.astype(jnp.int32).astype(jnp.float32) + (CODES + 1) / 2
    return (least + steps * ((most - least) / CODES)) * (jnp.exp2(power) / UNITS)


def whole_numbers(columns, lanes):
    rows = columns[0].shape[0]
    size = sum(column.shape[1] for column in columns)
    filled = jnp.concatenate([*columns, jnp.zeros((rows, lanes - size), jnp.float32)], axis=1)
    return filled.astype(jnp.int32).astype(jnp.int16)


def codes_kernel(gene, peak, message):
    codes, columns = encode(jnp.concatenate([gene[...], peak[...]], axis=1))
    for b, code in enumerate(codes):
        message[:, b * BLOCK : (b + 1) * BLOCK] = code
    at = len(codes) * BLOCK
    message[:, at:] = whole_numbers(columns, message.shape[1] - at)


def table_kernel(received_slots, out):
    slots = sum(received_slots[j].astype(jnp.float32) for j in range(received_slots.shape[0]))

    def hot(row, size, value):
        ids = lax.broadcasted_iota(jnp.int32, (size, slots.shape[1]), 0).astype(jnp.float32)
        return jnp.where(slots[row : row + 1] == ids, value, 0.0).astype(jnp.bfloat16)

    out[...] = across(hot(0, out.shape[0], slots[2:3]), hot(1, out.shape[1], 1.0))


def twins_kernel(spot, gene, peak, got, out):
    width = gene.shape[1] + peak.shape[1]
    groups = width // BLOCK
    columns = got[:, width:].astype(jnp.int32).astype(jnp.float32)
    power = columns[:, 2 * groups : 2 * groups + 1]
    at = g = 0
    first = spot[0] == 0
    for ref in (gene, peak):
        size = ref.shape[1]
        for b in range(size // BLOCK):
            mine = ref[:, b * BLOCK : (b + 1) * BLOCK]
            other = decode(
                got[:, g * BLOCK : (g + 1) * BLOCK], columns[:, g : g + 1], columns[:, groups + g : groups + g + 1], power
            )
            out[:, at + b * BLOCK : at + (b + 1) * BLOCK] = jnp.where(first, mine, other)
            out[:, at + size + b * BLOCK : at + size + (b + 1) * BLOCK] = jnp.where(first, other, mine)
            g += 1
        at += 2 * size


def in_hbm(value):
    return pltpu.with_memory_space_constraint(value, pltpu.HBM)


def parcels(spot, rna_counts, atac_counts, cell_factor, gene_factor, peak_factor, links, half):
    cells = rna_counts.shape[0]
    rank = cell_factor.shape[0]
    gene_width, peak_width = gene_factor.shape[1], peak_factor.shape[1]
    rows, lanes = cells + rank // 4, 2 * (gene_width + peak_width) + 2 * rank
    each = 8
    steps = half // each

    def columns(width, side):
        return pl.BlockSpec((cells, each * width), lambda i: (0, i + side * steps))

    def whole(array):
        return pl.BlockSpec(array.shape, lambda i: (0, 0))

    return pl.pallas_call(
        parcels_kernel,
        grid=(steps,),
        in_specs=[SMEM, columns(gene_width, 0), columns(gene_width, 1), columns(peak_width, 0), columns(peak_width, 1)]
        + [whole(a) for a in (cell_factor, gene_factor, peak_factor)]
        + [pl.BlockSpec(memory_space=pl.ANY)] * 4,
        out_specs=VMEM,
        out_shape=struct(half, rows, lanes, dtype=jnp.bfloat16),
        scratch_shapes=[pltpu.SMEM(link.shape, jnp.int32) for link in links]
        + [pltpu.VMEM((rank // 4, 2 * rank), jnp.bfloat16), pltpu.SemaphoreType.DMA((4,))],
        compiler_params=PARAMS,
    )(
        spot,
        *(in_hbm(a) for a in (rna_counts, rna_counts, atac_counts, atac_counts, cell_factor, gene_factor, peak_factor)),
        *(in_hbm(a) for a in links[:-1]),
        links[-1],
    )


def first_sums_kernel(order, received, sums, gram, state):
    rank, features = sums.shape
    cells = received.shape[1] - rank // 4
    high = jnp.concatenate([received[j, 0:cells, features : features + rank] for j in order], axis=1)
    rest = jnp.concatenate([received[j, 0:cells, features + rank :] for j in order], axis=1)
    counts = jnp.concatenate([received[j, 0:cells, 0:features] for j in order], axis=0)
    sums[...] = jnp.dot(high, counts, preferred_element_type=jnp.float32)
    gram[...] = gram_of(high, rest)
    state[...] = high.astype(jnp.float32) + rest.astype(jnp.float32)


def by_index(rank):
    row = lax.broadcasted_iota(jnp.int32, (rank, rank), 0)
    return row, lax.broadcasted_iota(jnp.int32, (rank, rank), 1)


def finish_sums(sums_value, gram_value, sums, message):
    rank, features = sums_value.shape
    sums[...] = sums_value
    codes, columns = encode(sums_value)
    for b, code in enumerate(codes):
        message[:, b * BLOCK : (b + 1) * BLOCK] = code
    power = power_of(jnp.max(jnp.max(gram_value, axis=1, keepdims=True), axis=0, keepdims=True))
    scaled = gram_value * (jnp.exp2(-power) * DIGIT)
    high = jnp.minimum(jnp.floor(scaled), DIGIT - 1)
    low = jnp.clip(jnp.floor((scaled - high) * DIGIT), 0.0, DIGIT - 1)
    row, column = by_index(rank)
    diagonal = jnp.sum(jnp.where(row == column, low, 0.0), axis=1, keepdims=True)
    columns = [jnp.where(row <= column, high, low), diagonal, jnp.broadcast_to(power, (rank, 1)), *columns]
    message[:, features:] = whole_numbers(columns, message.shape[1] - features)


def read_message(message, features, rank):
    groups = features // BLOCK
    beside = message[:, features:].astype(jnp.int32).astype(jnp.float32)
    lanes = beside.shape[1]
    square = jnp.concatenate([beside, jnp.zeros((lanes - rank, lanes), jnp.float32)], axis=0).T
    upright, turned_over = beside[:, :rank], square[:rank, :rank]
    diagonal, power = beside[:, rank : rank + 1], beside[:, rank + 1 : rank + 2]
    row, column = by_index(rank)
    high = jnp.where(row <= column, upright, turned_over)
    low = jnp.where(row == column, diagonal, jnp.where(row < column, turned_over, upright))
    gram = (high + low / DIGIT) * (jnp.exp2(power) / DIGIT)
    at = rank + 2
    sums_power = beside[:, at + 2 * groups : at + 2 * groups + 1]
    blocks = [
        decode(
            message[:, b * BLOCK : (b + 1) * BLOCK],
            beside[:, at + b : at + b + 1],
            beside[:, at + groups + b : at + groups + b + 1],
            sums_power,
        )
        for b in range(groups)
    ]
    return gram, blocks


def first_links_kernel(
    link_scale, widths, spot, mine, other, half_table, half_table_other, sums_in, gram, sums, message, table, sem, table_smem
):
    half = mine.shape[0]
    rank, features = sums_in.shape
    gene_width, peak_width = widths
    gene_blocks, peak_blocks = gene_width // BLOCK, peak_width // BLOCK
    width = gene_width + peak_width
    table[...] = half_table[...] + half_table_other[...]
    copy = pltpu.make_async_copy(table, table_smem, sem)
    copy.start()
    copy.wait()
    side, place, core = spot[0], spot[1], spot[2]
    total = [None] * (features // BLOCK)

    def add(target, weight, block):
        term = weight * block
        total[target] = term if total[target] is None else total[target] + term

    for j in range(half):
        blocks = []
        for b in range(width // BLOCK):
            pieces = [
                ref[j, :, s * width + b * BLOCK : s * width + (b + 1) * BLOCK] for ref in (mine, other) for s in range(2)
            ]
            blocks.append(jnp.concatenate(pieces, axis=0).astype(jnp.float32))
        for b in range(gene_blocks):
            row = (side * half + j) * gene_blocks + b
            for u in range(2 * peak_blocks):
                column = (place + u // peak_blocks * half) * peak_blocks + u % peak_blocks
                add(2 * gene_blocks + u, table_smem[row, column], blocks[b])
        for b in range(peak_blocks):
            column = (side * half + j) * peak_blocks + b
            for t in range(2 * gene_blocks):
                row = (place + t // gene_blocks * half) * gene_blocks + t % gene_blocks
                add(t, table_smem[row, column], blocks[gene_blocks + b])
    links = jnp.concatenate(total, axis=1)
    ahead, behind = links[: rank // 2], links[rank // 2 :]
    first = core == 0
    links = jnp.concatenate([jnp.where(first, ahead, behind), jnp.where(first, behind, ahead)], axis=0)
    finish_sums(sums_in[...] + link_scale * links, gram[...], sums, message)


def gram_rows(gram, lanes):
    rank = gram.shape[0]
    rows = rank * rank // lanes
    return jnp.concatenate([gram[b * rows : (b + 1) * rows] for b in range(rank // rows)], axis=1)


def gram_back(rows_value, rank):
    return jnp.concatenate(
        [rows_value[:, b * rank : (b + 1) * rank] for b in range(rows_value.shape[1] // rank)], axis=0
    )


def step_kernel(link_bit, gene_bit, spot, totals, totals_got, staying, got, genes, received, totals_out, staying_out, *outs):
    totals_out[...] = totals[...] + totals_got[...]
    rank, width = staying.shape
    low = genes[...]
    if gene_bit:
        to_gene = staying[...] + (got[:, :width].astype(jnp.float32) + got[:, width : 2 * width].astype(jnp.float32))
        clear = (spot[1] // gene_bit) % 2 == 0
        mine, other = low.astype(jnp.float32), got[:, 2 * width :].astype(jnp.float32)
        low = jnp.concatenate([jnp.where(clear, mine, other), jnp.where(clear, other, mine)], axis=1)
        low = low.astype(jnp.bfloat16)
    else:
        to_gene = staying[...] + got[...]
    if link_bit:
        clear = (spot[1] // link_bit) % 2 == 0
        left, right = to_gene[:, : width // 2], to_gene[:, width // 2 :]
        staying_out[...] = jnp.where(clear, left, right)
        leaving = halved(jnp.where(clear, right, left))
        outs[0][...] = jnp.concatenate([*leaving, low], axis=1)
    else:
        staying_out[...] = to_gene
    outs[-1][...] = low


def step(spot, received, link_bit, gene_bit, totals, staying, genes):
    rank, width = staying[0].shape
    size = genes.shape[1] * (2 if gene_bit else 1)
    outs = [struct(*totals[0].shape), struct(rank, width // 2 if link_bit else width)]
    outs += [struct(rank, width + size, dtype=jnp.bfloat16)] if link_bit else []
    outs += [struct(rank, size, dtype=jnp.bfloat16)]
    values = [*totals, *staying, genes, received]
    return pl.pallas_call(
        functools.partial(step_kernel, link_bit, gene_bit),
        in_specs=[SMEM] + [VMEM] * len(values),
        out_specs=[VMEM] * len(outs),
        out_shape=outs,
        compiler_params=PARAMS,
    )(spot, *values)


def next_sums_kernel(
    link_scale, widths, orders, spot, table, mine, other, state, received, to_gene, genes_mine, genes_other, *refs
):
    sums, message, gram, state_out, own = refs
    half = received.shape[0]
    rank, features = sums.shape
    cells = own.shape[1]
    gene_width, peak_width = widths
    gene_blocks, peak_blocks = gene_width // BLOCK, peak_width // BLOCK
    side, place, core = spot[0], spot[1], spot[2]
    first = core == 0
    old = state[...]
    left, right = mine[:rank], other[:rank]
    products = jnp.concatenate([jnp.where(first, left, right), jnp.where(first, right, left)], axis=1)
    new = old * products / (exact(gram_back(mine[rank:], rank), old) + EPSILON)
    state_out[...] = new
    mine_now = new[:, :cells]
    for position in range(1, half):
        at = position * cells
        mine_now = jnp.where(place == orders[0][position], new[:, at : at + cells], mine_now)
    own[...] = mine_now
    high, rest = halved(new)
    mine_low, other_low = genes_mine[...].astype(jnp.float32), genes_other[...].astype(jnp.float32)
    genes = jnp.concatenate(
        [jnp.where(first, mine_low, other_low), jnp.where(first, other_low, mine_low)], axis=1
    )
    total = [None] * (2 * peak_blocks)
    for position, j in enumerate(orders[1]):
        for b in range(gene_blocks):
            at = (position * gene_blocks + b) * BLOCK
            block = genes[:, at : at + BLOCK]
            row = (side * half + j) * gene_blocks + b
            for u in range(2 * peak_blocks):
                column = (place + u // peak_blocks * half) * peak_blocks + u % peak_blocks
                term = table[row, column] * block
                total[u] = term if total[u] is None else total[u] + term
    gene_links = to_gene[...]
    nothing = jnp.zeros_like(gene_links)
    links = jnp.concatenate(
        [jnp.where(side == 0, gene_links, nothing), jnp.where(side == 0, nothing, gene_links), *total], axis=1
    )
    counts = jnp.concatenate([received[j, 0:cells, 0:features] for j in orders[0]], axis=0)
    products = jnp.dot(high, counts, preferred_element_type=jnp.float32)
    gram[...] = gram_of(high, rest)
    finish_sums(products + link_scale * links, gram[...], sums, message)


def update_kernel(last, widths, orders, spot, table, sums, gram_mine, other, factors, received, *outs):
    half = received.shape[0]
    rank, features = sums.shape
    cells = received.shape[1] - rank // 4
    gene_width, peak_width = widths
    gene_blocks, peak_blocks = gene_width // BLOCK, peak_width // BLOCK
    side, place, core = spot[0], spot[1], spot[2]
    first = core == 0
    gram_other, blocks = read_message(other, features, rank)
    gram = gram_mine[...] + gram_other
    old = factors[...]
    below = exact(gram, old) + EPSILON
    whole = jnp.concatenate(
        [sums[:, b * BLOCK : (b + 1) * BLOCK] + block for b, block in enumerate(blocks)], axis=1
    )
    new = old * whole / below
    low = new.astype(jnp.bfloat16)
    counts = jnp.concatenate([received[j, 0:cells, 0:features] for j in orders[0]], axis=0)
    cell_sums = across(low, counts)
    gram_features = across(low, low)
    kept, sent, *outs = outs
    split = half // 2 * cells
    left, right = cell_sums[:, :split], cell_sums[:, split:]
    for ref, value in ((kept, jnp.where(first, left, right)), (sent, jnp.where(first, right, left))):
        ref[:rank] = value
        ref[rank:] = gram_rows(gram_features, split)

    def own(at, width):
        return jnp.where(side == 0, new[:, at : at + width], new[:, at + width : at + 2 * width])

    if last:
        gene_out, peak_out = outs
        gene_out[...] = own(0, gene_width)
        peak_out[...] = own(2 * gene_width, peak_width)
        return
    factors_out, links_kept, links_sent, gene_low = outs
    factors_out[...] = new
    gene_low[...] = own(0, gene_width).astype(jnp.bfloat16)
    peaks = low[:, 2 * gene_width :].astype(jnp.float32)
    peaks = [peaks[:, u * BLOCK : (u + 1) * BLOCK] for u in range(2 * peak_blocks)]
    for position in range(half // 2):
        pair = []
        for j in (orders[1][position], orders[1][position + half // 2]):
            parts = []
            for b in range(gene_blocks):
                row = (side * half + j) * gene_blocks + b
                part = None
                for u, block in enumerate(peaks):
                    column = (place + u // peak_blocks * half) * peak_blocks + u % peak_blocks
                    term = table[row, column] * block
                    part = term if part is None else part + term
                parts.append(part)
            pair.append(jnp.concatenate(parts, axis=1))
        at = position * gene_width
        links_kept[:, at : at + gene_width] = jnp.where(first, *pair)
        links_sent[:, at : at + gene_width] = jnp.where(first, pair[1], pair[0])


def last_cells_kernel(spot, mine, other, old, out):
    rank, cells = out.shape
    totals = mine[:rank] + other[:rank]
    gram = mine[rank:] + other[rank:]
    lanes = totals.shape[1]
    rows = rank * rank // (4 * lanes)
    gram = jnp.concatenate(
        [gram[i * rows : (i + 1) * rows, b * rank : (b + 1) * rank] for i in range(4) for b in range(lanes // rank)],
        axis=0,
    )
    own = totals[:, :cells]
    for position in range(1, lanes // cells):
        own = jnp.where(spot[3] == position, totals[:, position * cells : (position + 1) * cells], own)
    out[...] = old[...] * own / (exact(gram, old[...]) + EPSILON)


def shards_blocks(
    rna_counts,
    atac_counts,
    cell_factor,
    gene_factor,
    peak_factor,
    link_gene,
    link_peak,
    link_weight,
    link_count,
):
    count = lax.axis_size(AXIS)
    half = count // 2
    me = lax.axis_index(AXIS)
    side, place, core = me // half, me % half, me % 2
    chip_bits = bits_below(half)[1:]
    cell_bits, link_bits = chip_bits, turned(chip_bits, 1)
    tail = sum(
        jnp.where((me & bit) != 0, 1 << i, 0) for i, bit in enumerate(reversed(cell_bits[2:]))
    )
    spot = jnp.stack([side, place, core, tail]).astype(jnp.int32)
    rank, cells = cell_factor.shape
    gene_width, peak_width = gene_factor.shape[1], peak_factor.shape[1]
    widths = (gene_width, peak_width)
    width = gene_width + peak_width
    features = 2 * width
    link_scale = cells * count / 4.0
    table_shape = (rna_counts.shape[1] // BLOCK, atac_counts.shape[1] // BLOCK)
    cell_order = layout([1] + cell_bits)
    link_order = layout([1] + link_bits)
    gene_order = layout([1] + link_bits[::-1])

    links = (link_gene, link_peak, link_weight, link_count)
    sent = parcels(spot, rna_counts, atac_counts, cell_factor, gene_factor, peak_factor, links, half)
    halves = [list(range(half)), list(range(half, count))]
    received = lax.all_to_all(sent, AXIS, 0, 0, axis_index_groups=halves, tiled=True)
    rows_other = flip(received[:, cells:, :features], 1)
    received_here = pltpu.with_memory_space_constraint(received, pltpu.VMEM)
    codes = pl.pallas_call(
        codes_kernel,
        in_specs=[VMEM] * 2,
        out_specs=VMEM,
        out_shape=struct(rank, width + 2 * rank, dtype=jnp.int16),
        compiler_params=PARAMS,
    )(gene_factor, peak_factor)
    rows = rank // 4
    half_table = pl.pallas_call(
        table_kernel,
        grid=(1,),
        in_specs=[pl.BlockSpec((half, rows, 2 * rank), lambda i: (0, cells // rows, features // (2 * rank)))],
        out_specs=VMEM,
        out_shape=struct(*table_shape),
        compiler_params=PARAMS,
    )(received_here)
    half_table_other = flip(half_table, half)

    sums_shapes = (struct(rank, features), struct(rank, features + 2 * rank, dtype=jnp.int16))
    sums, gram, state = pl.pallas_call(
        functools.partial(first_sums_kernel, cell_order),
        in_specs=[VMEM],
        out_specs=[VMEM] * 3,
        out_shape=(struct(rank, features), struct(rank, rank), struct(rank, half * cells)),
        compiler_params=PARAMS,
    )(received_here)
    codes, sums, half_table_other = lax.optimization_barrier((codes, sums, half_table_other))
    codes_other = flip(codes, half)
    sums, message, link_table = pl.pallas_call(
        functools.partial(first_links_kernel, link_scale, widths),
        grid=(1,),
        in_specs=[
            SMEM,
            pl.BlockSpec((half, rows, features + 2 * rank), lambda i: (0, cells // rows, 0)),
            VMEM,
            VMEM,
            VMEM,
            VMEM,
            VMEM,
        ],
        out_specs=[VMEM] * 3,
        out_shape=(*sums_shapes, struct(*table_shape)),
        scratch_shapes=[pltpu.SemaphoreType.DMA, pltpu.SMEM(table_shape, jnp.float32)],
        compiler_params=PARAMS,
    )(spot, received_here, rows_other, half_table, half_table_other, sums, gram)

    message, codes_other = lax.optimization_barrier((message, codes_other))
    factors = pl.pallas_call(
        twins_kernel,
        in_specs=[SMEM] + [VMEM] * 3,
        out_specs=VMEM,
        out_shape=struct(rank, features),
        compiler_params=PARAMS,
    )(spot, gene_factor, peak_factor, codes_other)

    split = half // 2 * cells
    for sweep_index in range(ROUNDS):
        last = sweep_index == ROUNDS - 1
        other = flip(message, half)
        outs = [struct(rank + rank * rank // split, split)] * 2
        if last:
            outs += [struct(rank, gene_width), struct(rank, peak_width)]
        else:
            outs += [struct(rank, features)] + [struct(rank, half // 2 * gene_width)] * 2
            outs += [struct(rank, gene_width, dtype=jnp.bfloat16)]
        kept, sent, *outs = pl.pallas_call(
            functools.partial(update_kernel, last, widths, (cell_order, link_order)),
            in_specs=[SMEM] * 2 + [VMEM] * 5,
            out_specs=[VMEM] * len(outs),
            out_shape=outs,
            compiler_params=PARAMS,
        )(spot, link_table, sums, gram, other, factors, received_here)
        if last:
            gene_out, peak_out = outs
            totals = kept + flip(sent, 1)
            first, second = cell_bits[:2]
            quarters = jnp.split(totals[:rank], 4, axis=1)
            gram_part = jnp.concatenate(jnp.split(totals[rank:], 4, axis=1), axis=0)
            is_first, is_second = (me & first) != 0, (me & second) != 0

            def quarter(flip_first, flip_second):
                low, high = (
                    jnp.where(is_second ^ flip_second, quarters[2 * i + 1], quarters[2 * i]) for i in range(2)
                )
                return jnp.concatenate([jnp.where(is_first ^ flip_first, high, low), gram_part], axis=0)

            got = [
                flip(quarter(*which), bit)
                for which, bit in (((True, False), first), ((False, True), second), ((True, True), first | second))
            ]
            totals = quarter(False, False) + (got[0] + got[1] + got[2])
            for bit in cell_bits[2:-1]:
                totals = totals + flip(totals, bit)
            cell_out = pl.pallas_call(
                last_cells_kernel,
                in_specs=[SMEM] + [VMEM] * 3,
                out_specs=VMEM,
                out_shape=struct(rank, cells),
                compiler_params=PARAMS,
            )(spot, totals, flip(totals, cell_bits[-1]), own_cells)
            return cell_out, gene_out, peak_out
        factors, links_kept, links_sent, genes = outs
        totals, staying, leaving, genes = step(
            spot, received_here, link_bits[0], 0, (kept, flip(sent, 1)), (links_kept, flip(links_sent, 1)), genes
        )
        for i, (cell_bit, link_bit) in enumerate(zip(cell_bits, link_bits)):
            going = lax.optimization_barrier((totals, leaving))
            got = lax.optimization_barrier((flip(going[0], cell_bit), flip(going[1], link_bit)))
            next_bit = link_bits[i + 1] if i + 1 < len(link_bits) else 0
            totals, staying, *leaving, genes = step(
                spot, received_here, next_bit, link_bit, (totals, got[0]), (staying, got[1]), genes
            )
            leaving = leaving[0] if next_bit else None
        to_gene = staying
        sums, message, gram, state, own_cells = pl.pallas_call(
            functools.partial(next_sums_kernel, link_scale, widths, (cell_order, gene_order)),
            in_specs=[SMEM] * 2 + [VMEM] * 7,
            out_specs=[VMEM] * 5,
            out_shape=(*sums_shapes, struct(rank, rank), struct(rank, half * cells), struct(rank, cells)),
            compiler_params=PARAMS,
        )(spot, link_table, totals, flip(totals, 1), state, received_here, to_gene, genes, flip(genes, 1))


def shards(rna_counts, atac_counts, cell_factor, gene_factor, peak_factor, link_gene, *links):
    half = lax.axis_size(AXIS) // 2
    rank, cells = cell_factor.shape
    gene_width, peak_width = gene_factor.shape[1], peak_factor.shape[1]
    features = 2 * (gene_width + peak_width)
    in_blocks = (
        half % 16 == 0
        and rank == cells
        and 2 * rank == BLOCK
        and gene_width % BLOCK == 0
        and peak_width % BLOCK == 0
        and rank + 3 + 2 * (features // BLOCK) <= 2 * rank
        and half * link_gene.shape[0] <= 2 * rank
        and rank % 64 == 0
        and atac_counts.shape[1] // BLOCK == 2 * rank
        and max(rna_counts.shape[1], atac_counts.shape[1]) // BLOCK <= 256
    )
    run = shards_blocks if in_blocks else shards_any
    return run(rna_counts, atac_counts, cell_factor, gene_factor, peak_factor, link_gene, *links)


def solution(mesh):
    columns = P(None, ("groups", "cells"))
    slots = P(("groups", "cells"))
    in_specs = (P(("groups", "cells"), None),) * 2 + (columns,) * 3 + (slots,) * 4
    return jax.shard_map(
        shards, mesh=mesh, in_specs=in_specs, out_specs=(columns,) * 3, check_vma=False
    )
```

```python
import functools
import random

import jax
import jax.numpy as jnp
from jax import lax
from jax.experimental import pallas as pl
from jax.experimental.pallas import tpu as pltpu
from jax.sharding import PartitionSpec as P

BLOCK = 128
ROUNDS = 2
EPSILON = 1e-06
CODES = 65535.0
DIGIT = 32768.0
UNITS = 16384.0
TINY = 1e-30
AXIS = "cells"
SEED = 16
PARAMS = pltpu.CompilerParams(vmem_limit_bytes=14 * 1024 * 1024)
SMEM = pl.BlockSpec(memory_space=pltpu.SMEM)
VMEM = pl.BlockSpec(memory_space=pltpu.VMEM)


def flip(value, bit):
    count = lax.axis_size(AXIS)
    return lax.ppermute(value, AXIS, [(i, i ^ bit) for i in range(count)])


def in_order(bit, mine, other):
    mine_first = (lax.axis_index(AXIS) & bit) == 0
    return jnp.where(mine_first, mine, other), jnp.where(mine_first, other, mine)


def bits_below(size):
    return [1 << b for b in range(size.bit_length() - 1)]


def own_table(link_gene, link_peak, link_weight, link_count, gene_blocks, peak_blocks):
    slot_ids = jnp.arange(link_gene.shape[0], dtype=jnp.int32)
    live_weight = jnp.where(slot_ids < link_count[0], link_weight, 0).astype(jnp.float32)
    gene_hot = (link_gene[:, None] == jnp.arange(gene_blocks, dtype=jnp.int32)[None, :]).astype(
        jnp.float32
    )
    peak_hot = (link_peak[:, None] == jnp.arange(peak_blocks, dtype=jnp.int32)[None, :]).astype(
        jnp.float32
    )
    return jnp.dot((gene_hot * live_weight[:, None]).T, peak_hot, precision=lax.Precision.HIGHEST)


def split_low(value):
    high = lax.reduce_precision(value, exponent_bits=8, mantissa_bits=7)
    return high.astype(jnp.bfloat16), (value - high).astype(jnp.bfloat16)


def gather_half(value, half):
    for bit in bits_below(half):
        value = jnp.concatenate(in_order(bit, value, flip(value, bit)), axis=1)
    return value


def scatter_half(value, half):
    for bit in reversed(bits_below(half)):
        low, high = jnp.split(value, 2, axis=1)
        clear = (lax.axis_index(AXIS) & bit) == 0
        value = jnp.where(clear, low, high) + flip(jnp.where(clear, high, low), bit)
    return value


def weigh(weights, source):
    rank = source.shape[0]
    blocks = source.astype(jnp.float32).reshape(rank, weights.shape[1], BLOCK)
    result = jnp.einsum("ksc,ts->ktc", blocks, weights, precision=lax.Precision.HIGHEST)
    return result.reshape(rank, weights.shape[0] * BLOCK)


def coupling(link_table, factors, widths):
    gene_width, peak_width = widths
    half = lax.axis_size(AXIS) // 2
    me = lax.axis_index(AXIS)
    side, place = me // half, me % half
    low = factors.astype(jnp.bfloat16)
    genes, peaks = low[:, : 2 * gene_width], low[:, 2 * gene_width :]
    own_gene = jnp.where(side == 0, genes[:, :gene_width], genes[:, gene_width:])
    side_blocks = half * gene_width // BLOCK
    peak_blocks = peak_width // BLOCK
    side_rows = lax.dynamic_slice_in_dim(link_table, side * side_blocks, side_blocks, 0)
    weights = jnp.concatenate(
        [
            lax.dynamic_slice_in_dim(side_rows, (place + s * half) * peak_blocks, peak_blocks, 1)
            for s in range(2)
        ],
        axis=1,
    )
    to_gene = scatter_half(weigh(weights, peaks), half)
    to_peak = weigh(weights.T, gather_half(own_gene, half))
    nothing = jnp.zeros_like(to_gene)
    return jnp.concatenate([*(jnp.where(side == s, to_gene, nothing) for s in range(2)), to_peak], axis=1)


def shards_any(
    rna_counts,
    atac_counts,
    cell_factor,
    gene_factor,
    peak_factor,
    link_gene,
    link_peak,
    link_weight,
    link_count,
):
    count = lax.axis_size(AXIS)
    half = count // 2
    me = lax.axis_index(AXIS)
    side = me // half
    rank, cells = cell_factor.shape
    gene_width, peak_width = gene_factor.shape[1], peak_factor.shape[1]
    features = 2 * (gene_width + peak_width)
    link_scale = cells * count / 4.0

    link_table = own_table(
        link_gene,
        link_peak,
        link_weight,
        link_count,
        rna_counts.shape[1] // BLOCK,
        atac_counts.shape[1] // BLOCK,
    )
    for bit in bits_below(count):
        link_table = link_table + flip(link_table, bit)

    def by_place(counts, width):
        return counts.reshape(cells, 2, half, width).transpose(2, 0, 1, 3).reshape(half, cells, 2 * width)

    cell_pair = jnp.concatenate([part.T for part in split_low(cell_factor)], axis=1)
    parcels = jnp.concatenate(
        [
            by_place(rna_counts, gene_width),
            by_place(atac_counts, peak_width),
            jnp.broadcast_to(cell_pair[None], (half, cells, 2 * rank)),
        ],
        axis=2,
    )
    halves = [list(range(half)), list(range(half, count))]
    received = lax.all_to_all(parcels, AXIS, 0, 0, axis_index_groups=halves, tiled=True)
    received = received.reshape(half * cells, features + 2 * rank)
    counts, cell_pair = received[:, :features], received[:, features:]

    gene_pair = in_order(half, gene_factor, flip(gene_factor, half))
    peak_pair = in_order(half, peak_factor, flip(peak_factor, half))
    factors = jnp.concatenate([*gene_pair, *peak_pair], axis=1)
    cell_low, cell_rest = cell_pair[:, :rank].T, cell_pair[:, rank:].T
    cell_state = cell_factor

    for sweep_index in range(ROUNDS):
        links = link_scale * coupling(link_table, factors, (gene_width, peak_width))
        pair = jnp.concatenate([cell_low, cell_rest], axis=0)
        squares = lax.dot_general(
            pair, pair, (((1,), (1,)), ((), ())), preferred_element_type=jnp.float32
        )
        gram_cells = (
            squares[:rank, :rank] + squares[:rank, rank:] + squares[rank:, :rank] + squares[rank:, rank:]
        )
        sums = jnp.dot(cell_low, counts, preferred_element_type=jnp.float32) + links
        gram_cells = gram_cells + flip(gram_cells, half)
        sums = sums + flip(sums, half)
        factors = (
            factors
            * sums
            / (jnp.dot(gram_cells, factors, precision=lax.Precision.HIGHEST) + EPSILON)
        )
        low = factors.astype(jnp.bfloat16)
        gram_features = lax.dot_general(
            low, low, (((1,), (1,)), ((), ())), preferred_element_type=jnp.float32
        )
        cell_sums = lax.dot_general(
            low, counts, (((1,), (1,)), ((), ())), preferred_element_type=jnp.float32
        )
        last = sweep_index == ROUNDS - 1
        if last:
            for bit in reversed(bits_below(half)):
                left, right = jnp.split(cell_sums, 2, axis=1)
                clear = (me & bit) == 0
                sent = jnp.concatenate([jnp.where(clear, right, left), gram_features], axis=1)
                got = flip(sent, bit)
                kept = cell_sums.shape[1] // 2
                cell_sums = jnp.where(clear, left, right) + got[:, :kept]
                gram_features = gram_features + got[:, kept:]
        else:
            left, right = jnp.split(cell_sums, 2, axis=1)
            clear = (me & 1) == 0
            sent = jnp.concatenate([jnp.where(clear, right, left), gram_features], axis=1)
            kept = jnp.concatenate([jnp.where(clear, left, right), gram_features], axis=1)
            for bit in bits_below(half):
                kept = kept + flip(sent, bit)
                sent = kept
            width = cell_sums.shape[1] // 2
            cell_sums, gram_features = kept[:, :width], kept[:, width:]
            low_rest = [jnp.where(clear, *jnp.split(part, 2, axis=1)) for part in (cell_low, cell_rest)]
            cell_state = low_rest[0].astype(jnp.float32) + low_rest[1].astype(jnp.float32)
        cell_state = (
            cell_state
            * cell_sums
            / (jnp.dot(gram_features, cell_state, precision=lax.Precision.HIGHEST) + EPSILON)
        )
        if not last:
            pair = jnp.concatenate(split_low(cell_state), axis=0)
            pair = jnp.concatenate(in_order(1, pair, flip(pair, 1)), axis=1)
            cell_low, cell_rest = pair[:rank], pair[rank:]
            mine = lax.dynamic_slice_in_dim(pair, (me % half) * cells, cells, 1).astype(jnp.float32)
            cell_state = mine[:rank] + mine[rank:]

    def own(first, width):
        return jnp.where(side == 0, factors[:, first : first + width], factors[:, first + width : first + 2 * width])

    return cell_state, own(0, gene_width), own(2 * gene_width, peak_width)


def layout(bits):
    size = 1 << len(bits)
    return [
        sum(bit for i, bit in enumerate(bits) if position >> (len(bits) - 1 - i) & 1)
        for position in range(size)
    ]


def shuffled(size, seed):
    places = list(range(size))
    random.Random(seed).shuffle(places)
    return places


def turned(bits, by):
    return bits[by:] + bits[:by]


def across(left, right):
    return lax.dot_general(left, right, (((1,), (1,)), ((), ())), preferred_element_type=jnp.float32)


def halved(value):
    high = value.astype(jnp.bfloat16)
    return high, (value - high.astype(jnp.float32)).astype(jnp.bfloat16)


def exact(left, right):
    left_high, left_low = halved(left)
    right_high, right_low = halved(right)
    return jnp.dot(
        jnp.concatenate([left_low, left_low, left_high, left_high], axis=1),
        jnp.concatenate([right_low, right_high, right_low, right_high], axis=0),
        preferred_element_type=jnp.float32,
    )


def struct(*shape, dtype=jnp.float32):
    return jax.ShapeDtypeStruct(shape, dtype)


def gram_of(high, rest):
    pair = jnp.concatenate([high, rest], axis=0)
    squares = across(pair, pair)
    rank = high.shape[0]
    return (squares[:rank, :rank] + squares[rank:, rank:]) + (squares[:rank, rank:] + squares[rank:, :rank])


def parcels_kernel(seats, spot, rna_0, rna_1, atac_0, atac_1, cell, gene, peak, *refs):
    links, out, copied, slots, sems = refs[:4], refs[4], refs[5:9], refs[9], refs[10]

    copies = [pltpu.make_async_copy(link, to, sems.at[i]) for i, (link, to) in enumerate(zip(links, copied))]

    @pl.when(pl.program_id(0) == 0)
    def _():
        for copy in copies:
            copy.start()

    rank = cell.shape[0]
    cells = rna_0.shape[0]
    gene_width, peak_width = gene.shape[1], peak.shape[1]
    width = gene_width + peak_width
    cell_pair = jnp.concatenate(halved(cell[...]), axis=1)
    gene_low = gene[...].astype(jnp.bfloat16)
    peak_low = peak[...].astype(jnp.bfloat16)
    part = rank // 4
    for j, seat in enumerate(seats):
        at = 0
        for source, size in ((rna_0, gene_width), (rna_1, gene_width), (atac_0, peak_width), (atac_1, peak_width)):
            out[seat, 0:cells, at : at + size] = source[:, j * size : (j + 1) * size]
            at += size
        out[seat, 0:cells, at:] = cell_pair
        for s in range(2):
            row = (2 * (j % 2) + s) * part
            out[seat, cells:, s * width : s * width + gene_width] = gene_low[row : row + part]
            out[seat, cells:, s * width + gene_width : (s + 1) * width] = peak_low[row : row + part]

    @pl.when(pl.program_id(0) == 0)
    def _():
        for copy in copies:
            copy.wait()
        link_gene, link_peak, link_weight, link_count = copied
        count = link_gene.shape[0]
        lane = lax.broadcasted_iota(jnp.int32, slots.shape, 1) - spot[1] * count
        row = lax.broadcasted_iota(jnp.int32, slots.shape, 0)
        value = jnp.zeros(slots.shape, jnp.float32)
        for s in range(count):
            weight = jnp.where(s < link_count[0], link_weight[s], 0)
            for r, entry in enumerate((link_gene[s], link_peak[s], weight)):
                value = jnp.where((lane == s) & (row == r), entry.astype(jnp.float32), value)
        slots[...] = value.astype(jnp.bfloat16)

    for seat in seats:
        out[seat, cells:, 2 * width :] = slots[...]


def power_of(top):
    return jnp.floor(jnp.log2(jnp.maximum(top, TINY))) + 1.0


def encode(value):
    groups = [value[:, at : at + BLOCK] for at in range(0, value.shape[1], BLOCK)]
    least = [jnp.min(group, axis=1, keepdims=True) for group in groups]
    most = [jnp.max(group, axis=1, keepdims=True) for group in groups]
    power = power_of(functools.reduce(jnp.maximum, most))
    unit, per_unit = jnp.exp2(power) / UNITS, jnp.exp2(-power) * UNITS
    least = [jnp.floor(low * per_unit) for low in least]
    most = [jnp.ceil(high * per_unit) for high in most]
    codes = []
    for group, low, high in zip(groups, least, most):
        spread = (high - low) * unit
        per = jnp.where(spread > 0.0, CODES / spread, 0.0)
        code = jnp.clip(jnp.floor((group - low * unit) * per + 0.5), 0.0, CODES) - (CODES + 1) / 2
        codes.append(code.astype(jnp.int32).astype(jnp.int16))
    return codes, [*least, *most, power]


def decode(code, least, most, power):
    steps = code.astype(jnp.int32).astype(jnp.float32) + (CODES + 1) / 2
    return (least + steps * ((most - least) / CODES)) * (jnp.exp2(power) / UNITS)


def whole_numbers(columns, lanes):
    rows = columns[0].shape[0]
    size = sum(column.shape[1] for column in columns)
    filled = jnp.concatenate([*columns, jnp.zeros((rows, lanes - size), jnp.float32)], axis=1)
    return filled.astype(jnp.int32).astype(jnp.int16)


def codes_kernel(gene, peak, message):
    codes, columns = encode(jnp.concatenate([gene[...], peak[...]], axis=1))
    for b, code in enumerate(codes):
        message[:, b * BLOCK : (b + 1) * BLOCK] = code
    at = len(codes) * BLOCK
    message[:, at:] = whole_numbers(columns, message.shape[1] - at)


def table_kernel(received_slots, out):
    slots = sum(received_slots[j].astype(jnp.float32) for j in range(received_slots.shape[0]))

    def hot(row, size, value):
        ids = lax.broadcasted_iota(jnp.int32, (size, slots.shape[1]), 0).astype(jnp.float32)
        return jnp.where(slots[row : row + 1] == ids, value, 0.0).astype(jnp.bfloat16)

    out[...] = across(hot(0, out.shape[0], slots[2:3]), hot(1, out.shape[1], 1.0))


def twins_kernel(spot, gene, peak, got, out):
    width = gene.shape[1] + peak.shape[1]
    groups = width // BLOCK
    columns = got[:, width:].astype(jnp.int32).astype(jnp.float32)
    power = columns[:, 2 * groups : 2 * groups + 1]
    at = g = 0
    first = spot[0] == 0
    for ref in (gene, peak):
        size = ref.shape[1]
        for b in range(size // BLOCK):
            mine = ref[:, b * BLOCK : (b + 1) * BLOCK]
            other = decode(
                got[:, g * BLOCK : (g + 1) * BLOCK], columns[:, g : g + 1], columns[:, groups + g : groups + g + 1], power
            )
            out[:, at + b * BLOCK : at + (b + 1) * BLOCK] = jnp.where(first, mine, other)
            out[:, at + size + b * BLOCK : at + size + (b + 1) * BLOCK] = jnp.where(first, other, mine)
            g += 1
        at += 2 * size


def in_hbm(value):
    return pltpu.with_memory_space_constraint(value, pltpu.HBM)


def parcels(spot, rna_counts, atac_counts, cell_factor, gene_factor, peak_factor, links, seats):
    half = len(seats)
    cells = rna_counts.shape[0]
    rank = cell_factor.shape[0]
    gene_width, peak_width = gene_factor.shape[1], peak_factor.shape[1]
    rows, lanes = cells + rank // 4, 2 * (gene_width + peak_width) + 2 * rank

    def columns(width, side):
        return pl.BlockSpec((cells, half * width), lambda i: (0, side))

    def whole(array):
        return pl.BlockSpec(array.shape, lambda i: (0, 0))

    return pl.pallas_call(
        functools.partial(parcels_kernel, seats),
        grid=(1,),
        in_specs=[SMEM, columns(gene_width, 0), columns(gene_width, 1), columns(peak_width, 0), columns(peak_width, 1)]
        + [whole(a) for a in (cell_factor, gene_factor, peak_factor)]
        + [pl.BlockSpec(memory_space=pl.ANY)] * 4,
        out_specs=VMEM,
        out_shape=struct(half, rows, lanes, dtype=jnp.bfloat16),
        scratch_shapes=[pltpu.SMEM(link.shape, jnp.int32) for link in links]
        + [pltpu.VMEM((rank // 4, 2 * rank), jnp.bfloat16), pltpu.SemaphoreType.DMA((4,))],
        compiler_params=PARAMS,
    )(
        spot,
        *(in_hbm(a) for a in (rna_counts, rna_counts, atac_counts, atac_counts, cell_factor, gene_factor, peak_factor)),
        *(in_hbm(a) for a in links[:-1]),
        links[-1],
    )


def first_sums_kernel(order, received, sums, gram, state):
    rank, features = sums.shape
    cells = received.shape[1] - rank // 4
    high = jnp.concatenate([received[j, 0:cells, features : features + rank] for j in order], axis=1)
    rest = jnp.concatenate([received[j, 0:cells, features + rank :] for j in order], axis=1)
    counts = jnp.concatenate([received[j, 0:cells, 0:features] for j in order], axis=0)
    sums[...] = jnp.dot(high, counts, preferred_element_type=jnp.float32)
    gram[...] = gram_of(high, rest)
    state[...] = high.astype(jnp.float32) + rest.astype(jnp.float32)


def by_index(rank):
    row = lax.broadcasted_iota(jnp.int32, (rank, rank), 0)
    return row, lax.broadcasted_iota(jnp.int32, (rank, rank), 1)


def finish_sums(sums_value, gram_value, sums, message):
    rank, features = sums_value.shape
    sums[...] = sums_value
    codes, columns = encode(sums_value)
    for b, code in enumerate(codes):
        message[:, b * BLOCK : (b + 1) * BLOCK] = code
    power = power_of(jnp.max(jnp.max(gram_value, axis=1, keepdims=True), axis=0, keepdims=True))
    scaled = gram_value * (jnp.exp2(-power) * DIGIT)
    high = jnp.minimum(jnp.floor(scaled), DIGIT - 1)
    low = jnp.clip(jnp.floor((scaled - high) * DIGIT), 0.0, DIGIT - 1)
    row, column = by_index(rank)
    diagonal = jnp.sum(jnp.where(row == column, low, 0.0), axis=1, keepdims=True)
    columns = [jnp.where(row <= column, high, low), diagonal, jnp.broadcast_to(power, (rank, 1)), *columns]
    message[:, features:] = whole_numbers(columns, message.shape[1] - features)


def read_message(message, features, rank):
    groups = features // BLOCK
    beside = message[:, features:].astype(jnp.int32).astype(jnp.float32)
    lanes = beside.shape[1]
    square = jnp.concatenate([beside, jnp.zeros((lanes - rank, lanes), jnp.float32)], axis=0).T
    upright, turned_over = beside[:, :rank], square[:rank, :rank]
    diagonal, power = beside[:, rank : rank + 1], beside[:, rank + 1 : rank + 2]
    row, column = by_index(rank)
    high = jnp.where(row <= column, upright, turned_over)
    low = jnp.where(row == column, diagonal, jnp.where(row < column, turned_over, upright))
    gram = (high + low / DIGIT) * (jnp.exp2(power) / DIGIT)
    at = rank + 2
    sums_power = beside[:, at + 2 * groups : at + 2 * groups + 1]
    blocks = [
        decode(
            message[:, b * BLOCK : (b + 1) * BLOCK],
            beside[:, at + b : at + b + 1],
            beside[:, at + groups + b : at + groups + b + 1],
            sums_power,
        )
        for b in range(groups)
    ]
    return gram, blocks


def first_links_kernel(
    link_scale, widths, seats, spot, mine, other, half_table, half_table_other, sums_in, gram, sums, message, table, sem, table_smem
):
    half = mine.shape[0]
    rank, features = sums_in.shape
    gene_width, peak_width = widths
    gene_blocks, peak_blocks = gene_width // BLOCK, peak_width // BLOCK
    width = gene_width + peak_width
    table[...] = half_table[...] + half_table_other[...]
    copy = pltpu.make_async_copy(table, table_smem, sem)
    copy.start()
    copy.wait()
    side, place, core = spot[0], spot[1], spot[2]
    total = [None] * (features // BLOCK)

    def add(target, weight, block):
        term = weight * block
        total[target] = term if total[target] is None else total[target] + term

    for j in range(half):
        blocks = []
        for b in range(width // BLOCK):
            pieces = [
                ref[seats[j], :, s * width + b * BLOCK : s * width + (b + 1) * BLOCK]
                for ref in (mine, other)
                for s in range(2)
            ]
            blocks.append(jnp.concatenate(pieces, axis=0).astype(jnp.float32))
        for b in range(gene_blocks):
            row = (side * half + j) * gene_blocks + b
            for u in range(2 * peak_blocks):
                column = (place + u // peak_blocks * half) * peak_blocks + u % peak_blocks
                add(2 * gene_blocks + u, table_smem[row, column], blocks[b])
        for b in range(peak_blocks):
            column = (side * half + j) * peak_blocks + b
            for t in range(2 * gene_blocks):
                row = (place + t // gene_blocks * half) * gene_blocks + t % gene_blocks
                add(t, table_smem[row, column], blocks[gene_blocks + b])
    links = jnp.concatenate(total, axis=1)
    ahead, behind = links[: rank // 2], links[rank // 2 :]
    first = core == 0
    links = jnp.concatenate([jnp.where(first, ahead, behind), jnp.where(first, behind, ahead)], axis=0)
    finish_sums(sums_in[...] + link_scale * links, gram[...], sums, message)


def gram_rows(gram, lanes):
    rank = gram.shape[0]
    rows = rank * rank // lanes
    return jnp.concatenate([gram[b * rows : (b + 1) * rows] for b in range(rank // rows)], axis=1)


def gram_back(rows_value, rank):
    return jnp.concatenate(
        [rows_value[:, b * rank : (b + 1) * rank] for b in range(rows_value.shape[1] // rank)], axis=0
    )


def step_kernel(link_bit, gene_bit, spot, totals, totals_got, staying, got, genes, received, totals_out, staying_out, *outs):
    totals_out[...] = totals[...] + totals_got[...]
    rank, width = staying.shape
    low = genes[...]
    if gene_bit:
        to_gene = staying[...] + (got[:, :width].astype(jnp.float32) + got[:, width : 2 * width].astype(jnp.float32))
        clear = (spot[1] // gene_bit) % 2 == 0
        mine, other = low.astype(jnp.float32), got[:, 2 * width :].astype(jnp.float32)
        low = jnp.concatenate([jnp.where(clear, mine, other), jnp.where(clear, other, mine)], axis=1)
        low = low.astype(jnp.bfloat16)
    else:
        to_gene = staying[...] + got[...]
    if link_bit:
        clear = (spot[1] // link_bit) % 2 == 0
        left, right = to_gene[:, : width // 2], to_gene[:, width // 2 :]
        staying_out[...] = jnp.where(clear, left, right)
        leaving = halved(jnp.where(clear, right, left))
        outs[0][...] = jnp.concatenate([*leaving, low], axis=1)
    else:
        staying_out[...] = to_gene
    outs[-1][...] = low


def step(spot, received, link_bit, gene_bit, totals, staying, genes):
    rank, width = staying[0].shape
    size = genes.shape[1] * (2 if gene_bit else 1)
    outs = [struct(*totals[0].shape), struct(rank, width // 2 if link_bit else width)]
    outs += [struct(rank, width + size, dtype=jnp.bfloat16)] if link_bit else []
    outs += [struct(rank, size, dtype=jnp.bfloat16)]
    values = [*totals, *staying, genes, received]
    return pl.pallas_call(
        functools.partial(step_kernel, link_bit, gene_bit),
        in_specs=[SMEM] + [VMEM] * len(values),
        out_specs=[VMEM] * len(outs),
        out_shape=outs,
        compiler_params=PARAMS,
    )(spot, *values)


def next_sums_kernel(
    link_scale, widths, orders, spot, table, mine, other, state, received, to_gene, genes_mine, genes_other, *refs
):
    sums, message, gram, state_out, own = refs
    half = received.shape[0]
    rank, features = sums.shape
    cells = own.shape[1]
    gene_width, peak_width = widths
    gene_blocks, peak_blocks = gene_width // BLOCK, peak_width // BLOCK
    side, place, core = spot[0], spot[1], spot[2]
    first = core == 0
    old = state[...]
    left, right = mine[:rank], other[:rank]
    products = jnp.concatenate([jnp.where(first, left, right), jnp.where(first, right, left)], axis=1)
    new = old * products / (exact(gram_back(mine[rank:], rank), old) + EPSILON)
    state_out[...] = new
    mine_now = new[:, :cells]
    for position in range(1, half):
        at = position * cells
        mine_now = jnp.where(place == orders[0][position], new[:, at : at + cells], mine_now)
    own[...] = mine_now
    high, rest = halved(new)
    mine_low, other_low = genes_mine[...].astype(jnp.float32), genes_other[...].astype(jnp.float32)
    genes = jnp.concatenate(
        [jnp.where(first, mine_low, other_low), jnp.where(first, other_low, mine_low)], axis=1
    )
    total = [None] * (2 * peak_blocks)
    for position, j in enumerate(orders[1]):
        for b in range(gene_blocks):
            at = (position * gene_blocks + b) * BLOCK
            block = genes[:, at : at + BLOCK]
            row = (side * half + j) * gene_blocks + b
            for u in range(2 * peak_blocks):
                column = (place + u // peak_blocks * half) * peak_blocks + u % peak_blocks
                term = table[row, column] * block
                total[u] = term if total[u] is None else total[u] + term
    gene_links = to_gene[...]
    nothing = jnp.zeros_like(gene_links)
    links = jnp.concatenate(
        [jnp.where(side == 0, gene_links, nothing), jnp.where(side == 0, nothing, gene_links), *total], axis=1
    )
    counts = jnp.concatenate([received[j, 0:cells, 0:features] for j in orders[2]], axis=0)
    products = jnp.dot(high, counts, preferred_element_type=jnp.float32)
    gram[...] = gram_of(high, rest)
    finish_sums(products + link_scale * links, gram[...], sums, message)


def update_kernel(last, widths, orders, spot, table, sums, gram_mine, other, factors, received, *outs):
    half = received.shape[0]
    rank, features = sums.shape
    cells = received.shape[1] - rank // 4
    gene_width, peak_width = widths
    gene_blocks, peak_blocks = gene_width // BLOCK, peak_width // BLOCK
    side, place, core = spot[0], spot[1], spot[2]
    first = core == 0
    gram_other, blocks = read_message(other, features, rank)
    gram = gram_mine[...] + gram_other
    old = factors[...]
    below = exact(gram, old) + EPSILON
    whole = jnp.concatenate(
        [sums[:, b * BLOCK : (b + 1) * BLOCK] + block for b, block in enumerate(blocks)], axis=1
    )
    new = old * whole / below
    low = new.astype(jnp.bfloat16)
    counts = jnp.concatenate([received[j, 0:cells, 0:features] for j in orders[0]], axis=0)
    cell_sums = across(low, counts)
    gram_features = across(low, low)
    kept, sent, *outs = outs
    split = half // 2 * cells
    left, right = cell_sums[:, :split], cell_sums[:, split:]
    for ref, value in ((kept, jnp.where(first, left, right)), (sent, jnp.where(first, right, left))):
        ref[:rank] = value
        ref[rank:] = gram_rows(gram_features, split)

    def own(at, width):
        return jnp.where(side == 0, new[:, at : at + width], new[:, at + width : at + 2 * width])

    if last:
        gene_out, peak_out = outs
        gene_out[...] = own(0, gene_width)
        peak_out[...] = own(2 * gene_width, peak_width)
        return
    factors_out, links_kept, links_sent, gene_low = outs
    factors_out[...] = new
    gene_low[...] = own(0, gene_width).astype(jnp.bfloat16)
    peaks = low[:, 2 * gene_width :].astype(jnp.float32)
    peaks = [peaks[:, u * BLOCK : (u + 1) * BLOCK] for u in range(2 * peak_blocks)]
    for position in range(half // 2):
        pair = []
        for j in (orders[1][position], orders[1][position + half // 2]):
            parts = []
            for b in range(gene_blocks):
                row = (side * half + j) * gene_blocks + b
                part = None
                for u, block in enumerate(peaks):
                    column = (place + u // peak_blocks * half) * peak_blocks + u % peak_blocks
                    term = table[row, column] * block
                    part = term if part is None else part + term
                parts.append(part)
            pair.append(jnp.concatenate(parts, axis=1))
        at = position * gene_width
        links_kept[:, at : at + gene_width] = jnp.where(first, *pair)
        links_sent[:, at : at + gene_width] = jnp.where(first, pair[1], pair[0])


def last_cells_kernel(spot, mine, other, old, out):
    rank, cells = out.shape
    totals = mine[:rank] + other[:rank]
    gram = mine[rank:] + other[rank:]
    lanes = totals.shape[1]
    rows = rank * rank // (4 * lanes)
    gram = jnp.concatenate(
        [gram[i * rows : (i + 1) * rows, b * rank : (b + 1) * rank] for i in range(4) for b in range(lanes // rank)],
        axis=0,
    )
    own = totals[:, :cells]
    for position in range(1, lanes // cells):
        own = jnp.where(spot[3] == position, totals[:, position * cells : (position + 1) * cells], own)
    out[...] = old[...] * own / (exact(gram, old[...]) + EPSILON)


def shards_blocks(
    rna_counts,
    atac_counts,
    cell_factor,
    gene_factor,
    peak_factor,
    link_gene,
    link_peak,
    link_weight,
    link_count,
):
    count = lax.axis_size(AXIS)
    half = count // 2
    me = lax.axis_index(AXIS)
    side, place, core = me // half, me % half, me % 2
    chip_bits = bits_below(half)[1:]
    cell_bits, link_bits = chip_bits, turned(chip_bits, 1)
    tail = sum(
        jnp.where((me & bit) != 0, 1 << i, 0) for i, bit in enumerate(reversed(cell_bits[2:]))
    )
    spot = jnp.stack([side, place, core, tail]).astype(jnp.int32)
    rank, cells = cell_factor.shape
    gene_width, peak_width = gene_factor.shape[1], peak_factor.shape[1]
    widths = (gene_width, peak_width)
    width = gene_width + peak_width
    features = 2 * width
    link_scale = cells * count / 4.0
    table_shape = (rna_counts.shape[1] // BLOCK, atac_counts.shape[1] // BLOCK)
    cell_order = layout([1] + cell_bits)
    link_order = layout([1] + link_bits)
    gene_order = layout([1] + link_bits[::-1])

    links = (link_gene, link_peak, link_weight, link_count)
    in_seats = shuffled(half, SEED)
    seats = [in_seats.index(j) for j in range(half)]
    cell_seats = [seats[j] for j in cell_order]
    sent = parcels(spot, rna_counts, atac_counts, cell_factor, gene_factor, peak_factor, links, seats)
    halves = [[side_start + j for j in in_seats] for side_start in (0, half)]
    received = lax.all_to_all(sent, AXIS, 0, 0, axis_index_groups=halves, tiled=True)
    rows_other = flip(received[:, cells:, :features], 1)
    received_here = pltpu.with_memory_space_constraint(received, pltpu.VMEM)
    codes = pl.pallas_call(
        codes_kernel,
        in_specs=[VMEM] * 2,
        out_specs=VMEM,
        out_shape=struct(rank, width + 2 * rank, dtype=jnp.int16),
        compiler_params=PARAMS,
    )(gene_factor, peak_factor)
    rows = rank // 4
    half_table = pl.pallas_call(
        table_kernel,
        grid=(1,),
        in_specs=[pl.BlockSpec((half, rows, 2 * rank), lambda i: (0, cells // rows, features // (2 * rank)))],
        out_specs=VMEM,
        out_shape=struct(*table_shape),
        compiler_params=PARAMS,
    )(received_here)
    half_table_other = flip(half_table, half)

    sums_shapes = (struct(rank, features), struct(rank, features + 2 * rank, dtype=jnp.int16))
    sums, gram, state = pl.pallas_call(
        functools.partial(first_sums_kernel, cell_seats),
        in_specs=[VMEM],
        out_specs=[VMEM] * 3,
        out_shape=(struct(rank, features), struct(rank, rank), struct(rank, half * cells)),
        compiler_params=PARAMS,
    )(received_here)
    codes, sums, half_table_other = lax.optimization_barrier((codes, sums, half_table_other))
    codes_other = flip(codes, half)
    sums, message, link_table = pl.pallas_call(
        functools.partial(first_links_kernel, link_scale, widths, seats),
        grid=(1,),
        in_specs=[
            SMEM,
            pl.BlockSpec((half, rows, features + 2 * rank), lambda i: (0, cells // rows, 0)),
            VMEM,
            VMEM,
            VMEM,
            VMEM,
            VMEM,
        ],
        out_specs=[VMEM] * 3,
        out_shape=(*sums_shapes, struct(*table_shape)),
        scratch_shapes=[pltpu.SemaphoreType.DMA, pltpu.SMEM(table_shape, jnp.float32)],
        compiler_params=PARAMS,
    )(spot, received_here, rows_other, half_table, half_table_other, sums, gram)

    message, codes_other = lax.optimization_barrier((message, codes_other))
    factors = pl.pallas_call(
        twins_kernel,
        in_specs=[SMEM] + [VMEM] * 3,
        out_specs=VMEM,
        out_shape=struct(rank, features),
        compiler_params=PARAMS,
    )(spot, gene_factor, peak_factor, codes_other)

    split = half // 2 * cells
    for sweep_index in range(ROUNDS):
        last = sweep_index == ROUNDS - 1
        other = flip(message, half)
        outs = [struct(rank + rank * rank // split, split)] * 2
        if last:
            outs += [struct(rank, gene_width), struct(rank, peak_width)]
        else:
            outs += [struct(rank, features)] + [struct(rank, half // 2 * gene_width)] * 2
            outs += [struct(rank, gene_width, dtype=jnp.bfloat16)]
        kept, sent, *outs = pl.pallas_call(
            functools.partial(update_kernel, last, widths, (cell_seats, link_order)),
            in_specs=[SMEM] * 2 + [VMEM] * 5,
            out_specs=[VMEM] * len(outs),
            out_shape=outs,
            compiler_params=PARAMS,
        )(spot, link_table, sums, gram, other, factors, received_here)
        if last:
            gene_out, peak_out = outs
            totals = kept + flip(sent, 1)
            first, second = cell_bits[:2]
            quarters = jnp.split(totals[:rank], 4, axis=1)
            gram_part = jnp.concatenate(jnp.split(totals[rank:], 4, axis=1), axis=0)
            is_first, is_second = (me & first) != 0, (me & second) != 0

            def quarter(flip_first, flip_second):
                low, high = (
                    jnp.where(is_second ^ flip_second, quarters[2 * i + 1], quarters[2 * i]) for i in range(2)
                )
                return jnp.concatenate([jnp.where(is_first ^ flip_first, high, low), gram_part], axis=0)

            got = [
                flip(quarter(*which), bit)
                for which, bit in (((True, False), first), ((False, True), second), ((True, True), first | second))
            ]
            totals = quarter(False, False) + (got[0] + got[1] + got[2])
            for bit in cell_bits[2:-1]:
                totals = totals + flip(totals, bit)
            cell_out = pl.pallas_call(
                last_cells_kernel,
                in_specs=[SMEM] + [VMEM] * 3,
                out_specs=VMEM,
                out_shape=struct(rank, cells),
                compiler_params=PARAMS,
            )(spot, totals, flip(totals, cell_bits[-1]), own_cells)
            return cell_out, gene_out, peak_out
        factors, links_kept, links_sent, genes = outs
        totals, staying, leaving, genes = step(
            spot, received_here, link_bits[0], 0, (kept, flip(sent, 1)), (links_kept, flip(links_sent, 1)), genes
        )
        for i, (cell_bit, link_bit) in enumerate(zip(cell_bits, link_bits)):
            going = lax.optimization_barrier((totals, leaving))
            got = lax.optimization_barrier((flip(going[0], cell_bit), flip(going[1], link_bit)))
            next_bit = link_bits[i + 1] if i + 1 < len(link_bits) else 0
            totals, staying, *leaving, genes = step(
                spot, received_here, next_bit, link_bit, (totals, got[0]), (staying, got[1]), genes
            )
            leaving = leaving[0] if next_bit else None
        to_gene = staying
        sums, message, gram, state, own_cells = pl.pallas_call(
            functools.partial(next_sums_kernel, link_scale, widths, (cell_order, gene_order, cell_seats)),
            in_specs=[SMEM] * 2 + [VMEM] * 7,
            out_specs=[VMEM] * 5,
            out_shape=(*sums_shapes, struct(rank, rank), struct(rank, half * cells), struct(rank, cells)),
            compiler_params=PARAMS,
        )(spot, link_table, totals, flip(totals, 1), state, received_here, to_gene, genes, flip(genes, 1))


def shards(rna_counts, atac_counts, cell_factor, gene_factor, peak_factor, link_gene, *links):
    half = lax.axis_size(AXIS) // 2
    rank, cells = cell_factor.shape
    gene_width, peak_width = gene_factor.shape[1], peak_factor.shape[1]
    features = 2 * (gene_width + peak_width)
    in_blocks = (
        half % 16 == 0
        and rank == cells
        and 2 * rank == BLOCK
        and gene_width % BLOCK == 0
        and peak_width % BLOCK == 0
        and rank + 3 + 2 * (features // BLOCK) <= 2 * rank
        and half * link_gene.shape[0] <= 2 * rank
        and rank % 64 == 0
        and atac_counts.shape[1] // BLOCK == 2 * rank
        and max(rna_counts.shape[1], atac_counts.shape[1]) // BLOCK <= 256
    )
    run = shards_blocks if in_blocks else shards_any
    return run(rna_counts, atac_counts, cell_factor, gene_factor, peak_factor, link_gene, *links)


def solution(mesh):
    columns = P(None, ("groups", "cells"))
    slots = P(("groups", "cells"))
    in_specs = (P(("groups", "cells"), None),) * 2 + (columns,) * 3 + (slots,) * 4
    return jax.shard_map(
        shards, mesh=mesh, in_specs=in_specs, out_specs=(columns,) * 3, check_vma=False
    )
```

```python
import functools
import random

import jax
import jax.numpy as jnp
from jax import lax
from jax.experimental import pallas as pl
from jax.experimental.pallas import tpu as pltpu
from jax.sharding import PartitionSpec as P

BLOCK = 128
ROUNDS = 2
EPSILON = 1e-06
CODES = 65535.0
DIGIT = 32768.0
UNITS = 16384.0
TINY = 1e-30
AXIS = "cells"
SEED = 16
PARAMS = pltpu.CompilerParams(vmem_limit_bytes=14 * 1024 * 1024)
SMEM = pl.BlockSpec(memory_space=pltpu.SMEM)
VMEM = pl.BlockSpec(memory_space=pltpu.VMEM)


def flip(value, bit):
    count = lax.axis_size(AXIS)
    return lax.ppermute(value, AXIS, [(i, i ^ bit) for i in range(count)])


def in_order(bit, mine, other):
    mine_first = (lax.axis_index(AXIS) & bit) == 0
    return jnp.where(mine_first, mine, other), jnp.where(mine_first, other, mine)


def bits_below(size):
    return [1 << b for b in range(size.bit_length() - 1)]


def own_table(link_gene, link_peak, link_weight, link_count, gene_blocks, peak_blocks):
    slot_ids = jnp.arange(link_gene.shape[0], dtype=jnp.int32)
    live_weight = jnp.where(slot_ids < link_count[0], link_weight, 0).astype(jnp.float32)
    gene_hot = (link_gene[:, None] == jnp.arange(gene_blocks, dtype=jnp.int32)[None, :]).astype(
        jnp.float32
    )
    peak_hot = (link_peak[:, None] == jnp.arange(peak_blocks, dtype=jnp.int32)[None, :]).astype(
        jnp.float32
    )
    return jnp.dot((gene_hot * live_weight[:, None]).T, peak_hot, precision=lax.Precision.HIGHEST)


def split_low(value):
    high = lax.reduce_precision(value, exponent_bits=8, mantissa_bits=7)
    return high.astype(jnp.bfloat16), (value - high).astype(jnp.bfloat16)


def gather_half(value, half):
    for bit in bits_below(half):
        value = jnp.concatenate(in_order(bit, value, flip(value, bit)), axis=1)
    return value


def scatter_half(value, half):
    for bit in reversed(bits_below(half)):
        low, high = jnp.split(value, 2, axis=1)
        clear = (lax.axis_index(AXIS) & bit) == 0
        value = jnp.where(clear, low, high) + flip(jnp.where(clear, high, low), bit)
    return value


def weigh(weights, source):
    rank = source.shape[0]
    blocks = source.astype(jnp.float32).reshape(rank, weights.shape[1], BLOCK)
    result = jnp.einsum("ksc,ts->ktc", blocks, weights, precision=lax.Precision.HIGHEST)
    return result.reshape(rank, weights.shape[0] * BLOCK)


def coupling(link_table, factors, widths):
    gene_width, peak_width = widths
    half = lax.axis_size(AXIS) // 2
    me = lax.axis_index(AXIS)
    side, place = me // half, me % half
    low = factors.astype(jnp.bfloat16)
    genes, peaks = low[:, : 2 * gene_width], low[:, 2 * gene_width :]
    own_gene = jnp.where(side == 0, genes[:, :gene_width], genes[:, gene_width:])
    side_blocks = half * gene_width // BLOCK
    peak_blocks = peak_width // BLOCK
    side_rows = lax.dynamic_slice_in_dim(link_table, side * side_blocks, side_blocks, 0)
    weights = jnp.concatenate(
        [
            lax.dynamic_slice_in_dim(side_rows, (place + s * half) * peak_blocks, peak_blocks, 1)
            for s in range(2)
        ],
        axis=1,
    )
    to_gene = scatter_half(weigh(weights, peaks), half)
    to_peak = weigh(weights.T, gather_half(own_gene, half))
    nothing = jnp.zeros_like(to_gene)
    return jnp.concatenate([*(jnp.where(side == s, to_gene, nothing) for s in range(2)), to_peak], axis=1)


def shards_any(
    rna_counts,
    atac_counts,
    cell_factor,
    gene_factor,
    peak_factor,
    link_gene,
    link_peak,
    link_weight,
    link_count,
):
    count = lax.axis_size(AXIS)
    half = count // 2
    me = lax.axis_index(AXIS)
    side = me // half
    rank, cells = cell_factor.shape
    gene_width, peak_width = gene_factor.shape[1], peak_factor.shape[1]
    features = 2 * (gene_width + peak_width)
    link_scale = cells * count / 4.0

    link_table = own_table(
        link_gene,
        link_peak,
        link_weight,
        link_count,
        rna_counts.shape[1] // BLOCK,
        atac_counts.shape[1] // BLOCK,
    )
    for bit in bits_below(count):
        link_table = link_table + flip(link_table, bit)

    def by_place(counts, width):
        return counts.reshape(cells, 2, half, width).transpose(2, 0, 1, 3).reshape(half, cells, 2 * width)

    cell_pair = jnp.concatenate([part.T for part in split_low(cell_factor)], axis=1)
    parcels = jnp.concatenate(
        [
            by_place(rna_counts, gene_width),
            by_place(atac_counts, peak_width),
            jnp.broadcast_to(cell_pair[None], (half, cells, 2 * rank)),
        ],
        axis=2,
    )
    halves = [list(range(half)), list(range(half, count))]
    received = lax.all_to_all(parcels, AXIS, 0, 0, axis_index_groups=halves, tiled=True)
    received = received.reshape(half * cells, features + 2 * rank)
    counts, cell_pair = received[:, :features], received[:, features:]

    gene_pair = in_order(half, gene_factor, flip(gene_factor, half))
    peak_pair = in_order(half, peak_factor, flip(peak_factor, half))
    factors = jnp.concatenate([*gene_pair, *peak_pair], axis=1)
    cell_low, cell_rest = cell_pair[:, :rank].T, cell_pair[:, rank:].T
    cell_state = cell_factor

    for sweep_index in range(ROUNDS):
        links = link_scale * coupling(link_table, factors, (gene_width, peak_width))
        pair = jnp.concatenate([cell_low, cell_rest], axis=0)
        squares = lax.dot_general(
            pair, pair, (((1,), (1,)), ((), ())), preferred_element_type=jnp.float32
        )
        gram_cells = (
            squares[:rank, :rank] + squares[:rank, rank:] + squares[rank:, :rank] + squares[rank:, rank:]
        )
        sums = jnp.dot(cell_low, counts, preferred_element_type=jnp.float32) + links
        gram_cells = gram_cells + flip(gram_cells, half)
        sums = sums + flip(sums, half)
        factors = (
            factors
            * sums
            / (jnp.dot(gram_cells, factors, precision=lax.Precision.HIGHEST) + EPSILON)
        )
        low = factors.astype(jnp.bfloat16)
        gram_features = lax.dot_general(
            low, low, (((1,), (1,)), ((), ())), preferred_element_type=jnp.float32
        )
        cell_sums = lax.dot_general(
            low, counts, (((1,), (1,)), ((), ())), preferred_element_type=jnp.float32
        )
        last = sweep_index == ROUNDS - 1
        if last:
            for bit in reversed(bits_below(half)):
                left, right = jnp.split(cell_sums, 2, axis=1)
                clear = (me & bit) == 0
                sent = jnp.concatenate([jnp.where(clear, right, left), gram_features], axis=1)
                got = flip(sent, bit)
                kept = cell_sums.shape[1] // 2
                cell_sums = jnp.where(clear, left, right) + got[:, :kept]
                gram_features = gram_features + got[:, kept:]
        else:
            left, right = jnp.split(cell_sums, 2, axis=1)
            clear = (me & 1) == 0
            sent = jnp.concatenate([jnp.where(clear, right, left), gram_features], axis=1)
            kept = jnp.concatenate([jnp.where(clear, left, right), gram_features], axis=1)
            for bit in bits_below(half):
                kept = kept + flip(sent, bit)
                sent = kept
            width = cell_sums.shape[1] // 2
            cell_sums, gram_features = kept[:, :width], kept[:, width:]
            low_rest = [jnp.where(clear, *jnp.split(part, 2, axis=1)) for part in (cell_low, cell_rest)]
            cell_state = low_rest[0].astype(jnp.float32) + low_rest[1].astype(jnp.float32)
        cell_state = (
            cell_state
            * cell_sums
            / (jnp.dot(gram_features, cell_state, precision=lax.Precision.HIGHEST) + EPSILON)
        )
        if not last:
            pair = jnp.concatenate(split_low(cell_state), axis=0)
            pair = jnp.concatenate(in_order(1, pair, flip(pair, 1)), axis=1)
            cell_low, cell_rest = pair[:rank], pair[rank:]
            mine = lax.dynamic_slice_in_dim(pair, (me % half) * cells, cells, 1).astype(jnp.float32)
            cell_state = mine[:rank] + mine[rank:]

    def own(first, width):
        return jnp.where(side == 0, factors[:, first : first + width], factors[:, first + width : first + 2 * width])

    return cell_state, own(0, gene_width), own(2 * gene_width, peak_width)


def layout(bits):
    size = 1 << len(bits)
    return [
        sum(bit for i, bit in enumerate(bits) if position >> (len(bits) - 1 - i) & 1)
        for position in range(size)
    ]


def shuffled(size, seed):
    places = list(range(size))
    random.Random(seed).shuffle(places)
    return places


def turned(bits, by):
    return bits[by:] + bits[:by]


def across(left, right):
    return lax.dot_general(left, right, (((1,), (1,)), ((), ())), preferred_element_type=jnp.float32)


def halved(value):
    high = value.astype(jnp.bfloat16)
    return high, (value - high.astype(jnp.float32)).astype(jnp.bfloat16)


def exact(left, right):
    left_high, left_low = halved(left)
    right_high, right_low = halved(right)
    return jnp.dot(
        jnp.concatenate([left_low, left_low, left_high, left_high], axis=1),
        jnp.concatenate([right_low, right_high, right_low, right_high], axis=0),
        preferred_element_type=jnp.float32,
    )


def struct(*shape, dtype=jnp.float32):
    return jax.ShapeDtypeStruct(shape, dtype)


def gram_of(high, rest):
    pair = jnp.concatenate([high, rest], axis=0)
    squares = across(pair, pair)
    rank = high.shape[0]
    return (squares[:rank, :rank] + squares[rank:, rank:]) + (squares[:rank, rank:] + squares[rank:, :rank])


def parcels_kernel(seats, spot, rna_0, rna_1, atac_0, atac_1, cell, gene, peak, *refs):
    links, out, copied, slots, sems = refs[:4], refs[4], refs[5:9], refs[9], refs[10]

    copies = [pltpu.make_async_copy(link, to, sems.at[i]) for i, (link, to) in enumerate(zip(links, copied))]

    @pl.when(pl.program_id(0) == 0)
    def _():
        for copy in copies:
            copy.start()

    rank = cell.shape[0]
    cells = rna_0.shape[0]
    gene_width, peak_width = gene.shape[1], peak.shape[1]
    width = gene_width + peak_width
    cell_pair = jnp.concatenate(halved(cell[...]), axis=1)
    gene_low = gene[...].astype(jnp.bfloat16)
    peak_low = peak[...].astype(jnp.bfloat16)
    part = rank // 4
    for j, seat in enumerate(seats):
        at = 0
        for source, size in ((rna_0, gene_width), (rna_1, gene_width), (atac_0, peak_width), (atac_1, peak_width)):
            out[seat, 0:cells, at : at + size] = source[:, j * size : (j + 1) * size]
            at += size
        out[seat, 0:cells, at:] = cell_pair
        for s in range(2):
            row = (2 * (j % 2) + s) * part
            out[seat, cells:, s * width : s * width + gene_width] = gene_low[row : row + part]
            out[seat, cells:, s * width + gene_width : (s + 1) * width] = peak_low[row : row + part]

    @pl.when(pl.program_id(0) == 0)
    def _():
        for copy in copies:
            copy.wait()
        link_gene, link_peak, link_weight, link_count = copied
        count = link_gene.shape[0]
        lane = lax.broadcasted_iota(jnp.int32, slots.shape, 1) - spot[1] * count
        row = lax.broadcasted_iota(jnp.int32, slots.shape, 0)
        value = jnp.zeros(slots.shape, jnp.float32)
        for s in range(count):
            weight = jnp.where(s < link_count[0], link_weight[s], 0)
            for r, entry in enumerate((link_gene[s], link_peak[s], weight)):
                value = jnp.where((lane == s) & (row == r), entry.astype(jnp.float32), value)
        slots[...] = value.astype(jnp.bfloat16)

    for seat in seats:
        out[seat, cells:, 2 * width :] = slots[...]


def power_of(top):
    return jnp.floor(jnp.log2(jnp.maximum(top, TINY))) + 1.0


def encode(value):
    groups = [value[:, at : at + BLOCK] for at in range(0, value.shape[1], BLOCK)]
    least = [jnp.min(group, axis=1, keepdims=True) for group in groups]
    most = [jnp.max(group, axis=1, keepdims=True) for group in groups]
    power = power_of(functools.reduce(jnp.maximum, most))
    unit, per_unit = jnp.exp2(power) / UNITS, jnp.exp2(-power) * UNITS
    least = [jnp.floor(low * per_unit) for low in least]
    most = [jnp.ceil(high * per_unit) for high in most]
    codes = []
    for group, low, high in zip(groups, least, most):
        spread = (high - low) * unit
        per = jnp.where(spread > 0.0, CODES / spread, 0.0)
        code = jnp.clip(jnp.floor((group - low * unit) * per + 0.5), 0.0, CODES) - (CODES + 1) / 2
        codes.append(code.astype(jnp.int32).astype(jnp.int16))
    return codes, [*least, *most, power]


def decode(code, least, most, power):
    steps = code.astype(jnp.int32).astype(jnp.float32) + (CODES + 1) / 2
    return (least + steps * ((most - least) / CODES)) * (jnp.exp2(power) / UNITS)


def whole_numbers(columns, lanes):
    rows = columns[0].shape[0]
    size = sum(column.shape[1] for column in columns)
    filled = jnp.concatenate([*columns, jnp.zeros((rows, lanes - size), jnp.float32)], axis=1)
    return filled.astype(jnp.int32).astype(jnp.int16)


def codes_kernel(gene, peak, message):
    codes, columns = encode(jnp.concatenate([gene[...], peak[...]], axis=1))
    for b, code in enumerate(codes):
        message[:, b * BLOCK : (b + 1) * BLOCK] = code
    at = len(codes) * BLOCK
    message[:, at:] = whole_numbers(columns, message.shape[1] - at)


def table_kernel(received_slots, out):
    slots = sum(received_slots[j].astype(jnp.float32) for j in range(received_slots.shape[0]))

    def hot(row, size, value):
        ids = lax.broadcasted_iota(jnp.int32, (size, slots.shape[1]), 0).astype(jnp.float32)
        return jnp.where(slots[row : row + 1] == ids, value, 0.0).astype(jnp.bfloat16)

    out[...] = across(hot(0, out.shape[0], slots[2:3]), hot(1, out.shape[1], 1.0))


def twins_kernel(spot, gene, peak, got, out):
    width = gene.shape[1] + peak.shape[1]
    groups = width // BLOCK
    columns = got[:, width:].astype(jnp.int32).astype(jnp.float32)
    power = columns[:, 2 * groups : 2 * groups + 1]
    at = g = 0
    first = spot[0] == 0
    for ref in (gene, peak):
        size = ref.shape[1]
        for b in range(size // BLOCK):
            mine = ref[:, b * BLOCK : (b + 1) * BLOCK]
            other = decode(
                got[:, g * BLOCK : (g + 1) * BLOCK], columns[:, g : g + 1], columns[:, groups + g : groups + g + 1], power
            )
            out[:, at + b * BLOCK : at + (b + 1) * BLOCK] = jnp.where(first, mine, other)
            out[:, at + size + b * BLOCK : at + size + (b + 1) * BLOCK] = jnp.where(first, other, mine)
            g += 1
        at += 2 * size


def in_hbm(value):
    return pltpu.with_memory_space_constraint(value, pltpu.HBM)


def parcels(spot, rna_counts, atac_counts, cell_factor, gene_factor, peak_factor, links, seats):
    half = len(seats)
    cells = rna_counts.shape[0]
    rank = cell_factor.shape[0]
    gene_width, peak_width = gene_factor.shape[1], peak_factor.shape[1]
    rows, lanes = cells + rank // 4, 2 * (gene_width + peak_width) + 2 * rank

    def columns(width, side):
        return pl.BlockSpec((cells, half * width), lambda i: (0, side))

    def whole(array):
        return pl.BlockSpec(array.shape, lambda i: (0, 0))

    return pl.pallas_call(
        functools.partial(parcels_kernel, seats),
        grid=(1,),
        in_specs=[SMEM, columns(gene_width, 0), columns(gene_width, 1), columns(peak_width, 0), columns(peak_width, 1)]
        + [whole(a) for a in (cell_factor, gene_factor, peak_factor)]
        + [pl.BlockSpec(memory_space=pl.ANY)] * 4,
        out_specs=VMEM,
        out_shape=struct(half, rows, lanes, dtype=jnp.bfloat16),
        scratch_shapes=[pltpu.SMEM(link.shape, jnp.int32) for link in links]
        + [pltpu.VMEM((rank // 4, 2 * rank), jnp.bfloat16), pltpu.SemaphoreType.DMA((4,))],
        compiler_params=PARAMS,
    )(
        spot,
        *(in_hbm(a) for a in (rna_counts, rna_counts, atac_counts, atac_counts, cell_factor, gene_factor, peak_factor)),
        *(in_hbm(a) for a in links[:-1]),
        links[-1],
    )


def first_sums_kernel(order, received, sums, gram, state):
    rank, features = sums.shape
    cells = received.shape[1] - rank // 4
    high = jnp.concatenate([received[j, 0:cells, features : features + rank] for j in order], axis=1)
    rest = jnp.concatenate([received[j, 0:cells, features + rank :] for j in order], axis=1)
    counts = jnp.concatenate([received[j, 0:cells, 0:features] for j in order], axis=0)
    sums[...] = jnp.dot(high, counts, preferred_element_type=jnp.float32)
    gram[...] = gram_of(high, rest)
    state[...] = high.astype(jnp.float32) + rest.astype(jnp.float32)


def by_index(rank):
    row = lax.broadcasted_iota(jnp.int32, (rank, rank), 0)
    return row, lax.broadcasted_iota(jnp.int32, (rank, rank), 1)


def finish_sums(sums_value, gram_value, sums, message):
    rank, features = sums_value.shape
    sums[...] = sums_value
    codes, columns = encode(sums_value)
    for b, code in enumerate(codes):
        message[:, b * BLOCK : (b + 1) * BLOCK] = code
    power = power_of(jnp.max(jnp.max(gram_value, axis=1, keepdims=True), axis=0, keepdims=True))
    scaled = gram_value * (jnp.exp2(-power) * DIGIT)
    high = jnp.minimum(jnp.floor(scaled), DIGIT - 1)
    low = jnp.clip(jnp.floor((scaled - high) * DIGIT), 0.0, DIGIT - 1)
    row, column = by_index(rank)
    diagonal = jnp.sum(jnp.where(row == column, low, 0.0), axis=1, keepdims=True)
    columns = [jnp.where(row <= column, high, low), diagonal, jnp.broadcast_to(power, (rank, 1)), *columns]
    message[:, features:] = whole_numbers(columns, message.shape[1] - features)


def read_message(message, features, rank):
    groups = features // BLOCK
    beside = message[:, features:].astype(jnp.int32).astype(jnp.float32)
    lanes = beside.shape[1]
    square = jnp.concatenate([beside, jnp.zeros((lanes - rank, lanes), jnp.float32)], axis=0).T
    upright, turned_over = beside[:, :rank], square[:rank, :rank]
    diagonal, power = beside[:, rank : rank + 1], beside[:, rank + 1 : rank + 2]
    row, column = by_index(rank)
    high = jnp.where(row <= column, upright, turned_over)
    low = jnp.where(row == column, diagonal, jnp.where(row < column, turned_over, upright))
    gram = (high + low / DIGIT) * (jnp.exp2(power) / DIGIT)
    at = rank + 2
    sums_power = beside[:, at + 2 * groups : at + 2 * groups + 1]
    blocks = [
        decode(
            message[:, b * BLOCK : (b + 1) * BLOCK],
            beside[:, at + b : at + b + 1],
            beside[:, at + groups + b : at + groups + b + 1],
            sums_power,
        )
        for b in range(groups)
    ]
    return gram, blocks


def first_links_kernel(
    link_scale, widths, seats, spot, mine, other, half_table, half_table_other, sums_in, gram, sums, message, table, sem, table_smem
):
    half = mine.shape[0]
    rank, features = sums_in.shape
    gene_width, peak_width = widths
    gene_blocks, peak_blocks = gene_width // BLOCK, peak_width // BLOCK
    width = gene_width + peak_width
    table[...] = half_table[...] + half_table_other[...]
    copy = pltpu.make_async_copy(table, table_smem, sem)
    copy.start()
    copy.wait()
    side, place, core = spot[0], spot[1], spot[2]
    total = [None] * (features // BLOCK)

    def add(target, weight, block):
        term = weight * block
        total[target] = term if total[target] is None else total[target] + term

    for j in range(half):
        blocks = []
        for b in range(width // BLOCK):
            pieces = [
                ref[seats[j], :, s * width + b * BLOCK : s * width + (b + 1) * BLOCK]
                for ref in (mine, other)
                for s in range(2)
            ]
            blocks.append(jnp.concatenate(pieces, axis=0).astype(jnp.float32))
        for b in range(gene_blocks):
            row = (side * half + j) * gene_blocks + b
            for u in range(2 * peak_blocks):
                column = (place + u // peak_blocks * half) * peak_blocks + u % peak_blocks
                add(2 * gene_blocks + u, table_smem[row, column], blocks[b])
        for b in range(peak_blocks):
            column = (side * half + j) * peak_blocks + b
            for t in range(2 * gene_blocks):
                row = (place + t // gene_blocks * half) * gene_blocks + t % gene_blocks
                add(t, table_smem[row, column], blocks[gene_blocks + b])
    links = jnp.concatenate(total, axis=1)
    ahead, behind = links[: rank // 2], links[rank // 2 :]
    first = core == 0
    links = jnp.concatenate([jnp.where(first, ahead, behind), jnp.where(first, behind, ahead)], axis=0)
    finish_sums(sums_in[...] + link_scale * links, gram[...], sums, message)


def gram_rows(gram, lanes):
    rank = gram.shape[0]
    rows = rank * rank // lanes
    return jnp.concatenate([gram[b * rows : (b + 1) * rows] for b in range(rank // rows)], axis=1)


def gram_back(rows_value, rank):
    return jnp.concatenate(
        [rows_value[:, b * rank : (b + 1) * rank] for b in range(rows_value.shape[1] // rank)], axis=0
    )


def step_kernel(link_bit, gene_bit, spot, totals, totals_got, staying, got, genes, received, totals_out, staying_out, *outs):
    totals_out[...] = totals[...] + totals_got[...]
    rank, width = staying.shape
    low = genes[...]
    if gene_bit:
        to_gene = staying[...] + (got[:, :width].astype(jnp.float32) + got[:, width : 2 * width].astype(jnp.float32))
        clear = (spot[1] // gene_bit) % 2 == 0
        mine, other = low.astype(jnp.float32), got[:, 2 * width :].astype(jnp.float32)
        low = jnp.concatenate([jnp.where(clear, mine, other), jnp.where(clear, other, mine)], axis=1)
        low = low.astype(jnp.bfloat16)
    else:
        to_gene = staying[...] + got[...]
    if link_bit:
        clear = (spot[1] // link_bit) % 2 == 0
        left, right = to_gene[:, : width // 2], to_gene[:, width // 2 :]
        staying_out[...] = jnp.where(clear, left, right)
        leaving = halved(jnp.where(clear, right, left))
        outs[0][...] = jnp.concatenate([*leaving, low], axis=1)
    else:
        staying_out[...] = to_gene
    outs[-1][...] = low


def step(spot, received, link_bit, gene_bit, totals, staying, genes):
    rank, width = staying[0].shape
    size = genes.shape[1] * (2 if gene_bit else 1)
    outs = [struct(*totals[0].shape), struct(rank, width // 2 if link_bit else width)]
    outs += [struct(rank, width + size, dtype=jnp.bfloat16)] if link_bit else []
    outs += [struct(rank, size, dtype=jnp.bfloat16)]
    values = [*totals, *staying, genes, received]
    return pl.pallas_call(
        functools.partial(step_kernel, link_bit, gene_bit),
        in_specs=[SMEM] + [VMEM] * len(values),
        out_specs=[VMEM] * len(outs),
        out_shape=outs,
        compiler_params=PARAMS,
    )(spot, *values)


def next_sums_kernel(
    link_scale, widths, orders, spot, table, mine, other, state, received, to_gene, genes_mine, genes_other, *refs
):
    sums, message, gram, state_out, own = refs
    half = received.shape[0]
    rank, features = sums.shape
    cells = own.shape[1]
    gene_width, peak_width = widths
    gene_blocks, peak_blocks = gene_width // BLOCK, peak_width // BLOCK
    side, place, core = spot[0], spot[1], spot[2]
    first = core == 0
    old = state[...]
    left, right = mine[:rank], other[:rank]
    products = jnp.concatenate([jnp.where(first, left, right), jnp.where(first, right, left)], axis=1)
    new = old * products / (exact(gram_back(mine[rank:], rank), old) + EPSILON)
    state_out[...] = new
    mine_now = new[:, :cells]
    for position in range(1, half):
        at = position * cells
        mine_now = jnp.where(place == orders[0][position], new[:, at : at + cells], mine_now)
    own[...] = mine_now
    high, rest = halved(new)
    mine_low, other_low = genes_mine[...].astype(jnp.float32), genes_other[...].astype(jnp.float32)
    genes = jnp.concatenate(
        [jnp.where(first, mine_low, other_low), jnp.where(first, other_low, mine_low)], axis=1
    )
    total = [None] * (2 * peak_blocks)
    for position, j in enumerate(orders[1]):
        for b in range(gene_blocks):
            at = (position * gene_blocks + b) * BLOCK
            block = genes[:, at : at + BLOCK]
            row = (side * half + j) * gene_blocks + b
            for u in range(2 * peak_blocks):
                column = (place + u // peak_blocks * half) * peak_blocks + u % peak_blocks
                term = table[row, column] * block
                total[u] = term if total[u] is None else total[u] + term
    gene_links = to_gene[...]
    nothing = jnp.zeros_like(gene_links)
    links = jnp.concatenate(
        [jnp.where(side == 0, gene_links, nothing), jnp.where(side == 0, nothing, gene_links), *total], axis=1
    )
    counts = jnp.concatenate([received[j, 0:cells, 0:features] for j in orders[2]], axis=0)
    products = jnp.dot(high, counts, preferred_element_type=jnp.float32)
    gram[...] = gram_of(high, rest)
    finish_sums(products + link_scale * links, gram[...], sums, message)


def update_kernel(last, widths, orders, spot, table, sums, gram_mine, other, factors, received, *outs):
    half = received.shape[0]
    rank, features = sums.shape
    cells = received.shape[1] - rank // 4
    gene_width, peak_width = widths
    gene_blocks, peak_blocks = gene_width // BLOCK, peak_width // BLOCK
    side, place, core = spot[0], spot[1], spot[2]
    first = core == 0
    gram_other, blocks = read_message(other, features, rank)
    gram = gram_mine[...] + gram_other
    old = factors[...]
    below = exact(gram, old) + EPSILON
    whole = jnp.concatenate(
        [sums[:, b * BLOCK : (b + 1) * BLOCK] + block for b, block in enumerate(blocks)], axis=1
    )
    new = old * whole / below
    low = new.astype(jnp.bfloat16)
    counts = jnp.concatenate([received[j, 0:cells, 0:features] for j in orders[0]], axis=0)
    cell_sums = across(low, counts)
    gram_features = across(low, low)
    kept, sent, *outs = outs
    split = half // 2 * cells
    left, right = cell_sums[:, :split], cell_sums[:, split:]
    for ref, value in ((kept, jnp.where(first, left, right)), (sent, jnp.where(first, right, left))):
        ref[:rank] = value
        ref[rank:] = gram_rows(gram_features, split)

    def own(at, width):
        return jnp.where(side == 0, new[:, at : at + width], new[:, at + width : at + 2 * width])

    if last:
        gene_out, peak_out = outs
        gene_out[...] = own(0, gene_width)
        peak_out[...] = own(2 * gene_width, peak_width)
        return
    factors_out, links_kept, links_sent, gene_low = outs
    factors_out[...] = new
    gene_low[...] = own(0, gene_width).astype(jnp.bfloat16)
    peaks = low[:, 2 * gene_width :].astype(jnp.float32)
    peaks = [peaks[:, u * BLOCK : (u + 1) * BLOCK] for u in range(2 * peak_blocks)]
    for position in range(half // 2):
        pair = []
        for j in (orders[1][position], orders[1][position + half // 2]):
            parts = []
            for b in range(gene_blocks):
                row = (side * half + j) * gene_blocks + b
                part = None
                for u, block in enumerate(peaks):
                    column = (place + u // peak_blocks * half) * peak_blocks + u % peak_blocks
                    term = table[row, column] * block
                    part = term if part is None else part + term
                parts.append(part)
            pair.append(jnp.concatenate(parts, axis=1))
        at = position * gene_width
        links_kept[:, at : at + gene_width] = jnp.where(first, *pair)
        links_sent[:, at : at + gene_width] = jnp.where(first, pair[1], pair[0])


def last_cells_kernel(spot, mine, other, old, out):
    rank, cells = out.shape
    totals = mine[:rank] + other[:rank]
    gram = mine[rank:] + other[rank:]
    lanes = totals.shape[1]
    rows = rank * rank // (4 * lanes)
    gram = jnp.concatenate(
        [gram[i * rows : (i + 1) * rows, b * rank : (b + 1) * rank] for i in range(4) for b in range(lanes // rank)],
        axis=0,
    )
    own = totals[:, :cells]
    for position in range(1, lanes // cells):
        own = jnp.where(spot[3] == position, totals[:, position * cells : (position + 1) * cells], own)
    out[...] = old[...] * own / (exact(gram, old[...]) + EPSILON)


def shards_blocks(
    rna_counts,
    atac_counts,
    cell_factor,
    gene_factor,
    peak_factor,
    link_gene,
    link_peak,
    link_weight,
    link_count,
):
    count = lax.axis_size(AXIS)
    half = count // 2
    me = lax.axis_index(AXIS)
    side, place, core = me // half, me % half, me % 2
    chip_bits = bits_below(half)[1:]
    cell_bits, link_bits = turned(chip_bits, 1), turned(chip_bits, 2)
    tail = sum(
        jnp.where((me & bit) != 0, 1 << i, 0) for i, bit in enumerate(reversed(cell_bits[2:]))
    )
    spot = jnp.stack([side, place, core, tail]).astype(jnp.int32)
    rank, cells = cell_factor.shape
    gene_width, peak_width = gene_factor.shape[1], peak_factor.shape[1]
    widths = (gene_width, peak_width)
    width = gene_width + peak_width
    features = 2 * width
    link_scale = cells * count / 4.0
    table_shape = (rna_counts.shape[1] // BLOCK, atac_counts.shape[1] // BLOCK)
    cell_order = layout([1] + cell_bits)
    link_order = layout([1] + link_bits)
    gene_order = layout([1] + link_bits[::-1])

    links = (link_gene, link_peak, link_weight, link_count)
    in_seats = shuffled(half, SEED)
    seats = [in_seats.index(j) for j in range(half)]
    cell_seats = [seats[j] for j in cell_order]
    sent = parcels(spot, rna_counts, atac_counts, cell_factor, gene_factor, peak_factor, links, seats)
    halves = [[side_start + j for j in in_seats] for side_start in (0, half)]
    received = lax.all_to_all(sent, AXIS, 0, 0, axis_index_groups=halves, tiled=True)
    rows_other = flip(received[:, cells:, :features], 1)
    received_here = pltpu.with_memory_space_constraint(received, pltpu.VMEM)
    codes = pl.pallas_call(
        codes_kernel,
        in_specs=[VMEM] * 2,
        out_specs=VMEM,
        out_shape=struct(rank, width + 2 * rank, dtype=jnp.int16),
        compiler_params=PARAMS,
    )(gene_factor, peak_factor)
    rows = rank // 4
    half_table = pl.pallas_call(
        table_kernel,
        grid=(1,),
        in_specs=[pl.BlockSpec((half, rows, 2 * rank), lambda i: (0, cells // rows, features // (2 * rank)))],
        out_specs=VMEM,
        out_shape=struct(*table_shape),
        compiler_params=PARAMS,
    )(received_here)
    half_table_other = flip(half_table, half)

    sums_shapes = (struct(rank, features), struct(rank, features + 2 * rank, dtype=jnp.int16))
    sums, gram, state = pl.pallas_call(
        functools.partial(first_sums_kernel, cell_seats),
        in_specs=[VMEM],
        out_specs=[VMEM] * 3,
        out_shape=(struct(rank, features), struct(rank, rank), struct(rank, half * cells)),
        compiler_params=PARAMS,
    )(received_here)
    codes, sums, half_table_other = lax.optimization_barrier((codes, sums, half_table_other))
    codes_other = flip(codes, half)
    sums, message, link_table = pl.pallas_call(
        functools.partial(first_links_kernel, link_scale, widths, seats),
        grid=(1,),
        in_specs=[
            SMEM,
            pl.BlockSpec((half, rows, features + 2 * rank), lambda i: (0, cells // rows, 0)),
            VMEM,
            VMEM,
            VMEM,
            VMEM,
            VMEM,
        ],
        out_specs=[VMEM] * 3,
        out_shape=(*sums_shapes, struct(*table_shape)),
        scratch_shapes=[pltpu.SemaphoreType.DMA, pltpu.SMEM(table_shape, jnp.float32)],
        compiler_params=PARAMS,
    )(spot, received_here, rows_other, half_table, half_table_other, sums, gram)

    message, codes_other = lax.optimization_barrier((message, codes_other))
    factors = pl.pallas_call(
        twins_kernel,
        in_specs=[SMEM] + [VMEM] * 3,
        out_specs=VMEM,
        out_shape=struct(rank, features),
        compiler_params=PARAMS,
    )(spot, gene_factor, peak_factor, codes_other)

    split = half // 2 * cells
    for sweep_index in range(ROUNDS):
        last = sweep_index == ROUNDS - 1
        other = flip(message, half)
        outs = [struct(rank + rank * rank // split, split)] * 2
        if last:
            outs += [struct(rank, gene_width), struct(rank, peak_width)]
        else:
            outs += [struct(rank, features)] + [struct(rank, half // 2 * gene_width)] * 2
            outs += [struct(rank, gene_width, dtype=jnp.bfloat16)]
        kept, sent, *outs = pl.pallas_call(
            functools.partial(update_kernel, last, widths, (cell_seats, link_order)),
            in_specs=[SMEM] * 2 + [VMEM] * 5,
            out_specs=[VMEM] * len(outs),
            out_shape=outs,
            compiler_params=PARAMS,
        )(spot, link_table, sums, gram, other, factors, received_here)
        if last:
            gene_out, peak_out = outs
            totals = kept + flip(sent, 1)
            first, second = cell_bits[:2]
            quarters = jnp.split(totals[:rank], 4, axis=1)
            gram_part = jnp.concatenate(jnp.split(totals[rank:], 4, axis=1), axis=0)
            is_first, is_second = (me & first) != 0, (me & second) != 0

            def quarter(flip_first, flip_second):
                low, high = (
                    jnp.where(is_second ^ flip_second, quarters[2 * i + 1], quarters[2 * i]) for i in range(2)
                )
                return jnp.concatenate([jnp.where(is_first ^ flip_first, high, low), gram_part], axis=0)

            got = [
                flip(quarter(*which), bit)
                for which, bit in (((True, False), first), ((False, True), second), ((True, True), first | second))
            ]
            totals = quarter(False, False) + (got[0] + got[1] + got[2])
            for bit in cell_bits[2:-1]:
                totals = totals + flip(totals, bit)
            cell_out = pl.pallas_call(
                last_cells_kernel,
                in_specs=[SMEM] + [VMEM] * 3,
                out_specs=VMEM,
                out_shape=struct(rank, cells),
                compiler_params=PARAMS,
            )(spot, totals, flip(totals, cell_bits[-1]), own_cells)
            return cell_out, gene_out, peak_out
        factors, links_kept, links_sent, genes = outs
        totals, staying, leaving, genes = step(
            spot, received_here, link_bits[0], 0, (kept, flip(sent, 1)), (links_kept, flip(links_sent, 1)), genes
        )
        for i, (cell_bit, link_bit) in enumerate(zip(cell_bits, link_bits)):
            going = lax.optimization_barrier((totals, leaving))
            got = lax.optimization_barrier((flip(going[0], cell_bit), flip(going[1], link_bit)))
            next_bit = link_bits[i + 1] if i + 1 < len(link_bits) else 0
            totals, staying, *leaving, genes = step(
                spot, received_here, next_bit, link_bit, (totals, got[0]), (staying, got[1]), genes
            )
            leaving = leaving[0] if next_bit else None
        to_gene = staying
        sums, message, gram, state, own_cells = pl.pallas_call(
            functools.partial(next_sums_kernel, link_scale, widths, (cell_order, gene_order, cell_seats)),
            in_specs=[SMEM] * 2 + [VMEM] * 7,
            out_specs=[VMEM] * 5,
            out_shape=(*sums_shapes, struct(rank, rank), struct(rank, half * cells), struct(rank, cells)),
            compiler_params=PARAMS,
        )(spot, link_table, totals, flip(totals, 1), state, received_here, to_gene, genes, flip(genes, 1))


def shards(rna_counts, atac_counts, cell_factor, gene_factor, peak_factor, link_gene, *links):
    half = lax.axis_size(AXIS) // 2
    rank, cells = cell_factor.shape
    gene_width, peak_width = gene_factor.shape[1], peak_factor.shape[1]
    features = 2 * (gene_width + peak_width)
    in_blocks = (
        half % 16 == 0
        and rank == cells
        and 2 * rank == BLOCK
        and gene_width % BLOCK == 0
        and peak_width % BLOCK == 0
        and rank + 3 + 2 * (features // BLOCK) <= 2 * rank
        and half * link_gene.shape[0] <= 2 * rank
        and rank % 64 == 0
        and atac_counts.shape[1] // BLOCK == 2 * rank
        and max(rna_counts.shape[1], atac_counts.shape[1]) // BLOCK <= 256
    )
    run = shards_blocks if in_blocks else shards_any
    return run(rna_counts, atac_counts, cell_factor, gene_factor, peak_factor, link_gene, *links)


def solution(mesh):
    columns = P(None, ("groups", "cells"))
    slots = P(("groups", "cells"))
    in_specs = (P(("groups", "cells"), None),) * 2 + (columns,) * 3 + (slots,) * 4
    return jax.shard_map(
        shards, mesh=mesh, in_specs=in_specs, out_specs=(columns,) * 3, check_vma=False
    )
```
